32 devices in a mesh: grp: 2 (over y), brick: 4 (over z), vec: 2 (over x), sub: 2 (over core).
Axes of the slice: x: 2, y: 2, z: 4, core: 2. Of those that a mesh axis runs over, the one named last changes fastest.
Arguments:
- vectors: float32 [128, 3, 2, 16384], P(('vec', 'sub'), None, None, ('grp', 'brick')), parts along dimension 3, may hold values from -6 to 6
- gauge_links: float32 [3, 3, 3, 2, 16384], P(None, None, None, None, ('grp', 'brick')), parts along dimension 4, may hold values from -1 to 1, as said below
- momenta: int32 [27, 3], replicated, may hold values from -3 to 3
Outputs:
- elementals: float32 [128, 54, 2, 128], P(('vec', 'sub'), 'grp', None, 'brick'), parts along dimension 1
The draws below stay inside these ranges and needn't reach their ends.
There are 2 independent parts, one for each index of `grp`. The reference program is written for one: setup_inputs(seed, part) draws one part's arguments, and reference() takes and returns one part's arrays. A program takes and returns all parts, laid end to end along the dimension named above; an argument that names none is the same for every part. Nothing has to cross between parts.
Inputs may be any that keep to these rules, and one draw needn't show every extreme that they name: Each gauge_links[mu, :, :, :, s] is a unitary 3x3 complex matrix.
All inputs are finite; a program needn't handle non-finite values.
Results may differ from the reference program's by a relative error of at most 0.0049.
Values may be sent and summed in bfloat16 or wider, within the bound.
No kernel may reach another device: no remote copies, remote signals or barrier semaphores. Data moves between devices by JAX's collectives and lax.ppermute only.
A program may use at most 128 MiB of HBM per device.

```python
import math
import jax
import jax.numpy as jnp
from jax import lax

NV = 128
P_SIZE = 27
LY = 64
LZ = 8
ITERS = 2
NX = 16
SITES = 8192


def inner_product(first, second):
    real_part = jnp.sum(first[:, :, 0] * second[:, :, 0] + first[:, :, 1] * second[:, :, 1], axis=1)
    imag_part = jnp.sum(first[:, :, 0] * second[:, :, 1] - first[:, :, 1] * second[:, :, 0], axis=1)
    return (real_part[:, None], imag_part[:, None])


def remove_along(first, second):
    real_part, imag_part = inner_product(first, second)
    new_real = second[:, :, 0] - (real_part * first[:, :, 0] - imag_part * first[:, :, 1])
    new_imag = second[:, :, 1] - (real_part * first[:, :, 1] + imag_part * first[:, :, 0])
    return jnp.stack([new_real, new_imag], axis=2)


def normalize(matrix_row):
    length = jnp.sum(matrix_row * matrix_row, axis=(1, 2))
    return matrix_row * jax.lax.rsqrt(length + 1e-06)[:, None, None, :]


def draw_gauge_links(key, part):
    noise = jax.random.normal(jax.random.fold_in(key, 7), (3, 3, 3, 2, SITES), jnp.float32)
    first = normalize(noise[:, 0])
    second = normalize(remove_along(first, noise[:, 1]))
    third = remove_along(second, remove_along(first, noise[:, 2]))
    third = normalize(third)
    return jnp.stack([first, second, third], axis=1)


def place_ends(values, own_key, least, largest):
    place = [jax.random.randint(jax.random.fold_in(own_key, axis), (), 0, length) for axis, length in enumerate(values.shape)]
    widest = values.shape.index(max(values.shape))
    next_to = place[:widest] + [(place[widest] + 1) % values.shape[widest]] + place[widest + 1:]
    return values.at[tuple(place)].set(least).at[tuple(next_to)].set(largest)


def steps_of(rng, shape, cuts, smallest, top_value):
    loudness, own = 1.0, jax.random.fold_in(rng, 6)
    for position, parts in cuts:
        heights = jnp.exp(jax.random.uniform(jax.random.fold_in(own, position), (parts,), jnp.float32, smallest / len(cuts), top_value / len(cuts)))
        loudness = loudness * jnp.repeat(heights, shape[position] // parts).reshape([-1 if axis == position else 1 for axis in range(len(shape))])
    return loudness


def scatter_about(key, shape, width, reach, cuts=(), held_as=jnp.bfloat16):
    result = width * jax.random.normal(key, shape, jnp.float32)
    if cuts:
        result = result * steps_of(key, shape, cuts, -0.22, 0.18)
    return jnp.clip(result, -reach, reach).astype(held_as)


def setup_inputs(seed: int = 0, part: int = 0) -> dict:
    keys = jax.random.split(jax.random.key(seed), 4)
    part_keys = jax.random.split(jax.random.fold_in(keys[3], part), 4)
    vectors = scatter_about(part_keys[0], (NV, 3, 2, SITES), 1.0, 6.0, ((0, 4), (3, 4)), jnp.float32)
    gauge_links = draw_gauge_links(jax.random.fold_in(jax.random.fold_in(keys[3], part), 71), part)
    momenta = place_ends(jax.random.randint(keys[2], (P_SIZE, 3), -3, 4), jax.random.fold_in(keys[2], 1), -3, 3).astype(jnp.int32)
    return {"vectors": vectors, "gauge_links": gauge_links, "momenta": momenta}


KAPPA = 0.125


def matrix_apply(matrix, source):
    matrix_real = matrix[:, :, 0][None]
    matrix_imag = matrix[:, :, 1][None]
    source_real = source[:, None, :, 0]
    source_imag = source[:, None, :, 1]
    real_part = jnp.sum(matrix_real * source_real - matrix_imag * source_imag, axis=2)
    imag_part = jnp.sum(matrix_real * source_imag + matrix_imag * source_real, axis=2)
    return jnp.stack([real_part, imag_part], axis=2)


def adjoint(matrix):
    return jnp.stack([jnp.swapaxes(matrix[:, :, 0], 0, 1), -jnp.swapaxes(matrix[:, :, 1], 0, 1)], axis=2)


def smear_step(field, gauge):
    total = None
    for direction in range(3):
        axis = 3 + direction
        forward = matrix_apply(gauge[direction], jnp.roll(field, -1, axis=axis))
        behind = adjoint(jnp.roll(gauge[direction], 1, axis=axis))
        backward = matrix_apply(behind, jnp.roll(field, 1, axis=axis))
        term = forward + backward
        total = term if total is None else total + term
    return field + KAPPA * (total - 6.0 * field)


def reference(vectors, gauge_links, momenta):
    field = vectors.reshape((NV, 3, 2, NX, LY, LZ))
    gauge = gauge_links.reshape((3, 3, 3, 2, NX, LY, LZ))
    for step in range(ITERS):
        field = smear_step(field, gauge)
    smeared_low = field.reshape((NV, 3, 2, SITES)).astype(jnp.bfloat16)
    smeared_wide = lax.optimization_barrier(smeared_low).astype(jnp.float32)
    raw_wide = lax.optimization_barrier(vectors.astype(jnp.bfloat16)).astype(jnp.float32)
    right = smeared_wide.reshape((NV, 6 * SITES))
    site = jnp.arange(SITES, dtype=jnp.int32)
    layer_index = site // (LY * LZ)
    column_index = (site // LZ) % LY
    depth_index = site % LZ

    def one_momentum(triple):
        fraction = (jnp.mod(triple[0] * layer_index, NX).astype(jnp.float32) / NX
                    + jnp.mod(triple[1] * column_index, LY).astype(jnp.float32) / LY
                    + jnp.mod(triple[2] * depth_index, LZ).astype(jnp.float32) / LZ)
        angle = (2.0 * math.pi) * fraction
        cosine = jnp.cos(angle)
        sine = jnp.sin(angle)
        real_part = raw_wide[:, :, 0] * cosine - raw_wide[:, :, 1] * sine
        imag_part = raw_wide[:, :, 0] * sine + raw_wide[:, :, 1] * cosine
        phased = jnp.stack([real_part, imag_part], axis=2).astype(jnp.bfloat16)
        phased = lax.optimization_barrier(phased).astype(jnp.float32)
        turned = jnp.stack([-phased[:, :, 1], phased[:, :, 0]], axis=2)
        left = jnp.concatenate([phased.reshape((NV, 6 * SITES)), turned.reshape((NV, 6 * SITES))], axis=0)
        product = lax.dot_general(left, right, (((1,), (1,)), ((), ())),
                                  precision=lax.Precision.HIGHEST, preferred_element_type=jnp.float32)
        return product.reshape((2, NV, NV))

    blocks = lax.map(one_momentum, momenta)
    scale = (3.0 * SITES) ** -0.5
    return jnp.transpose(blocks, (2, 0, 1, 3)) * scale
```

```python
import functools
import math

import jax
import jax.numpy as jnp
from jax import lax
from jax.experimental import pallas as pl
from jax.experimental.pallas import tpu as pltpu
from jax.sharding import PartitionSpec as P

LY = 64
LZ = 8
ITERS = 2
KAPPA = 0.125
LANES = 128
ROWS = 16
VMEM_LIMIT = 56 * 1024 * 1024
VMEM = pl.BlockSpec(memory_space=pltpu.VMEM)
SMEM = pl.BlockSpec(memory_space=pltpu.SMEM)


def shifted(array, axis, by):
    peers = lax.axis_size(axis)
    return lax.ppermute(array, axis, [(i, (i + by) % peers) for i in range(peers)])


def link_row(direction, row, column, part):
    return ((direction * 3 + row) * 3 + column) * 2 + part


def add_hop(total, link, field, adjoint):
    for row in range(3):
        for column in range(3):
            if adjoint:
                real, imag = link(column, row, 0), link(column, row, 1)
            else:
                real, imag = link(row, column, 0), link(row, column, 1)
            source_real, source_imag = field[2 * column], field[2 * column + 1]
            if adjoint:
                add_real = real * source_real + imag * source_imag
                add_imag = real * source_imag - imag * source_real
            else:
                add_real = real * source_real - imag * source_imag
                add_imag = real * source_imag + imag * source_real
            for part, add in ((0, add_real), (1, add_imag)):
                old = total[2 * row + part]
                total[2 * row + part] = add if old is None else old + add


def group_size(ref):
    return min(ROWS, ref.shape[1])


def group_rows(group, ref):
    size = group_size(ref)
    return pl.ds(pl.multiple_of(group * size, size), size)


def lane_roll(value, by):
    return pltpu.roll(value, by % value.shape[-1], value.ndim - 1)


def depth_shift(value, offset):
    tiles = []
    depth = lax.broadcasted_iota(jnp.int32, (value.shape[0], LANES), 1) % LZ
    for start in range(0, value.shape[-1], LANES):
        tile = value[:, start : start + LANES]
        if offset > 0:
            tile = jnp.where(depth == LZ - 1, lane_roll(tile, LZ - 1), lane_roll(tile, -1))
        else:
            tile = jnp.where(depth == 0, lane_roll(tile, 1 - LZ), lane_roll(tile, 1))
        tiles.append(tile)
    return jnp.concatenate(tiles, axis=1)


def column_shift(value, offset):
    return lane_roll(value, -offset * LZ)


def smear_layer(layer, layers, group, field_ref, link_ref, back_ref, ahead_ref, behind_ref):
    plane = LY * LZ
    rows = group_rows(group, field_ref)
    here = pl.ds(layer * plane, plane)

    def load(ref, lanes):
        return [ref[k, rows, lanes].astype(jnp.float32) for k in range(6)]

    def links(ref, direction, lanes):
        return lambda r, c, part: ref[pl.ds(link_row(direction, r, c, part), 1), lanes]

    center = load(field_ref, here)
    if layer == layers - 1:
        ahead = load(ahead_ref, pl.ds(0, plane))
    else:
        ahead = load(field_ref, pl.ds((layer + 1) * plane, plane))
    total = [None] * 6
    add_hop(total, links(link_ref, 0, here), ahead, False)
    if layer == 0:
        behind = load(behind_ref, pl.ds(0, plane))
        total = [a + b for a, b in zip(total, behind)]
    else:
        before = pl.ds((layer - 1) * plane, plane)
        add_hop(total, links(link_ref, 0, before), load(field_ref, before), True)
    for direction, shift in ((1, column_shift), (2, depth_shift)):
        add_hop(total, links(link_ref, direction, here), [shift(v, 1) for v in center], False)
        add_hop(total, links(back_ref, direction - 1, here), [shift(v, -1) for v in center], True)
    return [c + KAPPA * (t - 6.0 * c) for c, t in zip(center, total)]


def smear_kernel(last, field_ref, link_ref, back_ref, ahead_ref, behind_ref, out_ref, *edges):
    plane = LY * LZ
    layers = field_ref.shape[2] // plane
    for layer in range(layers):
        here = pl.ds(layer * plane, plane)

        @pl.loop(0, field_ref.shape[1] // group_size(field_ref))
        def _(group):
            rows = group_rows(group, field_ref)
            new = smear_layer(layer, layers, group, field_ref, link_ref, back_ref, ahead_ref, behind_ref)
            for k in range(6):
                out_ref[k, rows, here] = new[k]

    if not last:
        first_ref, turned_ref = edges
        write_edges(out_ref, link_ref, first_ref, turned_ref)


def write_edges(field_ref, link_ref, first_ref, turned_ref):
    plane = LY * LZ
    end = pl.ds(field_ref.shape[2] - plane, plane)
    first_ref[...] = field_ref[:, :, pl.ds(0, plane)].astype(jnp.bfloat16)

    @pl.loop(0, field_ref.shape[1] // group_size(field_ref))
    def _(group):
        rows = group_rows(group, field_ref)
        turned = [None] * 6
        source = [field_ref[k, rows, end] for k in range(6)]
        add_hop(turned, lambda r, c, part: link_ref[pl.ds(link_row(0, r, c, part), 1), end], source, True)
        for k in range(6):
            turned_ref[k, rows, :] = turned[k].astype(jnp.bfloat16)


def edge_kernel(field_ref, link_ref, first_ref, turned_ref, back_ref):
    write_edges(field_ref, link_ref, first_ref, turned_ref)
    plane = LY * LZ
    for layer in range(link_ref.shape[1] // plane):
        here = pl.ds(layer * plane, plane)
        for base, shift in ((0, column_shift), (18, depth_shift)):
            back_ref[base : base + 18, here] = shift(link_ref[18 + base : 36 + base, here], -1)


def params():
    return pltpu.CompilerParams(vmem_limit_bytes=VMEM_LIMIT)


def edges_of(field, links):
    plane = LY * LZ
    edge = jax.ShapeDtypeStruct((6, field.shape[1], plane), jnp.bfloat16)
    return pl.pallas_call(
        edge_kernel,
        out_shape=(edge, edge, jax.ShapeDtypeStruct((36, field.shape[2]), jnp.float32)),
        in_specs=[VMEM] * 2,
        out_specs=(VMEM,) * 3,
        compiler_params=params(),
        name="edges",
    )(field, links)


def smear(field, links, back, ahead, behind, last):
    plane = LY * LZ
    edge = jax.ShapeDtypeStruct((6, field.shape[1], plane), jnp.bfloat16)
    shapes = (jax.ShapeDtypeStruct(field.shape, jnp.float32),) + (() if last else (edge, edge))
    return pl.pallas_call(
        functools.partial(smear_kernel, last),
        out_shape=shapes,
        in_specs=[VMEM] * 5,
        out_specs=(VMEM,) * len(shapes),
        compiler_params=params(),
        cost_estimate=pl.CostEstimate(flops=field.size * 80, bytes_accessed=field.size * 8, transcendentals=0),
        name="smear",
    )(field, links, back, ahead, behind)


def product_kernel(groups, scale, slot_ref, field_ref, table_ref, *refs):
    raw_refs, out_refs, (left_ref, right_ref, total_ref) = refs[:groups], refs[groups : 2 * groups], refs[2 * groups :]
    count = table_ref.shape[0] // 2
    vectors = field_ref.shape[1]
    total_ref[...] = jnp.zeros_like(total_ref)

    @pl.loop(0, field_ref.shape[2] // LANES)
    def _(tile):
        lanes = pl.ds(pl.multiple_of(tile * LANES, LANES), LANES)
        field = [field_ref[k, :, lanes] for k in range(6)]
        for p in range(count):
            cosine = table_ref[pl.ds(2 * p, 1), lanes]
            sine = table_ref[pl.ds(2 * p + 1, 1), lanes]
            for color in range(3):
                real, imag = field[2 * color], field[2 * color + 1]
                rows = pl.ds(p * vectors, vectors)
                left_ref[rows, pl.ds(2 * color * LANES, LANES)] = (cosine * real + sine * imag).astype(jnp.bfloat16)
                left_ref[rows, pl.ds((2 * color + 1) * LANES, LANES)] = (cosine * imag - sine * real).astype(jnp.bfloat16)
        for g, raw_ref in enumerate(raw_refs):
            width = raw_ref.shape[1]
            for color in range(3):
                real, imag = raw_ref[2 * color, :, lanes], raw_ref[2 * color + 1, :, lanes]
                first = pl.ds(2 * g * width, width)
                second = pl.ds((2 * g + 1) * width, width)
                one = pl.ds(2 * color * LANES, LANES)
                two = pl.ds((2 * color + 1) * LANES, LANES)
                right_ref[first, one] = real
                right_ref[first, two] = imag
                right_ref[second, one] = -imag
                right_ref[second, two] = real
        total_ref[...] += lax.dot_general(
            left_ref[...], right_ref[...], (((1,), (1,)), ((), ())), preferred_element_type=jnp.float32
        )

    turned = jnp.transpose(total_ref[...] * scale)
    width = turned.shape[0] // groups
    for g in range(groups):
        block = turned[g * width : (g + 1) * width].astype(out_refs[0].dtype)
        for slot in range(groups):

            @pl.when(slot_ref[g] == slot)
            def _():
                out_refs[slot][...] = block


def product(slots, field, table, raws, scale, dtype):
    groups = len(raws)
    vectors = field.shape[1]
    count = table.shape[0] // 2
    width = 2 * vectors
    out = jax.ShapeDtypeStruct((width, count * vectors), dtype)
    depth = 6 * LANES
    return pl.pallas_call(
        functools.partial(product_kernel, groups, scale),
        out_shape=(out,) * groups,
        in_specs=[SMEM] + [VMEM] * (2 + groups),
        out_specs=(VMEM,) * groups,
        scratch_shapes=[
            pltpu.VMEM((count * vectors, depth), jnp.bfloat16),
            pltpu.VMEM((groups * width, depth), jnp.bfloat16),
            pltpu.VMEM((count * vectors, groups * width), jnp.float32),
        ],
        compiler_params=params(),
        name="product",
    )(slots, field, table, *raws)


def phase_table(momenta, total_x, first_site, sites):
    plane = LY * LZ
    site = first_site + lax.iota(jnp.int32, sites)
    fraction = (
        jnp.mod(momenta[:, 0:1] * (site // plane)[None], total_x).astype(jnp.float32) / total_x
        + jnp.mod(momenta[:, 1:2] * (site // LZ % LY)[None], LY).astype(jnp.float32) / LY
        + jnp.mod(momenta[:, 2:3] * (site % LZ)[None], LZ).astype(jnp.float32) / LZ
    )
    angle = 2.0 * math.pi * fraction
    return jnp.stack([jnp.cos(angle), jnp.sin(angle)], axis=1).reshape((2 * momenta.shape[0], sites))


def shards(vectors, gauge_links, momenta):
    plane = LY * LZ
    bricks, vecs, subs = (lax.axis_size(axis) for axis in ("brick", "vec", "sub"))
    groups = vecs * subs
    assert groups == bricks
    width, sites = vectors.shape[0], vectors.shape[3]
    total_x = bricks * (sites // plane)
    brick, vec, sub = (lax.axis_index(axis) for axis in ("brick", "vec", "sub"))
    links = gauge_links.reshape((54, sites))
    field = jnp.transpose(vectors.reshape((width, 6, sites)), (1, 0, 2))
    raw = field.astype(jnp.bfloat16)
    first, turned, back = edges_of(field, links)

    offsets = [(a, 0) for a in range(vecs)]
    raws = [raw] + [shifted(raw, "vec", a) for a in range(1, vecs)]
    for b in range(1, subs):
        for a in range(vecs):
            raws.append(shifted(raws[a], "sub", b))
            offsets.append((a, b))
    table = phase_table(momenta, total_x, brick * sites, sites)

    for step in range(ITERS):
        ahead = shifted(first, "brick", -1)
        behind = shifted(turned, "brick", 1)
        field, *edges = smear(field, links, back, ahead, behind, step == ITERS - 1)
        if edges:
            first, turned = edges

    owners = jnp.stack([(vec - a) % vecs * subs + (sub - b) % subs for a, b in offsets])
    slots = ((owners - brick) % groups).astype(jnp.int32)
    scale = (3.0 * total_x * plane) ** (-0.5)
    blocks = product(slots, field, table, raws, scale, jnp.bfloat16)
    shares = []
    for slot, block in enumerate(blocks):
        pairs = [
            (b * groups + g, g * groups + (b + slot) % groups) for b in range(bricks) for g in range(groups)
        ]
        shares.append(lax.ppermute(block, ("brick", "vec", "sub"), pairs))
    total = functools.reduce(jnp.add, [share.astype(jnp.float32) for share in shares])
    count = momenta.shape[0]
    return jnp.transpose(total.reshape((2, width, count, width)), (1, 2, 0, 3))


def solution(mesh):
    in_specs = (
        P(("vec", "sub"), None, None, ("grp", "brick")),
        P(None, None, None, None, ("grp", "brick")),
        P(),
    )
    out_specs = P(("vec", "sub"), "grp", None, "brick")
    return jax.shard_map(shards, mesh=mesh, in_specs=in_specs, out_specs=out_specs, check_vma=False)
```

```python
import functools
import math

import jax
import jax.numpy as jnp
from jax import lax
from jax.experimental import pallas as pl
from jax.experimental.pallas import tpu as pltpu
from jax.sharding import PartitionSpec as P

LY = 64
LZ = 8
ITERS = 2
KAPPA = 0.125
LANES = 128
PLANE = LY * LZ
TILES = PLANE // LANES
ROWS = 16
LOW = jnp.bfloat16
WIDE = jnp.float32
VMEM_LIMIT = 48 * 1024 * 1024
VMEM = pl.BlockSpec(memory_space=pltpu.VMEM)
SMEM = pl.BlockSpec(memory_space=pltpu.SMEM)


def shifted(array, axis, by):
    peers = lax.axis_size(axis)
    return lax.ppermute(array, axis, [(i, (i + by) % peers) for i in range(peers)])


def add_hop(total, link, field, adjoint):
    for row in range(3):
        for column in range(3):
            if adjoint:
                real, imag = link(column, row, 0), link(column, row, 1)
            else:
                real, imag = link(row, column, 0), link(row, column, 1)
            source_real, source_imag = field[2 * column], field[2 * column + 1]
            if adjoint:
                add_real = real * source_real + imag * source_imag
                add_imag = real * source_imag - imag * source_real
            else:
                add_real = real * source_real - imag * source_imag
                add_imag = real * source_imag + imag * source_real
            for part, add in ((0, add_real), (1, add_imag)):
                old = total[2 * row + part]
                total[2 * row + part] = add if old is None else old + add


def lane_roll(value, by):
    return pltpu.roll(value, by % LANES, 1)


def lanes_at(layer, tile):
    return pl.ds(pl.multiple_of(layer * PLANE + tile * LANES, LANES), LANES)


def row_groups(ref):
    size = min(ROWS, ref.shape[1])
    return [pl.ds(start, size) for start in range(0, ref.shape[1], size)]


def load(ref, rows, lanes):
    return [ref[k, rows, lanes].astype(WIDE) for k in range(6)]


def store(ref, rows, lanes, values):
    for k in range(6):
        ref[k, rows, lanes] = values[k].astype(ref.dtype)


def link_at(link_ref, direction, layer, tile):
    tiles = link_ref.shape[0] // 54

    def get(row, column, part):
        matrix = (direction * 3 + row) * 3 + column
        return link_ref[pl.ds((matrix * tiles + layer * TILES + tile) * 2 + part, 1), :]

    return get


def plane_hops(total, link_ref, back_ref, layer, tile, rows, fetch):
    here = fetch(tile)
    after, before = fetch((tile + 1) % TILES), fetch((tile + TILES - 1) % TILES)
    lane = lax.broadcasted_iota(jnp.int32, (rows.size, LANES), 1)
    ahead = [jnp.where(lane >= LANES - LZ, lane_roll(b, -LZ), lane_roll(a, -LZ)) for a, b in zip(here, after)]
    add_hop(total, link_at(link_ref, 1, layer, tile), ahead, False)
    behind = [jnp.where(lane < LZ, lane_roll(b, LZ), lane_roll(a, LZ)) for a, b in zip(here, before)]
    lanes = lanes_at(layer, tile)
    add_hop(total, lambda r, c, part: back_ref[part, pl.ds(3 * r + c, 1), lanes], behind, True)
    depth = lane % LZ
    ahead = [jnp.where(depth == LZ - 1, lane_roll(a, LZ - 1), lane_roll(a, -1)) for a in here]
    add_hop(total, link_at(link_ref, 2, layer, tile), ahead, False)
    turned = [None] * 6
    add_hop(turned, link_at(link_ref, 2, layer, tile), here, True)
    for k in range(6):
        total[k] += jnp.where(depth == 0, lane_roll(turned[k], 1 - LZ), lane_roll(turned[k], 1))
    return here


def combined(here, total):
    return [(1.0 - 6.0 * KAPPA) * a + KAPPA * b for a, b in zip(here, total)]


def open_kernel(vector_ref, link_ref, field_ref, inner_ref, rim_ref, first_ref, turned_ref):
    vectors, sites = field_ref.shape[1:]
    tiles = sites // LANES
    layers = sites // PLANE
    stride = 6 * tiles
    for k in range(6):
        for tile in range(tiles):
            row = ((k // 2) * tiles + tile) * 2 + k % 2
            value = vector_ref[pl.ds(row, vectors, stride=stride), :]
            field_ref[k, :, pl.ds(tile * LANES, LANES)] = value
            low = value.astype(LOW)
            layer, column = divmod(tile, TILES)
            if layer == 0:
                first_ref[k, :, pl.ds(column * LANES, LANES)] = low
                rim_ref[k, :, pl.ds(column * LANES, LANES)] = low
            elif layer == layers - 1:
                rim_ref[k, :, pl.ds(PLANE + column * LANES, LANES)] = low
            else:
                inner_ref[k, :, pl.ds(tile * LANES - PLANE, LANES)] = low

    @pl.loop(0, TILES)
    def _(tile):
        for rows in row_groups(field_ref):
            turned = [None] * 6
            source = load(field_ref, rows, lanes_at(layers - 1, tile))
            add_hop(turned, link_at(link_ref, 0, layers - 1, tile), source, True)
            store(turned_ref, rows, lanes_at(0, tile), turned)


def rim_kernel(field_ref, link_ref, low_ref, high_ref, first_ref, turned_ref, back_ref):
    sites = field_ref.shape[2]
    tiles, layers = sites // LANES, sites // PLANE
    lane = lax.broadcasted_iota(jnp.int32, (9, LANES), 1)
    for layer in range(layers):
        for part in range(2):
            row = lambda tile: (9 * tiles + layer * TILES + tile) * 2 + part
            value = [link_ref[pl.ds(row(tile), 9, stride=2 * tiles), :] for tile in range(TILES)]
            value = [lane_roll(v, LZ) for v in value]
            for tile in range(TILES):
                back_ref[part, pl.ds(0, 9), lanes_at(layer, tile)] = jnp.where(lane < LZ, value[tile - 1], value[tile])

    for layer, out_ref in ((0, low_ref), (layers - 1, high_ref)):

        @pl.loop(0, TILES)
        def _(tile):
            for rows in row_groups(field_ref):
                total = [None] * 6
                if layer == 0:
                    source = load(field_ref, rows, lanes_at(1, tile))
                    add_hop(total, link_at(link_ref, 0, 0, tile), source, False)
                else:
                    source = load(field_ref, rows, lanes_at(layer - 1, tile))
                    add_hop(total, link_at(link_ref, 0, layer - 1, tile), source, True)
                fetch = lambda t: load(field_ref, rows, lanes_at(layer, t))
                here = plane_hops(total, link_ref, back_ref, layer, tile, rows, fetch)
                new = combined(here, total)
                store(out_ref, rows, lanes_at(0, tile), new)
                if layer == 0:
                    store(first_ref, rows, lanes_at(0, tile), new)
                else:
                    turned = [None] * 6
                    add_hop(turned, link_at(link_ref, 0, layer, tile), new, True)
                    store(turned_ref, rows, lanes_at(0, tile), turned)


def unit_phase(turns):
    half = math.pi * (turns - jnp.round(turns))
    square = half * half
    cosine, sine = 1.0, 1.0
    for order in range(12, 0, -2):
        sine = 1.0 - square * sine * (1.0 / (order * (order + 1)))
        cosine = 1.0 - square * cosine * (1.0 / (order * (order - 1)))
    sine = half * sine
    return 1.0 - 2.0 * sine * sine, 2.0 * sine * cosine


def inner_kernel(total_x, place_ref, field_ref, link_ref, back_ref, momenta_ref, out_ref, table_ref):
    layers = field_ref.shape[2] // PLANE
    count = momenta_ref.shape[0]
    momenta = momenta_ref[...].astype(WIDE)
    lane = lax.broadcasted_iota(jnp.int32, (count, LANES), 1)

    @pl.loop(0, TILES)
    def _(tile):
        column = (tile * (LANES // LZ) + lane // LZ).astype(WIDE)
        depth = (lane % LZ).astype(WIDE)
        turns = [momenta[:, 1:2] * column / LY, momenta[:, 2:3] * depth / LZ]
        part = sum(t - jnp.round(t) for t in turns)
        for layer in range(layers):
            along = momenta[:, 0:1] * (place_ref[0] + layer).astype(WIDE) / total_x
            cosine, sine = unit_phase(along - jnp.round(along) + part)
            table_ref[0, :, lanes_at(layer, tile)] = cosine
            table_ref[1, :, lanes_at(layer, tile)] = sine

    for layer in range(1, layers - 1):

        @pl.loop(0, TILES)
        def _(tile):
            for rows in row_groups(field_ref):
                total = [None] * 6
                add_hop(total, link_at(link_ref, 0, layer, tile), load(field_ref, rows, lanes_at(layer + 1, tile)), False)
                before = load(field_ref, rows, lanes_at(layer - 1, tile))
                add_hop(total, link_at(link_ref, 0, layer - 1, tile), before, True)
                fetch = lambda t: load(field_ref, rows, lanes_at(layer, t))
                here = plane_hops(total, link_ref, back_ref, layer, tile, rows, fetch)
                store(out_ref, rows, lanes_at(layer - 1, tile), combined(here, total))


def second_kernel(field_ref, link_ref, back_ref, low_ref, high_ref, inner_ref, ahead_ref, behind_ref, out_ref, rim_ref, one_ref):
    layers = field_ref.shape[2] // PLANE

    @pl.loop(0, TILES)
    def _(tile):
        for rows in row_groups(field_ref):
            lanes = lanes_at(0, tile)
            low = [a + KAPPA * b for a, b in zip(load(low_ref, rows, lanes), load(behind_ref, rows, lanes))]
            store(one_ref, rows, lanes, low)
            hop = [None] * 6
            add_hop(hop, link_at(link_ref, 0, layers - 1, tile), load(ahead_ref, rows, lanes), False)
            high = [a + KAPPA * b for a, b in zip(load(high_ref, rows, lanes), hop)]
            store(one_ref, rows, lanes_at(1, tile), high)

    def fetch_from(layer, rows):
        if layer == 0:
            return lambda t: load(one_ref, rows, lanes_at(0, t))
        if layer == layers - 1:
            return lambda t: load(one_ref, rows, lanes_at(1, t))
        return lambda t: load(inner_ref, rows, lanes_at(layer - 1, t))

    for layer in range(layers):

        @pl.loop(0, TILES)
        def _(tile):
            for rows in row_groups(field_ref):
                total = [None] * 6
                if layer < layers - 1:
                    add_hop(total, link_at(link_ref, 0, layer, tile), fetch_from(layer + 1, rows)(tile), False)
                if layer > 0:
                    add_hop(total, link_at(link_ref, 0, layer - 1, tile), fetch_from(layer - 1, rows)(tile), True)
                here = plane_hops(total, link_ref, back_ref, layer, tile, rows, fetch_from(layer, rows))
                if layer in (0, layers - 1):
                    own = load(field_ref, rows, lanes_at(layer, tile))
                    total = [a + KAPPA * b for a, b in zip(total, own)]
                    store(rim_ref, rows, lanes_at(min(layer, 1), tile), combined(here, total))
                else:
                    store(out_ref, rows, lanes_at(layer - 1, tile), combined(here, total))


def add_products(field_ref, raw_refs, table_ref, total_ref, left_ref, right_ref, table_tile):
    count = table_ref.shape[1]
    vectors = field_ref.shape[1]

    @pl.loop(0, field_ref.shape[2] // LANES)
    def _(tile):
        lanes = pl.ds(pl.multiple_of(tile * LANES, LANES), LANES)
        phases = pl.ds(pl.multiple_of(table_tile(tile) * LANES, LANES), LANES)
        field = [field_ref[k, :, lanes] for k in range(6)]
        for p in range(count):
            cosine = table_ref[0, pl.ds(p, 1), phases]
            sine = table_ref[1, pl.ds(p, 1), phases]
            rows = pl.ds(p * vectors, vectors)
            for color in range(3):
                real, imag = field[2 * color], field[2 * color + 1]
                left_ref[rows, pl.ds(2 * color * LANES, LANES)] = (cosine * real + sine * imag).astype(LOW)
                left_ref[rows, pl.ds((2 * color + 1) * LANES, LANES)] = (cosine * imag - sine * real).astype(LOW)
        for g, raw_ref in enumerate(raw_refs):
            width = raw_ref.shape[1]
            for color in range(3):
                real, imag = raw_ref[2 * color, :, lanes], raw_ref[2 * color + 1, :, lanes]
                first = pl.ds(2 * g * width, width)
                second = pl.ds((2 * g + 1) * width, width)
                one = pl.ds(2 * color * LANES, LANES)
                two = pl.ds((2 * color + 1) * LANES, LANES)
                right_ref[first, one] = real
                right_ref[first, two] = imag
                right_ref[second, one] = -imag
                right_ref[second, two] = real
        total_ref[...] += lax.dot_general(
            left_ref[...], right_ref[...], (((1,), (1,)), ((), ())), preferred_element_type=WIDE
        )


def inner_product_kernel(groups, field_ref, table_ref, *refs):
    raw_refs, (total_ref, left_ref, right_ref) = refs[:groups], refs[groups:]
    total_ref[...] = jnp.zeros_like(total_ref)
    add_products(field_ref, raw_refs, table_ref, total_ref, left_ref, right_ref, lambda tile: tile + TILES)


def last_product_kernel(groups, scale, slot_ref, rim_ref, ahead_ref, behind_ref, link_ref, start_ref, table_ref, *refs):
    raw_refs, out_refs, (field_ref, total_ref, left_ref, right_ref) = (
        refs[:groups],
        refs[groups : 2 * groups],
        refs[2 * groups :],
    )
    tiles = table_ref.shape[2] // LANES

    @pl.loop(0, TILES)
    def _(tile):
        for rows in row_groups(field_ref):
            lanes = lanes_at(0, tile)
            low = [a + KAPPA * b for a, b in zip(load(rim_ref, rows, lanes), load(behind_ref, rows, lanes))]
            store(field_ref, rows, lanes, low)
            hop = [None] * 6
            add_hop(hop, link_at(link_ref, 0, tiles // TILES - 1, tile), load(ahead_ref, rows, lanes), False)
            high = lanes_at(1, tile)
            store(field_ref, rows, high, [a + KAPPA * b for a, b in zip(load(rim_ref, rows, high), hop)])

    total_ref[...] = start_ref[...]
    skip = tiles - 2 * TILES
    table_tile = lambda tile: tile + jnp.where(tile >= TILES, skip, 0)
    add_products(field_ref, raw_refs, table_ref, total_ref, left_ref, right_ref, table_tile)
    turned = jnp.transpose(total_ref[...] * scale)
    width = turned.shape[0] // groups
    for g in range(groups):
        block = turned[g * width : (g + 1) * width].astype(out_refs[0].dtype)
        for slot in range(groups):

            @pl.when(slot_ref[g] == slot)
            def _():
                out_refs[slot][...] = block


def call(kernel, name, shapes, operands, flops=0, scratch=(), smem=False):
    return pl.pallas_call(
        kernel,
        out_shape=tuple(jax.ShapeDtypeStruct(shape, dtype) for shape, dtype in shapes),
        in_specs=[SMEM if smem and i == 0 else VMEM for i in range(len(operands))],
        out_specs=(VMEM,) * len(shapes),
        scratch_shapes=list(scratch),
        compiler_params=pltpu.CompilerParams(vmem_limit_bytes=VMEM_LIMIT),
        cost_estimate=pl.CostEstimate(flops=flops, bytes_accessed=1 << 20, transcendentals=0),
        name=name,
    )(*operands)


def shards(vectors, gauge_links, momenta):
    bricks, vecs, subs = (lax.axis_size(axis) for axis in ("brick", "vec", "sub"))
    groups = vecs * subs
    width, sites = vectors.shape[0], vectors.shape[3]
    layers, tiles = sites // PLANE, sites // LANES
    assert groups == bricks and layers > 2 and ITERS == 2
    total_x = bricks * layers
    count = momenta.shape[0]
    brick, vec, sub = (lax.axis_index(axis) for axis in ("brick", "vec", "sub"))
    tiled_vectors = jnp.swapaxes(vectors.reshape((width, 3, 2, tiles, LANES)), 2, 3).reshape((-1, LANES))
    links = jnp.swapaxes(gauge_links.reshape((27, 2, tiles, LANES)), 1, 2).reshape((-1, LANES))
    full, edge, rim, inner = (
        (6, width, sites),
        (6, width, PLANE),
        (6, width, 2 * PLANE),
        (6, width, sites - 2 * PLANE),
    )
    field, raw_inner, raw_rim, first, turned = call(
        open_kernel,
        "open",
        ((full, WIDE), (inner, LOW), (rim, LOW), (edge, LOW), (edge, LOW)),
        (tiled_vectors, links),
    )
    ahead = shifted(first, "brick", -1)
    behind = shifted(turned, "brick", 1)

    def gathered(raw):
        raws = [raw] + [shifted(raw, "vec", a) for a in range(1, vecs)]
        return raws + [shifted(raws[a], "sub", b) for b in range(1, subs) for a in range(vecs)]

    offsets = [(a, b) for b in range(subs) for a in range(vecs)]
    raws_inner, raws_rim = gathered(raw_inner), gathered(raw_rim)
    low, high, first, turned, back = call(
        rim_kernel,
        "rim",
        ((edge, WIDE), (edge, WIDE), (edge, LOW), (edge, LOW), ((2, 16, sites), WIDE)),
        (field, links),
        flops=1 << 24,
    )
    ahead_one = shifted(first, "brick", -1)
    behind_one = shifted(turned, "brick", 1)
    place = (brick * layers).astype(jnp.int32).reshape((1,))
    one, table = call(
        functools.partial(inner_kernel, total_x),
        "inner",
        ((inner, WIDE), ((2, count, sites), WIDE)),
        (place, field, links, back, momenta),
        flops=1 << 24,
        smem=True,
    )
    smeared, rest = call(
        second_kernel,
        "second",
        ((inner, WIDE), (rim, WIDE)),
        (field, links, back, low, high, one, ahead, behind),
        flops=1 << 25,
        scratch=(pltpu.VMEM(rim, WIDE),),
    )
    product = (count * width, groups * 2 * width)
    depth = 6 * LANES
    scratch = (pltpu.VMEM((product[0], depth), LOW), pltpu.VMEM((product[1], depth), LOW))
    (start,) = call(
        functools.partial(inner_product_kernel, groups),
        "inner_product",
        ((product, WIDE),),
        (smeared, table, *raws_inner),
        flops=1 << 32,
        scratch=scratch,
    )
    owners = jnp.stack([(vec - a) % vecs * subs + (sub - b) % subs for a, b in offsets])
    slots = ((owners - brick) % groups).astype(jnp.int32)
    scale = (3.0 * total_x * PLANE) ** (-0.5)
    blocks = call(
        functools.partial(last_product_kernel, groups, scale),
        "last_product",
        (((2 * width, count * width), LOW),) * groups,
        (slots, rest, ahead_one, behind_one, links, start, table, *raws_rim),
        flops=1 << 32,
        scratch=(pltpu.VMEM(rim, WIDE), pltpu.VMEM(product, WIDE)) + scratch,
        smem=True,
    )
    shares = []
    for slot, block in enumerate(blocks):
        pairs = [(b * groups + g, g * groups + (b + slot) % groups) for b in range(bricks) for g in range(groups)]
        shares.append(lax.ppermute(block, ("brick", "vec", "sub"), pairs))
    total = functools.reduce(jnp.add, [share.astype(WIDE) for share in shares])
    return jnp.transpose(total.reshape((2, width, count, width)), (1, 2, 0, 3))


def solution(mesh):
    in_specs = (
        P(("vec", "sub"), None, None, ("grp", "brick")),
        P(None, None, None, None, ("grp", "brick")),
        P(),
    )
    out_specs = P(("vec", "sub"), "grp", None, "brick")
    return jax.shard_map(shards, mesh=mesh, in_specs=in_specs, out_specs=out_specs, check_vma=False)
```

```python
import functools
import math

import jax
import jax.numpy as jnp
from jax import lax
from jax.experimental import pallas as pl
from jax.experimental.pallas import tpu as pltpu
from jax.sharding import PartitionSpec as P

LY = 64
LZ = 8
ITERS = 2
KAPPA = 0.125
LANES = 128
PLANE = LY * LZ
TILES = PLANE // LANES
ROWS = 16
BYTES = 1 << 20
LOW = jnp.bfloat16
WIDE = jnp.float32
STEP = 2
CHUNKS = 2
VMEM_LIMIT = 40 * 1024 * 1024
VMEM = pl.BlockSpec(memory_space=pltpu.VMEM)
SMEM = pl.BlockSpec(memory_space=pltpu.SMEM)


def shifted(array, axis, by):
    peers = lax.axis_size(axis)
    return lax.ppermute(array, axis, [(i, (i + by) % peers) for i in range(peers)])


def add_hop(total, link, field, adjoint):
    for row in range(3):
        for column in range(3):
            if adjoint:
                real, imag = link(column, row, 0), link(column, row, 1)
            else:
                real, imag = link(row, column, 0), link(row, column, 1)
            source_real, source_imag = field[2 * column], field[2 * column + 1]
            if adjoint:
                add_real = real * source_real + imag * source_imag
                add_imag = real * source_imag - imag * source_real
            else:
                add_real = real * source_real - imag * source_imag
                add_imag = real * source_imag + imag * source_real
            for part, add in ((0, add_real), (1, add_imag)):
                old = total[2 * row + part]
                total[2 * row + part] = add if old is None else old + add


def lane_roll(value, by):
    return pltpu.roll(value, by % LANES, 1)


def lanes_at(layer, tile):
    return pl.ds(pl.multiple_of(layer * PLANE + tile * LANES, LANES), LANES)


def row_groups(ref):
    size = min(ROWS, ref.shape[1])
    return [pl.ds(start, size) for start in range(0, ref.shape[1], size)]


def load(ref, rows, lanes):
    return [ref[k, rows, lanes].astype(WIDE) for k in range(6)]


def store(ref, rows, lanes, values):
    for k in range(6):
        ref[k, rows, lanes] = values[k].astype(ref.dtype)


def link_at(link_ref, direction, layer, tile):
    tiles = link_ref.shape[0] // 54

    def get(row, column, part):
        matrix = (direction * 3 + row) * 3 + column
        return link_ref[pl.ds((matrix * tiles + layer * TILES + tile) * 2 + part, 1), :]

    return get


def plane_hops(total, link_ref, back_ref, layer, tile, rows, fetch):
    here = fetch(tile)
    after, before = fetch((tile + 1) % TILES), fetch((tile + TILES - 1) % TILES)
    lane = lax.broadcasted_iota(jnp.int32, (rows.size, LANES), 1)
    ahead = [jnp.where(lane >= LANES - LZ, lane_roll(b, -LZ), lane_roll(a, -LZ)) for a, b in zip(here, after)]
    add_hop(total, link_at(link_ref, 1, layer, tile), ahead, False)
    behind = [jnp.where(lane < LZ, lane_roll(b, LZ), lane_roll(a, LZ)) for a, b in zip(here, before)]
    lanes = lanes_at(layer, tile)
    add_hop(total, lambda r, c, part: back_ref[part, pl.ds(3 * r + c, 1), lanes], behind, True)
    depth = lane % LZ
    ahead = [jnp.where(depth == LZ - 1, lane_roll(a, LZ - 1), lane_roll(a, -1)) for a in here]
    add_hop(total, link_at(link_ref, 2, layer, tile), ahead, False)
    turned = [None] * 6
    add_hop(turned, link_at(link_ref, 2, layer, tile), here, True)
    for k in range(6):
        total[k] += jnp.where(depth == 0, lane_roll(turned[k], 1 - LZ), lane_roll(turned[k], 1))
    return here


def combined(here, total):
    return [(1.0 - 6.0 * KAPPA) * a + KAPPA * b for a, b in zip(here, total)]


def first_step(layer, tile, rows, field_ref, link_ref, back_ref):
    layers = field_ref.shape[2] // PLANE
    total = [None] * 6
    if layer < layers - 1:
        source = load(field_ref, rows, lanes_at(layer + 1, tile))
        add_hop(total, link_at(link_ref, 0, layer, tile), source, False)
    if layer > 0:
        source = load(field_ref, rows, lanes_at(layer - 1, tile))
        add_hop(total, link_at(link_ref, 0, layer - 1, tile), source, True)
    fetch = lambda t: load(field_ref, rows, lanes_at(layer, t))
    return combined(plane_hops(total, link_ref, back_ref, layer, tile, rows, fetch), total)


def open_kernel(vector_ref, link_ref, field_ref, raw_ref, down_ref, up_ref, rim_ref, back_ref):
    vectors, sites = field_ref.shape[1:]
    tiles, layers = sites // LANES, sites // PLANE
    stride = 6 * tiles
    for k in range(6):
        for tile in range(tiles):
            row = ((k // 2) * tiles + tile) * 2 + k % 2
            value = vector_ref[pl.ds(row, vectors, stride=stride), :]
            field_ref[k, :, pl.ds(tile * LANES, LANES)] = value
            low = value.astype(LOW)
            raw_ref[k, :, pl.ds(tile * LANES, LANES)] = low
            if tile < TILES:
                down_ref[k, :, pl.ds(tile * LANES, LANES)] = low
    lane = lax.broadcasted_iota(jnp.int32, (9, LANES), 1)
    for layer in range(layers):
        for part in range(2):
            row = lambda tile: (9 * tiles + layer * TILES + tile) * 2 + part
            value = [link_ref[pl.ds(row(tile), 9, stride=2 * tiles), :] for tile in range(TILES)]
            value = [lane_roll(v, LZ) for v in value]
            for tile in range(TILES):
                back_ref[part, pl.ds(0, 9), lanes_at(layer, tile)] = jnp.where(lane < LZ, value[tile - 1], value[tile])

    for place, layer in enumerate((0, layers - 1)):

        @pl.loop(0, TILES)
        def _(tile):
            lanes = lanes_at(0, tile)
            for rows in row_groups(field_ref):
                new = first_step(layer, tile, rows, field_ref, link_ref, back_ref)
                store(rim_ref, rows, lanes_at(place, tile), new)
                if place == 0:
                    store(down_ref.at[pl.ds(6, 6)], rows, lanes, new)
                else:
                    here = load(field_ref, rows, lanes_at(layer, tile))
                    for part, source in enumerate((here, new)):
                        turned = [None] * 6
                        add_hop(turned, link_at(link_ref, 0, layer, tile), source, True)
                        store(up_ref.at[pl.ds(6 * part, 6)], rows, lanes, turned)


def unit_phase(turns):
    half = math.pi * (turns - jnp.round(turns))
    square = half * half
    cosine, sine = 1.0, 1.0
    for order in range(12, 0, -2):
        sine = 1.0 - square * sine * (1.0 / (order * (order + 1)))
        cosine = 1.0 - square * cosine * (1.0 / (order * (order - 1)))
    sine = half * sine
    return 1.0 - 2.0 * sine * sine, 2.0 * sine * cosine


def local_kernel(
    total_x, place_ref, field_ref, link_ref, back_ref, rim_ref, momenta_ref, out_ref, table_ref, one_ref
):
    layers = field_ref.shape[2] // PLANE
    count = momenta_ref.shape[0]
    momenta = momenta_ref[...].astype(WIDE)
    lane = lax.broadcasted_iota(jnp.int32, (count, LANES), 1)

    @pl.loop(0, TILES)
    def _(tile):
        column = (tile * (LANES // LZ) + lane // LZ).astype(WIDE)
        depth = (lane % LZ).astype(WIDE)
        turns = [momenta[:, 1:2] * column / LY, momenta[:, 2:3] * depth / LZ]
        part = sum(t - jnp.round(t) for t in turns)
        for layer in range(layers):
            along = momenta[:, 0:1] * (place_ref[0] + layer).astype(WIDE) / total_x
            cosine, sine = unit_phase(along - jnp.round(along) + part)
            table_ref[0, :, lanes_at(layer, tile)] = cosine
            table_ref[1, :, lanes_at(layer, tile)] = sine


    one_ref[:, :, pl.ds(0, PLANE)] = rim_ref[:, :, pl.ds(0, PLANE)]
    one_ref[:, :, pl.ds((layers - 1) * PLANE, PLANE)] = rim_ref[:, :, pl.ds(PLANE, PLANE)]
    for layer in range(1, layers - 1):

        @pl.loop(0, TILES)
        def _(tile):
            for rows in row_groups(field_ref):
                new = first_step(layer, tile, rows, field_ref, link_ref, back_ref)
                store(one_ref, rows, lanes_at(layer, tile), new)

    for layer in range(layers):

        @pl.loop(0, TILES)
        def _(tile):
            for rows in row_groups(field_ref):
                new = first_step(layer, tile, rows, one_ref, link_ref, back_ref)
                if layer in (0, layers - 1):
                    own = load(field_ref, rows, lanes_at(layer, tile))
                    new = [a + KAPPA * KAPPA * b for a, b in zip(new, own)]
                store(out_ref, rows, lanes_at(layer, tile), new)


def close_kernel(part_ref, ahead_ref, behind_ref, link_ref, back_ref, out_ref, change_ref):
    layers = part_ref.shape[2] // PLANE
    fresh, older = pl.ds(6, 6), pl.ds(0, 6)

    @pl.loop(0, TILES)
    def _(tile):
        lanes = lanes_at(0, tile)
        for rows in row_groups(part_ref):
            low = load(behind_ref.at[older], rows, lanes)
            store(change_ref, rows, lanes, [KAPPA * a for a in low])
            high = [None] * 6
            add_hop(high, link_at(link_ref, 0, layers - 1, tile), load(ahead_ref.at[older], rows, lanes), False)
            store(change_ref, rows, lanes_at(1, tile), [KAPPA * a for a in high])

    for layer in range(layers):

        @pl.loop(0, TILES)
        def _(tile):
            lanes = lanes_at(0, tile)
            for rows in row_groups(part_ref):
                new = load(part_ref, rows, lanes_at(layer, tile))
                change = lambda place, t: load(change_ref, rows, lanes_at(place, t))
                hops = [None] * 6
                if layer == 1:
                    add_hop(hops, link_at(link_ref, 0, 0, tile), change(0, tile), True)
                if layer == layers - 2:
                    add_hop(hops, link_at(link_ref, 0, layer, tile), change(1, tile), False)
                if layer == 0:
                    came = load(behind_ref.at[fresh], rows, lanes)
                    hops = came if hops[0] is None else [a + b for a, b in zip(hops, came)]
                if layer == layers - 1:
                    add_hop(hops, link_at(link_ref, 0, layer, tile), load(ahead_ref.at[fresh], rows, lanes), False)
                for place, edge in ((0, 0), (1, layers - 1)):
                    if layer == edge:
                        here = plane_hops(hops, link_ref, back_ref, layer, tile, rows, lambda t: change(place, t))
                        new = [a + (1.0 - 6.0 * KAPPA) * b for a, b in zip(new, here)]
                if hops[0] is not None:
                    new = [a + KAPPA * b for a, b in zip(new, hops)]
                store(out_ref, rows, lanes_at(layer, tile), new)


def product_kernel(groups, begin, count, scale, slot_ref, field_ref, table_ref, *refs):
    raw_refs, out_refs, (total_ref, left_ref, right_ref) = refs[:groups], refs[groups : 2 * groups], refs[2 * groups :]
    vectors = field_ref.shape[1]
    depth = 6 * LANES
    step = left_ref.shape[1] // depth
    total_ref[...] = jnp.zeros_like(total_ref)

    @pl.loop(0, field_ref.shape[2] // LANES // step)
    def _(block):
        for part in range(step):
            lanes = pl.ds(pl.multiple_of((block * step + part) * LANES, LANES), LANES)
            field = [field_ref[k, :, lanes] for k in range(6)]
            one = [pl.ds(part * depth + 2 * color * LANES, LANES) for color in range(3)]
            two = [pl.ds(part * depth + (2 * color + 1) * LANES, LANES) for color in range(3)]
            for p in range(count):
                cosine = table_ref[0, pl.ds(begin + p, 1), lanes]
                sine = table_ref[1, pl.ds(begin + p, 1), lanes]
                rows = pl.ds(p * vectors, vectors)
                for color in range(3):
                    real, imag = field[2 * color], field[2 * color + 1]
                    right_ref[rows, one[color]] = (cosine * real + sine * imag).astype(LOW)
                    right_ref[rows, two[color]] = (cosine * imag - sine * real).astype(LOW)
            for g, raw_ref in enumerate(raw_refs):
                width = raw_ref.shape[1]
                first = pl.ds(2 * g * width, width)
                second = pl.ds((2 * g + 1) * width, width)
                for color in range(3):
                    real, imag = raw_ref[2 * color, :, lanes], raw_ref[2 * color + 1, :, lanes]
                    left_ref[first, one[color]] = real
                    left_ref[first, two[color]] = imag
                    left_ref[second, one[color]] = -imag
                    left_ref[second, two[color]] = real
        total_ref[...] += lax.dot_general(
            left_ref[...], right_ref[...], (((1,), (1,)), ((), ())), preferred_element_type=WIDE
        )

    width = total_ref.shape[0] // groups
    for g in range(groups):
        block = (total_ref[pl.ds(g * width, width), :] * scale).astype(out_refs[0].dtype)
        for slot in range(groups):

            @pl.when(slot_ref[g] == slot)
            def _():
                out_refs[slot][...] = block


def call(kernel, name, shapes, operands, flops=0, scratch=(), smem=False):
    return pl.pallas_call(
        kernel,
        out_shape=tuple(jax.ShapeDtypeStruct(shape, dtype) for shape, dtype in shapes),
        in_specs=[SMEM if smem and i == 0 else VMEM for i in range(len(operands))],
        out_specs=(VMEM,) * len(shapes),
        scratch_shapes=list(scratch),
        compiler_params=pltpu.CompilerParams(vmem_limit_bytes=VMEM_LIMIT),
        cost_estimate=pl.CostEstimate(flops=flops, bytes_accessed=BYTES, transcendentals=0),
        name=name,
    )(*operands)


def shards(vectors, gauge_links, momenta):
    bricks, vecs, subs = (lax.axis_size(axis) for axis in ("brick", "vec", "sub"))
    groups = vecs * subs
    width, sites = vectors.shape[0], vectors.shape[3]
    layers, tiles = sites // PLANE, sites // LANES
    assert groups == bricks and layers > 1 and ITERS == 2
    total_x = bricks * layers
    count = momenta.shape[0]
    brick, vec, sub = (lax.axis_index(axis) for axis in ("brick", "vec", "sub"))
    tiled_vectors = jnp.swapaxes(vectors.reshape((width, 3, 2, tiles, LANES)), 2, 3).reshape((-1, LANES))
    links = jnp.swapaxes(gauge_links.reshape((27, 2, tiles, LANES)), 1, 2).reshape((-1, LANES))
    full, faces = (6, width, sites), (12, width, PLANE)
    field, raw, down, up, rim, back = call(
        open_kernel,
        "open",
        ((full, WIDE), (full, LOW), (faces, LOW), (faces, LOW), ((6, width, 2 * PLANE), WIDE), ((2, 16, sites), WIDE)),
        (tiled_vectors, links),
        flops=1 << 24,
    )
    ahead, behind = shifted(down, "brick", -1), shifted(up, "brick", 1)
    across = [shifted(raw, "vec", a) for a in range(1, vecs)]
    beside = [shifted(raw, "sub", b) for b in range(1, subs)]
    place = (brick * layers).astype(jnp.int32).reshape((1,))
    part, table = call(
        functools.partial(local_kernel, total_x),
        "local",
        ((full, WIDE), ((2, count, sites), WIDE)),
        (place, field, links, back, rim, momenta),
        flops=1 << 25,
        scratch=(pltpu.VMEM(full, WIDE),),
        smem=True,
    )
    *across, ahead, behind, part = lax.optimization_barrier((*across, ahead, behind, part))
    raws = [raw, *across, *beside]
    raws += [shifted(array, "sub", b) for b in range(1, subs) for array in across]
    offsets = [(a, 0) for a in range(vecs)] + [(0, b) for b in range(1, subs)]
    offsets += [(a, b) for b in range(1, subs) for a in range(1, vecs)]
    (smeared,) = call(
        close_kernel,
        "close",
        ((full, WIDE),),
        (part, ahead, behind, links, back),
        flops=1 << 24,
        scratch=(pltpu.VMEM((6, width, 2 * PLANE), WIDE),),
    )
    owners = jnp.stack([(vec - a) % vecs * subs + (sub - b) % subs for a, b in offsets])
    slots = ((owners - brick) % groups).astype(jnp.int32)
    scale = (3.0 * total_x * PLANE) ** (-0.5)
    depth = STEP * 6 * LANES
    totals = []
    bounds = [count * n // CHUNKS for n in range(CHUNKS + 1)]
    for begin, end in zip(bounds[:-1], bounds[1:]):
        columns = (end - begin) * width
        blocks = call(
            functools.partial(product_kernel, groups, begin, end - begin, scale),
            "product",
            (((2 * width, columns), LOW),) * groups,
            (slots, smeared, table, *raws),
            flops=1 << 31,
            scratch=(
                pltpu.VMEM((groups * 2 * width, columns), WIDE),
                pltpu.VMEM((groups * 2 * width, depth), LOW),
                pltpu.VMEM((columns, depth), LOW),
            ),
            smem=True,
        )
        shares = []
        for slot, block in enumerate(blocks):
            pairs = [(b * groups + g, g * groups + (b + slot) % groups) for b in range(bricks) for g in range(groups)]
            shares.append(lax.ppermute(block, ("brick", "vec", "sub"), pairs))
        total = functools.reduce(jnp.add, [share.astype(WIDE) for share in shares])
        totals.append(total.reshape((2, width, end - begin, width)))
    return jnp.transpose(jnp.concatenate(totals, axis=2), (1, 2, 0, 3))


def solution(mesh):
    in_specs = (
        P(("vec", "sub"), None, None, ("grp", "brick")),
        P(None, None, None, None, ("grp", "brick")),
        P(),
    )
    out_specs = P(("vec", "sub"), "grp", None, "brick")
    return jax.shard_map(shards, mesh=mesh, in_specs=in_specs, out_specs=out_specs, check_vma=False)
```

```python
import functools
import math

import jax
import jax.numpy as jnp
from jax import lax
from jax.experimental import pallas as pl
from jax.experimental.pallas import tpu as pltpu
from jax.sharding import PartitionSpec as P

LY = 64
LZ = 8
ITERS = 2
KAPPA = 0.125
LANES = 128
PLANE = LY * LZ
TILES = PLANE // LANES
ROWS = 16
BYTES = 1 << 20
LOW = jnp.bfloat16
WIDE = jnp.float32
STEP = 2
CHUNKS = 1
VMEM_LIMIT = 40 * 1024 * 1024
VMEM = pl.BlockSpec(memory_space=pltpu.VMEM)
SMEM = pl.BlockSpec(memory_space=pltpu.SMEM)


def shifted(array, axis, by):
    peers = lax.axis_size(axis)
    return lax.ppermute(array, axis, [(i, (i + by) % peers) for i in range(peers)])


def add_hop(total, link, field, adjoint):
    for row in range(3):
        for column in range(3):
            if adjoint:
                real, imag = link(column, row, 0), link(column, row, 1)
            else:
                real, imag = link(row, column, 0), link(row, column, 1)
            source_real, source_imag = field[2 * column], field[2 * column + 1]
            if adjoint:
                add_real = real * source_real + imag * source_imag
                add_imag = real * source_imag - imag * source_real
            else:
                add_real = real * source_real - imag * source_imag
                add_imag = real * source_imag + imag * source_real
            for part, add in ((0, add_real), (1, add_imag)):
                old = total[2 * row + part]
                total[2 * row + part] = add if old is None else old + add


def lane_roll(value, by):
    return pltpu.roll(value, by % LANES, 1)


def lanes_at(layer, tile):
    return pl.ds(pl.multiple_of(layer * PLANE + tile * LANES, LANES), LANES)


def row_groups(ref):
    size = min(ROWS, ref.shape[1])
    return [pl.ds(start, size) for start in range(0, ref.shape[1], size)]


def load(ref, rows, lanes):
    return [ref[k, rows, lanes].astype(WIDE) for k in range(6)]


def store(ref, rows, lanes, values):
    for k in range(6):
        ref[k, rows, lanes] = values[k].astype(ref.dtype)


def link_at(link_ref, direction, layer, tile):
    tiles = link_ref.shape[0] // 54

    def get(row, column, part):
        matrix = (direction * 3 + row) * 3 + column
        return link_ref[pl.ds((matrix * tiles + layer * TILES + tile) * 2 + part, 1), :]

    return get


def plane_hops(total, link_ref, back_ref, layer, tile, rows, fetch):
    here = fetch(tile)
    after, before = fetch((tile + 1) % TILES), fetch((tile + TILES - 1) % TILES)
    lane = lax.broadcasted_iota(jnp.int32, (rows.size, LANES), 1)
    ahead = [jnp.where(lane >= LANES - LZ, lane_roll(b, -LZ), lane_roll(a, -LZ)) for a, b in zip(here, after)]
    add_hop(total, link_at(link_ref, 1, layer, tile), ahead, False)
    behind = [jnp.where(lane < LZ, lane_roll(b, LZ), lane_roll(a, LZ)) for a, b in zip(here, before)]
    lanes = lanes_at(layer, tile)
    add_hop(total, lambda r, c, part: back_ref[part, pl.ds(3 * r + c, 1), lanes], behind, True)
    depth = lane % LZ
    ahead = [jnp.where(depth == LZ - 1, lane_roll(a, LZ - 1), lane_roll(a, -1)) for a in here]
    add_hop(total, link_at(link_ref, 2, layer, tile), ahead, False)
    turned = [None] * 6
    add_hop(turned, link_at(link_ref, 2, layer, tile), here, True)
    for k in range(6):
        total[k] += jnp.where(depth == 0, lane_roll(turned[k], 1 - LZ), lane_roll(turned[k], 1))
    return here


def combined(here, total):
    return [(1.0 - 6.0 * KAPPA) * a + KAPPA * b for a, b in zip(here, total)]


def first_step(layer, tile, rows, field_ref, link_ref, back_ref):
    layers = field_ref.shape[2] // PLANE
    total = [None] * 6
    if layer < layers - 1:
        source = load(field_ref, rows, lanes_at(layer + 1, tile))
        add_hop(total, link_at(link_ref, 0, layer, tile), source, False)
    if layer > 0:
        source = load(field_ref, rows, lanes_at(layer - 1, tile))
        add_hop(total, link_at(link_ref, 0, layer - 1, tile), source, True)
    fetch = lambda t: load(field_ref, rows, lanes_at(layer, t))
    return combined(plane_hops(total, link_ref, back_ref, layer, tile, rows, fetch), total)


def open_kernel(vector_ref, link_ref, field_ref, raw_ref, down_ref, up_ref, rim_ref, back_ref):
    vectors, sites = field_ref.shape[1:]
    tiles, layers = sites // LANES, sites // PLANE
    stride = 6 * tiles
    for k in range(6):
        for tile in range(tiles):
            row = ((k // 2) * tiles + tile) * 2 + k % 2
            value = vector_ref[pl.ds(row, vectors, stride=stride), :]
            field_ref[k, :, pl.ds(tile * LANES, LANES)] = value
            low = value.astype(LOW)
            raw_ref[k, :, pl.ds(tile * LANES, LANES)] = low
            if tile < TILES:
                down_ref[k, :, pl.ds(tile * LANES, LANES)] = low
    lane = lax.broadcasted_iota(jnp.int32, (9, LANES), 1)
    for layer in range(layers):
        for part in range(2):
            row = lambda tile: (9 * tiles + layer * TILES + tile) * 2 + part
            value = [link_ref[pl.ds(row(tile), 9, stride=2 * tiles), :] for tile in range(TILES)]
            value = [lane_roll(v, LZ) for v in value]
            for tile in range(TILES):
                back_ref[part, pl.ds(0, 9), lanes_at(layer, tile)] = jnp.where(lane < LZ, value[tile - 1], value[tile])

    for place, layer in enumerate((0, layers - 1)):

        @pl.loop(0, TILES)
        def _(tile):
            lanes = lanes_at(0, tile)
            for rows in row_groups(field_ref):
                new = first_step(layer, tile, rows, field_ref, link_ref, back_ref)
                store(rim_ref, rows, lanes_at(place, tile), new)
                if place == 0:
                    store(down_ref.at[pl.ds(6, 6)], rows, lanes, new)
                else:
                    here = load(field_ref, rows, lanes_at(layer, tile))
                    for part, source in enumerate((here, new)):
                        turned = [None] * 6
                        add_hop(turned, link_at(link_ref, 0, layer, tile), source, True)
                        store(up_ref.at[pl.ds(6 * part, 6)], rows, lanes, turned)


def unit_phase(turns):
    half = math.pi * (turns - jnp.round(turns))
    square = half * half
    cosine, sine = 1.0, 1.0
    for order in range(12, 0, -2):
        sine = 1.0 - square * sine * (1.0 / (order * (order + 1)))
        cosine = 1.0 - square * cosine * (1.0 / (order * (order - 1)))
    sine = half * sine
    return 1.0 - 2.0 * sine * sine, 2.0 * sine * cosine


def local_kernel(
    total_x, place_ref, field_ref, link_ref, back_ref, rim_ref, momenta_ref, out_ref, table_ref, one_ref
):
    layers = field_ref.shape[2] // PLANE
    count = momenta_ref.shape[0]
    momenta = momenta_ref[...].astype(WIDE)
    lane = lax.broadcasted_iota(jnp.int32, (count, LANES), 1)

    @pl.loop(0, TILES)
    def _(tile):
        column = (tile * (LANES // LZ) + lane // LZ).astype(WIDE)
        depth = (lane % LZ).astype(WIDE)
        turns = [momenta[:, 1:2] * column / LY, momenta[:, 2:3] * depth / LZ]
        part = sum(t - jnp.round(t) for t in turns)
        for layer in range(layers):
            along = momenta[:, 0:1] * (place_ref[0] + layer).astype(WIDE) / total_x
            cosine, sine = unit_phase(along - jnp.round(along) + part)
            table_ref[0, :, lanes_at(layer, tile)] = cosine
            table_ref[1, :, lanes_at(layer, tile)] = sine


    one_ref[:, :, pl.ds(0, PLANE)] = rim_ref[:, :, pl.ds(0, PLANE)]
    one_ref[:, :, pl.ds((layers - 1) * PLANE, PLANE)] = rim_ref[:, :, pl.ds(PLANE, PLANE)]
    for layer in range(1, layers - 1):

        @pl.loop(0, TILES)
        def _(tile):
            for rows in row_groups(field_ref):
                new = first_step(layer, tile, rows, field_ref, link_ref, back_ref)
                store(one_ref, rows, lanes_at(layer, tile), new)

    for layer in range(layers):

        @pl.loop(0, TILES)
        def _(tile):
            for rows in row_groups(field_ref):
                new = first_step(layer, tile, rows, one_ref, link_ref, back_ref)
                if layer in (0, layers - 1):
                    own = load(field_ref, rows, lanes_at(layer, tile))
                    new = [a + KAPPA * KAPPA * b for a, b in zip(new, own)]
                store(out_ref, rows, lanes_at(layer, tile), new)


def close_kernel(part_ref, ahead_ref, behind_ref, link_ref, back_ref, out_ref, change_ref):
    layers = part_ref.shape[2] // PLANE
    fresh, older = pl.ds(6, 6), pl.ds(0, 6)

    @pl.loop(0, TILES)
    def _(tile):
        lanes = lanes_at(0, tile)
        for rows in row_groups(part_ref):
            low = load(behind_ref.at[older], rows, lanes)
            store(change_ref, rows, lanes, [KAPPA * a for a in low])
            high = [None] * 6
            add_hop(high, link_at(link_ref, 0, layers - 1, tile), load(ahead_ref.at[older], rows, lanes), False)
            store(change_ref, rows, lanes_at(1, tile), [KAPPA * a for a in high])

    for layer in range(layers):

        @pl.loop(0, TILES)
        def _(tile):
            lanes = lanes_at(0, tile)
            for rows in row_groups(part_ref):
                new = load(part_ref, rows, lanes_at(layer, tile))
                change = lambda place, t: load(change_ref, rows, lanes_at(place, t))
                hops = [None] * 6
                if layer == 1:
                    add_hop(hops, link_at(link_ref, 0, 0, tile), change(0, tile), True)
                if layer == layers - 2:
                    add_hop(hops, link_at(link_ref, 0, layer, tile), change(1, tile), False)
                if layer == 0:
                    came = load(behind_ref.at[fresh], rows, lanes)
                    hops = came if hops[0] is None else [a + b for a, b in zip(hops, came)]
                if layer == layers - 1:
                    add_hop(hops, link_at(link_ref, 0, layer, tile), load(ahead_ref.at[fresh], rows, lanes), False)
                for place, edge in ((0, 0), (1, layers - 1)):
                    if layer == edge:
                        here = plane_hops(hops, link_ref, back_ref, layer, tile, rows, lambda t: change(place, t))
                        new = [a + (1.0 - 6.0 * KAPPA) * b for a, b in zip(new, here)]
                if hops[0] is not None:
                    new = [a + KAPPA * b for a, b in zip(new, hops)]
                store(out_ref, rows, lanes_at(layer, tile), new)


def product_kernel(groups, begin, count, scale, slot_ref, field_ref, table_ref, *refs):
    raw_refs, out_refs, (total_ref, left_ref, right_ref) = refs[:groups], refs[groups : 2 * groups], refs[2 * groups :]
    vectors = field_ref.shape[1]
    depth = 6 * LANES
    step = left_ref.shape[1] // depth
    total_ref[...] = jnp.zeros_like(total_ref)

    @pl.loop(0, field_ref.shape[2] // LANES // step)
    def _(block):
        for part in range(step):
            lanes = pl.ds(pl.multiple_of((block * step + part) * LANES, LANES), LANES)
            field = [field_ref[k, :, lanes] for k in range(6)]
            one = [pl.ds(part * depth + 2 * color * LANES, LANES) for color in range(3)]
            two = [pl.ds(part * depth + (2 * color + 1) * LANES, LANES) for color in range(3)]
            for p in range(count):
                cosine = table_ref[0, pl.ds(begin + p, 1), lanes]
                sine = table_ref[1, pl.ds(begin + p, 1), lanes]
                rows = pl.ds(p * vectors, vectors)
                for color in range(3):
                    real, imag = field[2 * color], field[2 * color + 1]
                    right_ref[rows, one[color]] = (cosine * real + sine * imag).astype(LOW)
                    right_ref[rows, two[color]] = (cosine * imag - sine * real).astype(LOW)
            for g, raw_ref in enumerate(raw_refs):
                width = raw_ref.shape[1]
                first = pl.ds(2 * g * width, width)
                second = pl.ds((2 * g + 1) * width, width)
                for color in range(3):
                    real, imag = raw_ref[2 * color, :, lanes], raw_ref[2 * color + 1, :, lanes]
                    left_ref[first, one[color]] = real
                    left_ref[first, two[color]] = imag
                    left_ref[second, one[color]] = -imag
                    left_ref[second, two[color]] = real
        total_ref[...] += lax.dot_general(
            left_ref[...], right_ref[...], (((1,), (1,)), ((), ())), preferred_element_type=WIDE
        )

    width = total_ref.shape[0] // groups
    for g in range(groups):
        block = (total_ref[pl.ds(g * width, width), :] * scale).astype(out_refs[0].dtype)
        for slot in range(groups):

            @pl.when(slot_ref[g] == slot)
            def _():
                out_refs[slot][...] = block


def call(kernel, name, shapes, operands, flops=0, scratch=(), smem=False):
    return pl.pallas_call(
        kernel,
        out_shape=tuple(jax.ShapeDtypeStruct(shape, dtype) for shape, dtype in shapes),
        in_specs=[SMEM if smem and i == 0 else VMEM for i in range(len(operands))],
        out_specs=(VMEM,) * len(shapes),
        scratch_shapes=list(scratch),
        compiler_params=pltpu.CompilerParams(vmem_limit_bytes=VMEM_LIMIT),
        cost_estimate=pl.CostEstimate(flops=flops, bytes_accessed=BYTES, transcendentals=0),
        name=name,
    )(*operands)


def shards(vectors, gauge_links, momenta):
    bricks, vecs, subs = (lax.axis_size(axis) for axis in ("brick", "vec", "sub"))
    groups = vecs * subs
    width, sites = vectors.shape[0], vectors.shape[3]
    layers, tiles = sites // PLANE, sites // LANES
    assert groups == bricks and layers > 1 and ITERS == 2
    total_x = bricks * layers
    count = momenta.shape[0]
    brick, vec, sub = (lax.axis_index(axis) for axis in ("brick", "vec", "sub"))
    tiled_vectors = jnp.swapaxes(vectors.reshape((width, 3, 2, tiles, LANES)), 2, 3).reshape((-1, LANES))
    links = jnp.swapaxes(gauge_links.reshape((27, 2, tiles, LANES)), 1, 2).reshape((-1, LANES))
    full, faces = (6, width, sites), (12, width, PLANE)
    field, raw, down, up, rim, back = call(
        open_kernel,
        "open",
        ((full, WIDE), (full, LOW), (faces, LOW), (faces, LOW), ((6, width, 2 * PLANE), WIDE), ((2, 16, sites), WIDE)),
        (tiled_vectors, links),
        flops=1 << 24,
    )
    ahead, behind = shifted(down, "brick", -1), shifted(up, "brick", 1)
    across = [shifted(raw, "vec", a) for a in range(1, vecs)]
    beside = [shifted(raw, "sub", b) for b in range(1, subs)]
    place = (brick * layers).astype(jnp.int32).reshape((1,))
    part, table = call(
        functools.partial(local_kernel, total_x),
        "local",
        ((full, WIDE), ((2, count, sites), WIDE)),
        (place, field, links, back, rim, momenta),
        flops=1 << 25,
        scratch=(pltpu.VMEM(full, WIDE),),
        smem=True,
    )
    *across, ahead, behind, part = lax.optimization_barrier((*across, ahead, behind, part))
    raws = [raw, *across, *beside]
    raws += [shifted(array, "sub", b) for b in range(1, subs) for array in across]
    offsets = [(a, 0) for a in range(vecs)] + [(0, b) for b in range(1, subs)]
    offsets += [(a, b) for b in range(1, subs) for a in range(1, vecs)]
    (smeared,) = call(
        close_kernel,
        "close",
        ((full, WIDE),),
        (part, ahead, behind, links, back),
        flops=1 << 24,
        scratch=(pltpu.VMEM((6, width, 2 * PLANE), WIDE),),
    )
    owners = jnp.stack([(vec - a) % vecs * subs + (sub - b) % subs for a, b in offsets])
    slots = ((owners - brick) % groups).astype(jnp.int32)
    scale = (3.0 * total_x * PLANE) ** (-0.5)
    depth = STEP * 6 * LANES
    totals = []
    bounds = [count * n // CHUNKS for n in range(CHUNKS + 1)]
    for begin, end in zip(bounds[:-1], bounds[1:]):
        columns = (end - begin) * width
        blocks = call(
            functools.partial(product_kernel, groups, begin, end - begin, scale),
            "product",
            (((2 * width, columns), LOW),) * groups,
            (slots, smeared, table, *raws),
            flops=1 << 31,
            scratch=(
                pltpu.VMEM((groups * 2 * width, columns), WIDE),
                pltpu.VMEM((groups * 2 * width, depth), LOW),
                pltpu.VMEM((columns, depth), LOW),
            ),
            smem=True,
        )
        shares = []
        for slot, block in enumerate(blocks):
            pairs = [(b * groups + g, g * groups + (b + slot) % groups) for b in range(bricks) for g in range(groups)]
            shares.append(lax.ppermute(block, ("brick", "vec", "sub"), pairs))
        total = functools.reduce(jnp.add, [share.astype(WIDE) for share in shares])
        totals.append(total.reshape((2, width, end - begin, width)))
    return jnp.transpose(jnp.concatenate(totals, axis=2), (1, 2, 0, 3))


def solution(mesh):
    in_specs = (
        P(("vec", "sub"), None, None, ("grp", "brick")),
        P(None, None, None, None, ("grp", "brick")),
        P(),
    )
    out_specs = P(("vec", "sub"), "grp", None, "brick")
    return jax.shard_map(shards, mesh=mesh, in_specs=in_specs, out_specs=out_specs, check_vma=False)
```

```python
import functools
import math

import jax
import jax.numpy as jnp
from jax import lax
from jax.experimental import pallas as pl
from jax.experimental.pallas import tpu as pltpu
from jax.sharding import PartitionSpec as P

LY = 64
LZ = 8
ITERS = 2
KAPPA = 0.125
LANES = 128
PLANE = LY * LZ
TILES = PLANE // LANES
ROWS = 16
BYTES = 1 << 20
LOW = jnp.bfloat16
WIDE = jnp.float32
STEP = 2
VMEM_LIMIT = 40 * 1024 * 1024
VMEM = pl.BlockSpec(memory_space=pltpu.VMEM)
SMEM = pl.BlockSpec(memory_space=pltpu.SMEM)


def shifted(array, axis, by):
    peers = lax.axis_size(axis)
    return lax.ppermute(array, axis, [(i, (i + by) % peers) for i in range(peers)])


def add_hop(total, link, field, adjoint):
    for row in range(3):
        for column in range(3):
            if adjoint:
                real, imag = link(column, row, 0), link(column, row, 1)
            else:
                real, imag = link(row, column, 0), link(row, column, 1)
            source_real, source_imag = field[2 * column], field[2 * column + 1]
            if adjoint:
                add_real = real * source_real + imag * source_imag
                add_imag = real * source_imag - imag * source_real
            else:
                add_real = real * source_real - imag * source_imag
                add_imag = real * source_imag + imag * source_real
            for part, add in ((0, add_real), (1, add_imag)):
                old = total[2 * row + part]
                total[2 * row + part] = add if old is None else old + add


def lane_roll(value, by):
    return pltpu.roll(value, by % LANES, 1)


def lanes_at(layer, tile):
    return pl.ds(pl.multiple_of(layer * PLANE + tile * LANES, LANES), LANES)


def row_groups(ref):
    size = min(ROWS, ref.shape[1])
    return [pl.ds(start, size) for start in range(0, ref.shape[1], size)]


def load(ref, rows, lanes):
    return [ref[k, rows, lanes].astype(WIDE) for k in range(6)]


def store(ref, rows, lanes, values):
    for k in range(6):
        ref[k, rows, lanes] = values[k].astype(ref.dtype)


def link_at(link_ref, direction, layer, tile):
    tiles = link_ref.shape[0] // 54

    def get(row, column, part):
        matrix = (direction * 3 + row) * 3 + column
        return link_ref[pl.ds((matrix * tiles + layer * TILES + tile) * 2 + part, 1), :]

    return get


def plane_hops(total, link_ref, back_ref, layer, tile, rows, fetch):
    here = fetch(tile)
    after, before = fetch((tile + 1) % TILES), fetch((tile + TILES - 1) % TILES)
    lane = lax.broadcasted_iota(jnp.int32, (rows.size, LANES), 1)
    ahead = [jnp.where(lane >= LANES - LZ, lane_roll(b, -LZ), lane_roll(a, -LZ)) for a, b in zip(here, after)]
    add_hop(total, link_at(link_ref, 1, layer, tile), ahead, False)
    behind = [jnp.where(lane < LZ, lane_roll(b, LZ), lane_roll(a, LZ)) for a, b in zip(here, before)]
    lanes = lanes_at(layer, tile)
    add_hop(total, lambda r, c, part: back_ref[part, pl.ds(3 * r + c, 1), lanes], behind, True)
    depth = lane % LZ
    ahead = [jnp.where(depth == LZ - 1, lane_roll(a, LZ - 1), lane_roll(a, -1)) for a in here]
    add_hop(total, link_at(link_ref, 2, layer, tile), ahead, False)
    turned = [None] * 6
    add_hop(turned, link_at(link_ref, 2, layer, tile), here, True)
    for k in range(6):
        total[k] += jnp.where(depth == 0, lane_roll(turned[k], 1 - LZ), lane_roll(turned[k], 1))
    return here


def combined(here, total):
    return [(1.0 - 6.0 * KAPPA) * a + KAPPA * b for a, b in zip(here, total)]


def first_step(layer, tile, rows, field_ref, link_ref, back_ref):
    layers = field_ref.shape[2] // PLANE
    total = [None] * 6
    if layer < layers - 1:
        source = load(field_ref, rows, lanes_at(layer + 1, tile))
        add_hop(total, link_at(link_ref, 0, layer, tile), source, False)
    if layer > 0:
        source = load(field_ref, rows, lanes_at(layer - 1, tile))
        add_hop(total, link_at(link_ref, 0, layer - 1, tile), source, True)
    fetch = lambda t: load(field_ref, rows, lanes_at(layer, t))
    return combined(plane_hops(total, link_ref, back_ref, layer, tile, rows, fetch), total)


def open_kernel(vector_ref, link_ref, field_ref, raw_ref, down_ref, up_ref, rim_ref, back_ref):
    vectors, sites = field_ref.shape[1:]
    tiles, layers = sites // LANES, sites // PLANE
    stride = 6 * tiles
    for k in range(6):
        for tile in range(tiles):
            row = ((k // 2) * tiles + tile) * 2 + k % 2
            value = vector_ref[pl.ds(row, vectors, stride=stride), :]
            field_ref[k, :, pl.ds(tile * LANES, LANES)] = value
            low = value.astype(LOW)
            raw_ref[k, :, pl.ds(tile * LANES, LANES)] = low
            if tile < TILES:
                down_ref[k, :, pl.ds(tile * LANES, LANES)] = low
    lane = lax.broadcasted_iota(jnp.int32, (9, LANES), 1)
    for layer in range(layers):
        for part in range(2):
            row = lambda tile: (9 * tiles + layer * TILES + tile) * 2 + part
            value = [link_ref[pl.ds(row(tile), 9, stride=2 * tiles), :] for tile in range(TILES)]
            value = [lane_roll(v, LZ) for v in value]
            for tile in range(TILES):
                back_ref[part, pl.ds(0, 9), lanes_at(layer, tile)] = jnp.where(lane < LZ, value[tile - 1], value[tile])

    for place, layer in enumerate((0, layers - 1)):

        @pl.loop(0, TILES)
        def _(tile):
            lanes = lanes_at(0, tile)
            for rows in row_groups(field_ref):
                new = first_step(layer, tile, rows, field_ref, link_ref, back_ref)
                store(rim_ref, rows, lanes_at(place, tile), new)
                if place == 0:
                    store(down_ref.at[pl.ds(6, 6)], rows, lanes, new)
                else:
                    here = load(field_ref, rows, lanes_at(layer, tile))
                    for part, source in enumerate((here, new)):
                        turned = [None] * 6
                        add_hop(turned, link_at(link_ref, 0, layer, tile), source, True)
                        store(up_ref.at[pl.ds(6 * part, 6)], rows, lanes, turned)


def unit_phase(turns):
    half = math.pi * (turns - jnp.round(turns))
    square = half * half
    cosine, sine = 1.0, 1.0
    for order in range(12, 0, -2):
        sine = 1.0 - square * sine * (1.0 / (order * (order + 1)))
        cosine = 1.0 - square * cosine * (1.0 / (order * (order - 1)))
    sine = half * sine
    return 1.0 - 2.0 * sine * sine, 2.0 * sine * cosine


def local_kernel(
    total_x, place_ref, field_ref, link_ref, back_ref, rim_ref, momenta_ref, out_ref, table_ref, one_ref
):
    layers = field_ref.shape[2] // PLANE
    count = momenta_ref.shape[0]
    momenta = momenta_ref[...].astype(WIDE)
    lane = lax.broadcasted_iota(jnp.int32, (count, LANES), 1)

    @pl.loop(0, TILES)
    def _(tile):
        column = (tile * (LANES // LZ) + lane // LZ).astype(WIDE)
        depth = (lane % LZ).astype(WIDE)
        turns = [momenta[:, 1:2] * column / LY, momenta[:, 2:3] * depth / LZ]
        part = sum(t - jnp.round(t) for t in turns)
        for layer in range(layers):
            along = momenta[:, 0:1] * (place_ref[0] + layer).astype(WIDE) / total_x
            cosine, sine = unit_phase(along - jnp.round(along) + part)
            table_ref[0, :, lanes_at(layer, tile)] = cosine
            table_ref[1, :, lanes_at(layer, tile)] = sine


    one_ref[:, :, pl.ds(0, PLANE)] = rim_ref[:, :, pl.ds(0, PLANE)]
    one_ref[:, :, pl.ds((layers - 1) * PLANE, PLANE)] = rim_ref[:, :, pl.ds(PLANE, PLANE)]
    for layer in range(1, layers - 1):

        @pl.loop(0, TILES)
        def _(tile):
            for rows in row_groups(field_ref):
                new = first_step(layer, tile, rows, field_ref, link_ref, back_ref)
                store(one_ref, rows, lanes_at(layer, tile), new)

    for layer in range(layers):

        @pl.loop(0, TILES)
        def _(tile):
            for rows in row_groups(field_ref):
                new = first_step(layer, tile, rows, one_ref, link_ref, back_ref)
                if layer in (0, layers - 1):
                    own = load(field_ref, rows, lanes_at(layer, tile))
                    new = [a + KAPPA * KAPPA * b for a, b in zip(new, own)]
                store(out_ref, rows, lanes_at(layer, tile), new)


def close_kernel(part_ref, ahead_ref, behind_ref, link_ref, back_ref, out_ref, change_ref):
    layers = part_ref.shape[2] // PLANE
    fresh, older = pl.ds(6, 6), pl.ds(0, 6)

    @pl.loop(0, TILES)
    def _(tile):
        lanes = lanes_at(0, tile)
        for rows in row_groups(part_ref):
            low = load(behind_ref.at[older], rows, lanes)
            store(change_ref, rows, lanes, [KAPPA * a for a in low])
            high = [None] * 6
            add_hop(high, link_at(link_ref, 0, layers - 1, tile), load(ahead_ref.at[older], rows, lanes), False)
            store(change_ref, rows, lanes_at(1, tile), [KAPPA * a for a in high])

    for layer in range(layers):

        @pl.loop(0, TILES)
        def _(tile):
            lanes = lanes_at(0, tile)
            for rows in row_groups(part_ref):
                new = load(part_ref, rows, lanes_at(layer, tile))
                change = lambda place, t: load(change_ref, rows, lanes_at(place, t))
                hops = [None] * 6
                if layer == 1:
                    add_hop(hops, link_at(link_ref, 0, 0, tile), change(0, tile), True)
                if layer == layers - 2:
                    add_hop(hops, link_at(link_ref, 0, layer, tile), change(1, tile), False)
                if layer == 0:
                    came = load(behind_ref.at[fresh], rows, lanes)
                    hops = came if hops[0] is None else [a + b for a, b in zip(hops, came)]
                if layer == layers - 1:
                    add_hop(hops, link_at(link_ref, 0, layer, tile), load(ahead_ref.at[fresh], rows, lanes), False)
                for place, edge in ((0, 0), (1, layers - 1)):
                    if layer == edge:
                        here = plane_hops(hops, link_ref, back_ref, layer, tile, rows, lambda t: change(place, t))
                        new = [a + (1.0 - 6.0 * KAPPA) * b for a, b in zip(new, here)]
                if hops[0] is not None:
                    new = [a + KAPPA * b for a, b in zip(new, hops)]
                store(out_ref, rows, lanes_at(layer, tile), new)


def product_kernel(columns, begin, count, scale, slot_ref, field_ref, table_ref, *refs):
    groups = len(columns)
    raw_refs, out_refs, (total_ref, left_ref, right_ref) = refs[:groups], refs[groups:-3], refs[-3:]
    vectors = field_ref.shape[1]
    depth = 6 * LANES
    step = left_ref.shape[1] // depth
    total_ref[...] = jnp.zeros_like(total_ref)

    @pl.loop(0, field_ref.shape[2] // LANES // step)
    def _(block):
        for part in range(step):
            lanes = pl.ds(pl.multiple_of((block * step + part) * LANES, LANES), LANES)
            field = [field_ref[k, :, lanes] for k in range(6)]
            one = [pl.ds(part * depth + 2 * color * LANES, LANES) for color in range(3)]
            two = [pl.ds(part * depth + (2 * color + 1) * LANES, LANES) for color in range(3)]
            for p in range(count):
                cosine = table_ref[0, pl.ds(begin + p, 1), lanes]
                sine = table_ref[1, pl.ds(begin + p, 1), lanes]
                rows = pl.ds(p * vectors, vectors)
                for color in range(3):
                    real, imag = field[2 * color], field[2 * color + 1]
                    right_ref[rows, one[color]] = (cosine * real + sine * imag).astype(LOW)
                    right_ref[rows, two[color]] = (cosine * imag - sine * real).astype(LOW)
            for g, raw_ref in enumerate(raw_refs):
                width = raw_ref.shape[1]
                first = pl.ds(2 * g * width, width)
                second = pl.ds((2 * g + 1) * width, width)
                for color in range(3):
                    real, imag = raw_ref[2 * color, :, lanes], raw_ref[2 * color + 1, :, lanes]
                    left_ref[first, one[color]] = real
                    left_ref[first, two[color]] = imag
                    left_ref[second, one[color]] = -imag
                    left_ref[second, two[color]] = real
        total_ref[...] += lax.dot_general(
            left_ref[...], right_ref[...], (((1,), (1,)), ((), ())), preferred_element_type=WIDE
        )

    width = total_ref.shape[0] // groups
    for g in range(groups):
        block = total_ref[pl.ds(g * width, width), :] * scale
        out_refs[columns[g]][slot_ref[g]] = block.astype(LOW)


def call(kernel, name, shapes, operands, flops=0, scratch=(), smem=False):
    return pl.pallas_call(
        kernel,
        out_shape=tuple(jax.ShapeDtypeStruct(shape, dtype) for shape, dtype in shapes),
        in_specs=[SMEM if smem and i == 0 else VMEM for i in range(len(operands))],
        out_specs=(VMEM,) * len(shapes),
        scratch_shapes=list(scratch),
        compiler_params=pltpu.CompilerParams(vmem_limit_bytes=VMEM_LIMIT),
        cost_estimate=pl.CostEstimate(flops=flops, bytes_accessed=BYTES, transcendentals=0),
        name=name,
    )(*operands)


def shards(vectors, gauge_links, momenta):
    bricks, vecs, subs = (lax.axis_size(axis) for axis in ("brick", "vec", "sub"))
    groups = vecs * subs
    width, sites = vectors.shape[0], vectors.shape[3]
    layers, tiles = sites // PLANE, sites // LANES
    assert groups == bricks and layers > 1 and ITERS == 2
    total_x = bricks * layers
    count = momenta.shape[0]
    brick, vec, sub = (lax.axis_index(axis) for axis in ("brick", "vec", "sub"))
    tiled_vectors = jnp.swapaxes(vectors.reshape((width, 3, 2, tiles, LANES)), 2, 3).reshape((-1, LANES))
    links = jnp.swapaxes(gauge_links.reshape((27, 2, tiles, LANES)), 1, 2).reshape((-1, LANES))
    full, faces = (6, width, sites), (12, width, PLANE)
    field, raw, down, up, rim, back = call(
        open_kernel,
        "open",
        ((full, WIDE), (full, LOW), (faces, LOW), (faces, LOW), ((6, width, 2 * PLANE), WIDE), ((2, 16, sites), WIDE)),
        (tiled_vectors, links),
        flops=1 << 24,
    )
    ahead, behind = shifted(down, "brick", -1), shifted(up, "brick", 1)
    across = [shifted(raw, "vec", a) for a in range(1, vecs)]
    beside = [shifted(raw, "sub", b) for b in range(1, subs)]
    place = (brick * layers).astype(jnp.int32).reshape((1,))
    part, table = call(
        functools.partial(local_kernel, total_x),
        "local",
        ((full, WIDE), ((2, count, sites), WIDE)),
        (place, field, links, back, rim, momenta),
        flops=1 << 25,
        scratch=(pltpu.VMEM(full, WIDE),),
        smem=True,
    )
    *across, ahead, behind, part = lax.optimization_barrier((*across, ahead, behind, part))
    raws = [raw, *across, *beside]
    raws += [shifted(array, "sub", b) for b in range(1, subs) for array in across]
    offsets = [(a, 0) for a in range(vecs)] + [(0, b) for b in range(1, subs)]
    offsets += [(a, b) for b in range(1, subs) for a in range(1, vecs)]
    (smeared,) = call(
        close_kernel,
        "close",
        ((full, WIDE),),
        (part, ahead, behind, links, back),
        flops=1 << 24,
        scratch=(pltpu.VMEM((6, width, 2 * PLANE), WIDE),),
    )
    brick_vec, brick_sub = brick // subs, brick % subs
    slots = jnp.stack([(sub - b - brick_sub) % subs for a, b in offsets]).astype(jnp.int32)
    scale = (3.0 * total_x * PLANE) ** (-0.5)
    depth = STEP * 6 * LANES
    columns = count * width
    blocks = call(
        functools.partial(product_kernel, [-a % vecs for a, b in offsets], 0, count, scale),
        "product",
        (((subs, 2 * width, columns), LOW),) * vecs,
        (slots, smeared, table, *raws),
        flops=1 << 32,
        scratch=(
            pltpu.VMEM((groups * 2 * width, columns), WIDE),
            pltpu.VMEM((groups * 2 * width, depth), LOW),
            pltpu.VMEM((columns, depth), LOW),
        ),
        smem=True,
    )
    held = [shifted(block, "vec", a) if a else block for a, block in enumerate(blocks)]
    shares = []
    for q in range(vecs):
        place = (vec - brick_vec - q) % vecs
        block = held[0]
        for a in range(1, vecs):
            block = jnp.where(place == a, held[a], block)
        for r in range(subs):
            pairs = [
                (b * subs + s, ((b // subs + q) % vecs * subs + s) * subs + (b % subs + r) % subs)
                for b in range(bricks)
                for s in range(subs)
            ]
            shares.append(lax.ppermute(block[r], ("brick", "sub"), pairs))
    total = functools.reduce(jnp.add, [share.astype(WIDE) for share in shares])
    return jnp.transpose(total.reshape((2, width, count, width)), (1, 2, 0, 3))


def solution(mesh):
    in_specs = (
        P(("vec", "sub"), None, None, ("grp", "brick")),
        P(None, None, None, None, ("grp", "brick")),
        P(),
    )
    out_specs = P(("vec", "sub"), "grp", None, "brick")
    return jax.shard_map(shards, mesh=mesh, in_specs=in_specs, out_specs=out_specs, check_vma=False)
```

```python
import functools
import math

import jax
import jax.numpy as jnp
from jax import lax
from jax.experimental import pallas as pl
from jax.experimental.pallas import tpu as pltpu
from jax.sharding import PartitionSpec as P

LY = 64
LZ = 8
ITERS = 2
KAPPA = 0.125
LANES = 128
PLANE = LY * LZ
TILES = PLANE // LANES
ROWS = 16
BYTES = 1 << 20
LOW = jnp.bfloat16
WIDE = jnp.float32
STEP = 2
VMEM_LIMIT = 40 * 1024 * 1024
VMEM = pl.BlockSpec(memory_space=pltpu.VMEM)
SMEM = pl.BlockSpec(memory_space=pltpu.SMEM)


def shifted(array, axis, by):
    peers = lax.axis_size(axis)
    return lax.ppermute(array, axis, [(i, (i + by) % peers) for i in range(peers)])


def add_hop(total, link, field, adjoint):
    for row in range(3):
        for column in range(3):
            if adjoint:
                real, imag = link(column, row, 0), link(column, row, 1)
            else:
                real, imag = link(row, column, 0), link(row, column, 1)
            source_real, source_imag = field[2 * column], field[2 * column + 1]
            if adjoint:
                add_real = real * source_real + imag * source_imag
                add_imag = real * source_imag - imag * source_real
            else:
                add_real = real * source_real - imag * source_imag
                add_imag = real * source_imag + imag * source_real
            for part, add in ((0, add_real), (1, add_imag)):
                old = total[2 * row + part]
                total[2 * row + part] = add if old is None else old + add


def lane_roll(value, by):
    return pltpu.roll(value, by % LANES, 1)


def lanes_at(layer, tile):
    return pl.ds(pl.multiple_of(layer * PLANE + tile * LANES, LANES), LANES)


def row_groups(ref):
    size = min(ROWS, ref.shape[1])
    return [pl.ds(start, size) for start in range(0, ref.shape[1], size)]


def load(ref, rows, lanes):
    return [ref[k, rows, lanes].astype(WIDE) for k in range(6)]


def store(ref, rows, lanes, values):
    for k in range(6):
        ref[k, rows, lanes] = values[k].astype(ref.dtype)


def link_at(link_ref, direction, layer, tile):
    tiles = link_ref.shape[0] // 54

    def get(row, column, part):
        matrix = (direction * 3 + row) * 3 + column
        return link_ref[pl.ds((matrix * tiles + layer * TILES + tile) * 2 + part, 1), :]

    return get


def plane_hops(total, link_ref, back_ref, layer, tile, rows, fetch):
    here = fetch(tile)
    after, before = fetch((tile + 1) % TILES), fetch((tile + TILES - 1) % TILES)
    lane = lax.broadcasted_iota(jnp.int32, (rows.size, LANES), 1)
    ahead = [jnp.where(lane >= LANES - LZ, lane_roll(b, -LZ), lane_roll(a, -LZ)) for a, b in zip(here, after)]
    add_hop(total, link_at(link_ref, 1, layer, tile), ahead, False)
    behind = [jnp.where(lane < LZ, lane_roll(b, LZ), lane_roll(a, LZ)) for a, b in zip(here, before)]
    lanes = lanes_at(layer, tile)
    add_hop(total, lambda r, c, part: back_ref[part, pl.ds(3 * r + c, 1), lanes], behind, True)
    depth = lane % LZ
    ahead = [jnp.where(depth == LZ - 1, lane_roll(a, LZ - 1), lane_roll(a, -1)) for a in here]
    add_hop(total, link_at(link_ref, 2, layer, tile), ahead, False)
    turned = [None] * 6
    add_hop(turned, link_at(link_ref, 2, layer, tile), here, True)
    for k in range(6):
        total[k] += jnp.where(depth == 0, lane_roll(turned[k], 1 - LZ), lane_roll(turned[k], 1))
    return here


def combined(here, total):
    return [(1.0 - 6.0 * KAPPA) * a + KAPPA * b for a, b in zip(here, total)]


def first_step(layer, tile, rows, field_ref, link_ref, back_ref):
    layers = field_ref.shape[2] // PLANE
    total = [None] * 6
    if layer < layers - 1:
        source = load(field_ref, rows, lanes_at(layer + 1, tile))
        add_hop(total, link_at(link_ref, 0, layer, tile), source, False)
    if layer > 0:
        source = load(field_ref, rows, lanes_at(layer - 1, tile))
        add_hop(total, link_at(link_ref, 0, layer - 1, tile), source, True)
    fetch = lambda t: load(field_ref, rows, lanes_at(layer, t))
    return combined(plane_hops(total, link_ref, back_ref, layer, tile, rows, fetch), total)


def open_kernel(vector_ref, link_ref, field_ref, raw_ref, down_ref, up_ref):
    vectors, sites = field_ref.shape[1:]
    tiles, layers = sites // LANES, sites // PLANE
    stride = 6 * tiles
    for k in range(6):
        for tile in range(tiles):
            row = ((k // 2) * tiles + tile) * 2 + k % 2
            value = vector_ref[pl.ds(row, vectors, stride=stride), :]
            field_ref[k, :, pl.ds(tile * LANES, LANES)] = value
            low = value.astype(LOW)
            raw_ref[k, :, pl.ds(tile * LANES, LANES)] = low
            if tile < TILES:
                down_ref[k, :, pl.ds(tile * LANES, LANES)] = low

    @pl.loop(0, TILES)
    def _(tile):
        for rows in row_groups(field_ref):
            turned = [None] * 6
            source = load(field_ref, rows, lanes_at(layers - 1, tile))
            add_hop(turned, link_at(link_ref, 0, layers - 1, tile), source, True)
            store(up_ref, rows, lanes_at(0, tile), turned)


def rim_kernel(field_ref, link_ref, down_ref, up_ref, rim_ref, back_ref):
    sites = field_ref.shape[2]
    tiles, layers = sites // LANES, sites // PLANE
    lane = lax.broadcasted_iota(jnp.int32, (9, LANES), 1)
    for layer in range(layers):
        for part in range(2):
            row = lambda tile: (9 * tiles + layer * TILES + tile) * 2 + part
            value = [link_ref[pl.ds(row(tile), 9, stride=2 * tiles), :] for tile in range(TILES)]
            value = [lane_roll(v, LZ) for v in value]
            for tile in range(TILES):
                back_ref[part, pl.ds(0, 9), lanes_at(layer, tile)] = jnp.where(lane < LZ, value[tile - 1], value[tile])

    for place, layer in enumerate((0, layers - 1)):

        @pl.loop(0, TILES)
        def _(tile):
            lanes = lanes_at(0, tile)
            for rows in row_groups(field_ref):
                new = first_step(layer, tile, rows, field_ref, link_ref, back_ref)
                store(rim_ref, rows, lanes_at(place, tile), new)
                if place == 0:
                    store(down_ref, rows, lanes, new)
                else:
                    turned = [None] * 6
                    add_hop(turned, link_at(link_ref, 0, layer, tile), new, True)
                    store(up_ref, rows, lanes, turned)


def unit_phase(turns):
    half = math.pi * (turns - jnp.round(turns))
    square = half * half
    cosine, sine = 1.0, 1.0
    for order in range(12, 0, -2):
        sine = 1.0 - square * sine * (1.0 / (order * (order + 1)))
        cosine = 1.0 - square * cosine * (1.0 / (order * (order - 1)))
    sine = half * sine
    return 1.0 - 2.0 * sine * sine, 2.0 * sine * cosine


def local_kernel(
    total_x, place_ref, field_ref, link_ref, back_ref, rim_ref, momenta_ref, out_ref, table_ref, one_ref
):
    layers = field_ref.shape[2] // PLANE
    count = momenta_ref.shape[0]
    momenta = momenta_ref[...].astype(WIDE)
    lane = lax.broadcasted_iota(jnp.int32, (count, LANES), 1)

    @pl.loop(0, TILES)
    def _(tile):
        column = (tile * (LANES // LZ) + lane // LZ).astype(WIDE)
        depth = (lane % LZ).astype(WIDE)
        turns = [momenta[:, 1:2] * column / LY, momenta[:, 2:3] * depth / LZ]
        part = sum(t - jnp.round(t) for t in turns)
        for layer in range(layers):
            along = momenta[:, 0:1] * (place_ref[0] + layer).astype(WIDE) / total_x
            cosine, sine = unit_phase(along - jnp.round(along) + part)
            table_ref[0, :, lanes_at(layer, tile)] = cosine
            table_ref[1, :, lanes_at(layer, tile)] = sine


    one_ref[:, :, pl.ds(0, PLANE)] = rim_ref[:, :, pl.ds(0, PLANE)]
    one_ref[:, :, pl.ds((layers - 1) * PLANE, PLANE)] = rim_ref[:, :, pl.ds(PLANE, PLANE)]
    for layer in range(1, layers - 1):

        @pl.loop(0, TILES)
        def _(tile):
            for rows in row_groups(field_ref):
                new = first_step(layer, tile, rows, field_ref, link_ref, back_ref)
                store(one_ref, rows, lanes_at(layer, tile), new)

    for layer in range(layers):

        @pl.loop(0, TILES)
        def _(tile):
            for rows in row_groups(field_ref):
                new = first_step(layer, tile, rows, one_ref, link_ref, back_ref)
                if layer in (0, layers - 1):
                    own = load(field_ref, rows, lanes_at(layer, tile))
                    new = [a + KAPPA * KAPPA * b for a, b in zip(new, own)]
                store(out_ref, rows, lanes_at(layer, tile), new)


def close_kernel(part_ref, ahead_ref, behind_ref, link_ref, back_ref, out_ref, token_ref, change_ref):
    layers = part_ref.shape[2] // PLANE
    token_ref[...] = jnp.zeros_like(token_ref)

    @pl.loop(0, TILES)
    def _(tile):
        lanes = lanes_at(0, tile)
        for rows in row_groups(part_ref):
            store(change_ref, rows, lanes, [KAPPA * a for a in load(behind_ref, rows, lanes)])
            high = [None] * 6
            add_hop(high, link_at(link_ref, 0, layers - 1, tile), load(ahead_ref, rows, lanes), False)
            store(change_ref, rows, lanes_at(1, tile), [KAPPA * a for a in high])

    for layer in range(layers):

        @pl.loop(0, TILES)
        def _(tile):
            for rows in row_groups(part_ref):
                new = load(part_ref, rows, lanes_at(layer, tile))
                change = lambda place, t: load(change_ref, rows, lanes_at(place, t))
                hops = [None] * 6
                if layer == 1:
                    add_hop(hops, link_at(link_ref, 0, 0, tile), change(0, tile), True)
                if layer == layers - 2:
                    add_hop(hops, link_at(link_ref, 0, layer, tile), change(1, tile), False)
                for place, edge in ((0, 0), (1, layers - 1)):
                    if layer == edge:
                        if hops[0] is None:
                            hops = [jnp.zeros_like(a) for a in new]
                        here = plane_hops(hops, link_ref, back_ref, layer, tile, rows, lambda t: change(place, t))
                        new = [a + (1.0 - 6.0 * KAPPA) * b for a, b in zip(new, here)]
                if hops[0] is not None:
                    new = [a + KAPPA * b for a, b in zip(new, hops)]
                store(out_ref, rows, lanes_at(layer, tile), new)


def face_kernel(most_ref, ahead_ref, behind_ref, link_ref, token_ref, out_ref):
    layers = most_ref.shape[2] // PLANE

    @pl.loop(0, TILES)
    def _(tile):
        lanes, high = lanes_at(0, tile), lanes_at(1, tile)
        for rows in row_groups(most_ref):
            new = zip(load(most_ref, rows, lanes), load(behind_ref, rows, lanes))
            store(out_ref, rows, lanes, [a + KAPPA * b for a, b in new])
            hop = [None] * 6
            add_hop(hop, link_at(link_ref, 0, layers - 1, tile), load(ahead_ref, rows, lanes), False)
            new = zip(load(most_ref, rows, lanes_at(layers - 1, tile)), hop)
            store(out_ref, rows, high, [a + KAPPA * b for a, b in new])


def product_kernel(columns, count, scale, slot_ref, most_ref, face_ref, table_ref, *refs):
    groups = len(columns)
    raw_refs, out_refs, (total_ref, left_ref, right_ref) = refs[:groups], refs[groups:-3], refs[-3:]
    vectors = most_ref.shape[1]
    layers = most_ref.shape[2] // PLANE
    depth = 6 * LANES
    step = left_ref.shape[1] // depth
    total_ref[...] = jnp.zeros_like(total_ref)

    def add(field_ref, place):
        for part in range(step):
            own, lanes = place(part)
            field = [field_ref[k, :, own] for k in range(6)]
            one = [pl.ds(part * depth + 2 * color * LANES, LANES) for color in range(3)]
            two = [pl.ds(part * depth + (2 * color + 1) * LANES, LANES) for color in range(3)]
            for p in range(count):
                cosine = table_ref[0, pl.ds(p, 1), lanes]
                sine = table_ref[1, pl.ds(p, 1), lanes]
                rows = pl.ds(p * vectors, vectors)
                for color in range(3):
                    real, imag = field[2 * color], field[2 * color + 1]
                    right_ref[rows, one[color]] = (cosine * real + sine * imag).astype(LOW)
                    right_ref[rows, two[color]] = (cosine * imag - sine * real).astype(LOW)
            for g, raw_ref in enumerate(raw_refs):
                width = raw_ref.shape[1]
                first = pl.ds(2 * g * width, width)
                second = pl.ds((2 * g + 1) * width, width)
                for color in range(3):
                    real, imag = raw_ref[2 * color, :, lanes], raw_ref[2 * color + 1, :, lanes]
                    left_ref[first, one[color]] = real
                    left_ref[first, two[color]] = imag
                    left_ref[second, one[color]] = -imag
                    left_ref[second, two[color]] = real
        total_ref[...] += lax.dot_general(
            left_ref[...], right_ref[...], (((1,), (1,)), ((), ())), preferred_element_type=WIDE
        )

    blocks = TILES // step

    @pl.loop(0, (layers - 2) * blocks)
    def _(block):
        add(most_ref, lambda part: (lanes_at(1, block * step + part),) * 2)

    @pl.loop(0, 2 * blocks)
    def _(block):
        layer = block // blocks * (layers - 1)
        tile = block % blocks * step
        add(face_ref, lambda part: (lanes_at(0, block * step + part), lanes_at(layer, tile + part)))

    width = total_ref.shape[0] // groups
    for g in range(groups):
        block = total_ref[pl.ds(g * width, width), :] * scale
        out_refs[columns[g]][slot_ref[g]] = block.astype(LOW)


def call(kernel, name, shapes, operands, flops=0, scratch=(), smem=False):
    return pl.pallas_call(
        kernel,
        out_shape=tuple(jax.ShapeDtypeStruct(shape, dtype) for shape, dtype in shapes),
        in_specs=[SMEM if smem and i == 0 else VMEM for i in range(len(operands))],
        out_specs=(VMEM,) * len(shapes),
        scratch_shapes=list(scratch),
        compiler_params=pltpu.CompilerParams(vmem_limit_bytes=VMEM_LIMIT),
        cost_estimate=pl.CostEstimate(flops=flops, bytes_accessed=BYTES, transcendentals=0),
        name=name,
    )(*operands)


def shards(vectors, gauge_links, momenta):
    bricks, vecs, subs = (lax.axis_size(axis) for axis in ("brick", "vec", "sub"))
    groups = vecs * subs
    width, sites = vectors.shape[0], vectors.shape[3]
    layers, tiles = sites // PLANE, sites // LANES
    assert groups == bricks and layers > 1 and ITERS == 2
    total_x = bricks * layers
    count = momenta.shape[0]
    brick, vec, sub = (lax.axis_index(axis) for axis in ("brick", "vec", "sub"))
    tiled_vectors = jnp.swapaxes(vectors.reshape((width, 3, 2, tiles, LANES)), 2, 3).reshape((-1, LANES))
    links = jnp.swapaxes(gauge_links.reshape((27, 2, tiles, LANES)), 1, 2).reshape((-1, LANES))
    full, face = (6, width, sites), (6, width, PLANE)
    field, raw, down, up = call(
        open_kernel,
        "open",
        ((full, WIDE), (full, LOW), (face, LOW), (face, LOW)),
        (tiled_vectors, links),
        flops=1 << 22,
    )
    ahead, behind = shifted(down, "brick", -1), shifted(up, "brick", 1)
    across = [shifted(raw, "vec", a) for a in range(1, vecs)]
    down_two, up_two, rim, back = call(
        rim_kernel,
        "rim",
        ((face, LOW), (face, LOW), ((6, width, 2 * PLANE), WIDE), ((2, 16, sites), WIDE)),
        (field, links),
        flops=1 << 24,
    )
    ahead_two, behind_two = shifted(down_two, "brick", -1), shifted(up_two, "brick", 1)
    place = (brick * layers).astype(jnp.int32).reshape((1,))
    part, table = call(
        functools.partial(local_kernel, total_x),
        "local",
        ((full, WIDE), ((2, count, sites), WIDE)),
        (place, field, links, back, rim, momenta),
        flops=1 << 25,
        scratch=(pltpu.VMEM(full, WIDE),),
        smem=True,
    )
    most, token = call(
        close_kernel,
        "close",
        ((full, WIDE), ((8, LANES), WIDE)),
        (part, ahead, behind, links, back),
        flops=1 << 24,
        scratch=(pltpu.VMEM((6, width, 2 * PLANE), WIDE),),
    )
    late, token = lax.optimization_barrier((raw, token))
    *across, ahead_two, behind_two, token = lax.optimization_barrier((*across, ahead_two, behind_two, token))
    raws = [raw, *across] + [shifted(array, "sub", b) for b in range(1, subs) for array in (late, *across)]
    offsets = [(a, b) for b in range(subs) for a in range(vecs)]
    (faces,) = call(
        face_kernel,
        "face",
        (((6, width, 2 * PLANE), WIDE),),
        (most, ahead_two, behind_two, links, token),
        flops=1 << 22,
    )
    brick_vec, brick_sub = brick // subs, brick % subs
    slots = jnp.stack([(sub - b - brick_sub) % subs for a, b in offsets]).astype(jnp.int32)
    scale = (3.0 * total_x * PLANE) ** (-0.5)
    depth = STEP * 6 * LANES
    columns = count * width
    blocks = call(
        functools.partial(product_kernel, [-a % vecs for a, b in offsets], count, scale),
        "product",
        (((subs, 2 * width, columns), LOW),) * vecs,
        (slots, most, faces, table, *raws),
        flops=1 << 32,
        scratch=(
            pltpu.VMEM((groups * 2 * width, columns), WIDE),
            pltpu.VMEM((groups * 2 * width, depth), LOW),
            pltpu.VMEM((columns, depth), LOW),
        ),
        smem=True,
    )
    held = [shifted(block, "vec", a) if a else block for a, block in enumerate(blocks)]
    shares = []
    for q in range(vecs):
        place = (vec - brick_vec - q) % vecs
        block = held[0]
        for a in range(1, vecs):
            block = jnp.where(place == a, held[a], block)
        for r in range(subs):
            pairs = [
                (b * subs + s, ((b // subs + q) % vecs * subs + s) * subs + (b % subs + r) % subs)
                for b in range(bricks)
                for s in range(subs)
            ]
            shares.append(lax.ppermute(block[r], ("brick", "sub"), pairs))
    total = functools.reduce(jnp.add, [share.astype(WIDE) for share in shares])
    return jnp.transpose(total.reshape((2, width, count, width)), (1, 2, 0, 3))


def solution(mesh):
    in_specs = (
        P(("vec", "sub"), None, None, ("grp", "brick")),
        P(None, None, None, None, ("grp", "brick")),
        P(),
    )
    out_specs = P(("vec", "sub"), "grp", None, "brick")
    return jax.shard_map(shards, mesh=mesh, in_specs=in_specs, out_specs=out_specs, check_vma=False)
```

```python
import functools
import math

import jax
import jax.numpy as jnp
from jax import lax
from jax.experimental import pallas as pl
from jax.experimental.pallas import tpu as pltpu
from jax.sharding import PartitionSpec as P

LY = 64
LZ = 8
ITERS = 2
KAPPA = 0.125
LANES = 128
PLANE = LY * LZ
TILES = PLANE // LANES
ROWS = 16
BYTES = 1 << 20
LOW = jnp.bfloat16
WIDE = jnp.float32
STEP = 2
VMEM_LIMIT = 40 * 1024 * 1024
VMEM = pl.BlockSpec(memory_space=pltpu.VMEM)
AWAY = pl.BlockSpec(memory_space=pl.ANY)
SMEM = pl.BlockSpec(memory_space=pltpu.SMEM)


def shifted(array, axis, by):
    peers = lax.axis_size(axis)
    return lax.ppermute(array, axis, [(i, (i + by) % peers) for i in range(peers)])


def add_hop(total, link, field, adjoint):
    for row in range(3):
        for column in range(3):
            if adjoint:
                real, imag = link(column, row, 0), link(column, row, 1)
            else:
                real, imag = link(row, column, 0), link(row, column, 1)
            source_real, source_imag = field[2 * column], field[2 * column + 1]
            if adjoint:
                add_real = real * source_real + imag * source_imag
                add_imag = real * source_imag - imag * source_real
            else:
                add_real = real * source_real - imag * source_imag
                add_imag = real * source_imag + imag * source_real
            for part, add in ((0, add_real), (1, add_imag)):
                old = total[2 * row + part]
                total[2 * row + part] = add if old is None else old + add


def lane_roll(value, by):
    return pltpu.roll(value, by % LANES, 1)


def lanes_at(layer, tile):
    return pl.ds(pl.multiple_of(layer * PLANE + tile * LANES, LANES), LANES)


def row_groups(ref):
    size = min(ROWS, ref.shape[1])
    return [pl.ds(start, size) for start in range(0, ref.shape[1], size)]


def load(ref, rows, lanes):
    return [ref[k, rows, lanes].astype(WIDE) for k in range(6)]


def store(ref, rows, lanes, values):
    for k in range(6):
        ref[k, rows, lanes] = values[k].astype(ref.dtype)


def link_at(link_ref, direction, layer, tile):
    tiles = link_ref.shape[0] // 54

    def get(row, column, part):
        matrix = (direction * 3 + row) * 3 + column
        return link_ref[pl.ds((matrix * tiles + layer * TILES + tile) * 2 + part, 1), :]

    return get


def plane_hops(total, link_ref, back_ref, layer, tile, rows, fetch):
    here = fetch(tile)
    after, before = fetch((tile + 1) % TILES), fetch((tile + TILES - 1) % TILES)
    lane = lax.broadcasted_iota(jnp.int32, (rows.size, LANES), 1)
    ahead = [jnp.where(lane >= LANES - LZ, lane_roll(b, -LZ), lane_roll(a, -LZ)) for a, b in zip(here, after)]
    add_hop(total, link_at(link_ref, 1, layer, tile), ahead, False)
    behind = [jnp.where(lane < LZ, lane_roll(b, LZ), lane_roll(a, LZ)) for a, b in zip(here, before)]
    lanes = lanes_at(layer, tile)
    add_hop(total, lambda r, c, part: back_ref[part, pl.ds(3 * r + c, 1), lanes], behind, True)
    depth = lane % LZ
    ahead = [jnp.where(depth == LZ - 1, lane_roll(a, LZ - 1), lane_roll(a, -1)) for a in here]
    add_hop(total, link_at(link_ref, 2, layer, tile), ahead, False)
    turned = [None] * 6
    add_hop(turned, link_at(link_ref, 2, layer, tile), here, True)
    for k in range(6):
        total[k] += jnp.where(depth == 0, lane_roll(turned[k], 1 - LZ), lane_roll(turned[k], 1))
    return here


def combined(here, total):
    return [(1.0 - 6.0 * KAPPA) * a + KAPPA * b for a, b in zip(here, total)]


def first_step(layer, tile, rows, field_ref, link_ref, back_ref):
    layers = field_ref.shape[2] // PLANE
    total = [None] * 6
    if layer < layers - 1:
        source = load(field_ref, rows, lanes_at(layer + 1, tile))
        add_hop(total, link_at(link_ref, 0, layer, tile), source, False)
    if layer > 0:
        source = load(field_ref, rows, lanes_at(layer - 1, tile))
        add_hop(total, link_at(link_ref, 0, layer - 1, tile), source, True)
    fetch = lambda t: load(field_ref, rows, lanes_at(layer, t))
    return combined(plane_hops(total, link_ref, back_ref, layer, tile, rows, fetch), total)


def open_kernel(vector_ref, edge_ref, field_ref, raw_ref, down_ref, up_ref):
    vectors, sites = field_ref.shape[1:]
    tiles, layers = sites // LANES, sites // PLANE
    stride = 6 * tiles
    for k in range(6):
        for tile in range(tiles):
            row = ((k // 2) * tiles + tile) * 2 + k % 2
            value = vector_ref[pl.ds(row, vectors, stride=stride), :]
            field_ref[k, :, pl.ds(tile * LANES, LANES)] = value
            low = value.astype(LOW)
            raw_ref[k, :, pl.ds(tile * LANES, LANES)] = low
            if tile < TILES:
                down_ref[k, :, pl.ds(tile * LANES, LANES)] = low

    @pl.loop(0, TILES)
    def _(tile):
        for rows in row_groups(field_ref):
            turned = [None] * 6
            source = load(field_ref, rows, lanes_at(layers - 1, tile))
            link = lambda row, column, part: edge_ref[pl.ds(((3 * row + column) * TILES + tile) * 2 + part, 1), :]
            add_hop(turned, link, source, True)
            store(up_ref, rows, lanes_at(0, tile), turned)


def rim_kernel(field_ref, link_ref, down_ref, up_ref, rim_ref, back_ref):
    sites = field_ref.shape[2]
    tiles, layers = sites // LANES, sites // PLANE
    lane = lax.broadcasted_iota(jnp.int32, (9, LANES), 1)
    for layer in range(layers):
        for part in range(2):
            row = lambda tile: (9 * tiles + layer * TILES + tile) * 2 + part
            value = [link_ref[pl.ds(row(tile), 9, stride=2 * tiles), :] for tile in range(TILES)]
            value = [lane_roll(v, LZ) for v in value]
            for tile in range(TILES):
                back_ref[part, pl.ds(0, 9), lanes_at(layer, tile)] = jnp.where(lane < LZ, value[tile - 1], value[tile])

    for place, layer in enumerate((0, layers - 1)):

        @pl.loop(0, TILES)
        def _(tile):
            lanes = lanes_at(0, tile)
            for rows in row_groups(field_ref):
                new = first_step(layer, tile, rows, field_ref, link_ref, back_ref)
                store(rim_ref, rows, lanes_at(place, tile), new)
                if place == 0:
                    store(down_ref, rows, lanes, new)
                else:
                    turned = [None] * 6
                    add_hop(turned, link_at(link_ref, 0, layer, tile), new, True)
                    store(up_ref, rows, lanes, turned)


def unit_phase(turns):
    half = math.pi * (turns - jnp.round(turns))
    square = half * half
    cosine, sine = 1.0, 1.0
    for order in range(12, 0, -2):
        sine = 1.0 - square * sine * (1.0 / (order * (order + 1)))
        cosine = 1.0 - square * cosine * (1.0 / (order * (order - 1)))
    sine = half * sine
    return 1.0 - 2.0 * sine * sine, 2.0 * sine * cosine


def local_kernel(
    total_x, place_ref, field_ref, link_ref, back_ref, rim_ref, momenta_ref, *refs
):
    out_ref, table_ref, one_ref = refs[-3:]
    layers = field_ref.shape[2] // PLANE
    count = momenta_ref.shape[0]
    momenta = momenta_ref[...].astype(WIDE)
    lane = lax.broadcasted_iota(jnp.int32, (count, LANES), 1)

    @pl.loop(0, TILES)
    def _(tile):
        column = (tile * (LANES // LZ) + lane // LZ).astype(WIDE)
        depth = (lane % LZ).astype(WIDE)
        turns = [momenta[:, 1:2] * column / LY, momenta[:, 2:3] * depth / LZ]
        part = sum(t - jnp.round(t) for t in turns)
        for layer in range(layers):
            along = momenta[:, 0:1] * (place_ref[0] + layer).astype(WIDE) / total_x
            cosine, sine = unit_phase(along - jnp.round(along) + part)
            table_ref[0, :, lanes_at(layer, tile)] = cosine
            table_ref[1, :, lanes_at(layer, tile)] = sine


    one_ref[:, :, pl.ds(0, PLANE)] = rim_ref[:, :, pl.ds(0, PLANE)]
    one_ref[:, :, pl.ds((layers - 1) * PLANE, PLANE)] = rim_ref[:, :, pl.ds(PLANE, PLANE)]
    for layer in range(1, layers - 1):

        @pl.loop(0, TILES)
        def _(tile):
            for rows in row_groups(field_ref):
                new = first_step(layer, tile, rows, field_ref, link_ref, back_ref)
                store(one_ref, rows, lanes_at(layer, tile), new)

    for layer in range(layers):

        @pl.loop(0, TILES)
        def _(tile):
            for rows in row_groups(field_ref):
                new = first_step(layer, tile, rows, one_ref, link_ref, back_ref)
                if layer in (0, layers - 1):
                    own = load(field_ref, rows, lanes_at(layer, tile))
                    new = [a + KAPPA * KAPPA * b for a, b in zip(new, own)]
                store(out_ref, rows, lanes_at(layer, tile), new)


def close_kernel(part_ref, ahead_ref, behind_ref, link_ref, back_ref, out_ref, token_ref, change_ref):
    layers = part_ref.shape[2] // PLANE
    token_ref[...] = jnp.zeros_like(token_ref)

    @pl.loop(0, TILES)
    def _(tile):
        lanes = lanes_at(0, tile)
        for rows in row_groups(part_ref):
            store(change_ref, rows, lanes, [KAPPA * a for a in load(behind_ref, rows, lanes)])
            high = [None] * 6
            add_hop(high, link_at(link_ref, 0, layers - 1, tile), load(ahead_ref, rows, lanes), False)
            store(change_ref, rows, lanes_at(1, tile), [KAPPA * a for a in high])

    for layer in range(layers):

        @pl.loop(0, TILES)
        def _(tile):
            for rows in row_groups(part_ref):
                new = load(part_ref, rows, lanes_at(layer, tile))
                change = lambda place, t: load(change_ref, rows, lanes_at(place, t))
                hops = [None] * 6
                if layer == 1:
                    add_hop(hops, link_at(link_ref, 0, 0, tile), change(0, tile), True)
                if layer == layers - 2:
                    add_hop(hops, link_at(link_ref, 0, layer, tile), change(1, tile), False)
                for place, edge in ((0, 0), (1, layers - 1)):
                    if layer == edge:
                        if hops[0] is None:
                            hops = [jnp.zeros_like(a) for a in new]
                        here = plane_hops(hops, link_ref, back_ref, layer, tile, rows, lambda t: change(place, t))
                        new = [a + (1.0 - 6.0 * KAPPA) * b for a, b in zip(new, here)]
                if hops[0] is not None:
                    new = [a + KAPPA * b for a, b in zip(new, hops)]
                store(out_ref, rows, lanes_at(layer, tile), new)


def face_kernel(most_ref, ahead_ref, behind_ref, link_ref, token_ref, out_ref):
    layers = most_ref.shape[2] // PLANE

    @pl.loop(0, TILES)
    def _(tile):
        lanes, high = lanes_at(0, tile), lanes_at(1, tile)
        for rows in row_groups(most_ref):
            new = zip(load(most_ref, rows, lanes), load(behind_ref, rows, lanes))
            store(out_ref, rows, lanes, [a + KAPPA * b for a, b in new])
            hop = [None] * 6
            add_hop(hop, link_at(link_ref, 0, layers - 1, tile), load(ahead_ref, rows, lanes), False)
            new = zip(load(most_ref, rows, lanes_at(layers - 1, tile)), hop)
            store(out_ref, rows, high, [a + KAPPA * b for a, b in new])


def product_kernel(columns, count, scale, slot_ref, most_ref, face_ref, table_ref, *refs):
    groups = len(columns)
    away_refs, out_refs, (total_ref, left_ref, right_ref, held_ref, copied) = refs[:groups], refs[groups:-5], refs[-5:]
    raw_refs = [held_ref.at[g] for g in range(groups)]
    vectors = most_ref.shape[1]
    layers = most_ref.shape[2] // PLANE
    depth = 6 * LANES
    step = left_ref.shape[1] // depth

    def copies(layer):
        here = pl.ds(pl.multiple_of(layer * PLANE, PLANE), PLANE)
        return [
            pltpu.make_async_copy(away_refs[g].at[:, :, here], held_ref.at[g, :, :, here], copied.at[g, layer])
            for g in range(groups)
        ]

    for layer in (*range(1, layers - 1), 0, layers - 1):
        for copy in copies(layer):
            copy.start()
    total_ref[...] = jnp.zeros_like(total_ref)

    def ready(layer, block):
        @pl.when(block % blocks == 0)
        def _():
            for copy in copies(layer):
                copy.wait()

    def add(field_ref, place):
        for part in range(step):
            own, lanes = place(part)
            field = [field_ref[k, :, own] for k in range(6)]
            one = [pl.ds(part * depth + 2 * color * LANES, LANES) for color in range(3)]
            two = [pl.ds(part * depth + (2 * color + 1) * LANES, LANES) for color in range(3)]
            for p in range(count):
                cosine = table_ref[0, pl.ds(p, 1), lanes]
                sine = table_ref[1, pl.ds(p, 1), lanes]
                rows = pl.ds(p * vectors, vectors)
                for color in range(3):
                    real, imag = field[2 * color], field[2 * color + 1]
                    right_ref[rows, one[color]] = (cosine * real + sine * imag).astype(LOW)
                    right_ref[rows, two[color]] = (cosine * imag - sine * real).astype(LOW)
            for g, raw_ref in enumerate(raw_refs):
                width = raw_ref.shape[1]
                first = pl.ds(2 * g * width, width)
                second = pl.ds((2 * g + 1) * width, width)
                for color in range(3):
                    real, imag = raw_ref[2 * color, :, lanes], raw_ref[2 * color + 1, :, lanes]
                    left_ref[first, one[color]] = real
                    left_ref[first, two[color]] = imag
                    left_ref[second, one[color]] = -imag
                    left_ref[second, two[color]] = real
        total_ref[...] += lax.dot_general(
            left_ref[...], right_ref[...], (((1,), (1,)), ((), ())), preferred_element_type=WIDE
        )

    blocks = TILES // step

    @pl.loop(0, (layers - 2) * blocks)
    def _(block):
        ready(1 + block // blocks, block)
        add(most_ref, lambda part: (lanes_at(1, block * step + part),) * 2)

    @pl.loop(0, 2 * blocks)
    def _(block):
        layer = block // blocks * (layers - 1)
        tile = block % blocks * step
        ready(layer, block)
        add(face_ref, lambda part: (lanes_at(0, block * step + part), lanes_at(layer, tile + part)))

    width = total_ref.shape[0] // groups
    for g in range(groups):
        block = total_ref[pl.ds(g * width, width), :] * scale
        out_refs[columns[g]][slot_ref[g]] = block.astype(LOW)


def call(kernel, name, shapes, operands, flops=0, scratch=(), smem=False, away=0):
    return pl.pallas_call(
        kernel,
        out_shape=tuple(jax.ShapeDtypeStruct(shape, dtype) for shape, dtype in shapes),
        in_specs=([SMEM] if smem else []) + [VMEM] * (len(operands) - smem - away) + [AWAY] * away,
        out_specs=(VMEM,) * len(shapes),
        scratch_shapes=list(scratch),
        compiler_params=pltpu.CompilerParams(vmem_limit_bytes=VMEM_LIMIT),
        cost_estimate=pl.CostEstimate(flops=flops, bytes_accessed=BYTES, transcendentals=0),
        name=name,
    )(*operands)


def shards(vectors, gauge_links, momenta):
    bricks, vecs, subs = (lax.axis_size(axis) for axis in ("brick", "vec", "sub"))
    groups = vecs * subs
    width, sites = vectors.shape[0], vectors.shape[3]
    layers, tiles = sites // PLANE, sites // LANES
    assert groups == bricks and layers > 1 and ITERS == 2
    total_x = bricks * layers
    count = momenta.shape[0]
    brick, vec, sub = (lax.axis_index(axis) for axis in ("brick", "vec", "sub"))
    tiled_vectors = jnp.swapaxes(vectors.reshape((width, 3, 2, tiles, LANES)), 2, 3).reshape((-1, LANES))
    links = jnp.swapaxes(gauge_links.reshape((27, 2, tiles, LANES)), 1, 2)
    edge = links[:9, tiles - TILES :].reshape((-1, LANES))
    links = links.reshape((-1, LANES))
    full, face = (6, width, sites), (6, width, PLANE)
    field, raw, down, up = call(
        open_kernel,
        "open",
        ((full, WIDE), (full, LOW), (face, LOW), (face, LOW)),
        (tiled_vectors, edge),
        flops=1 << 22,
    )
    ahead, behind = shifted(down, "brick", -1), shifted(up, "brick", 1)
    across = [shifted(raw, "vec", a) for a in range(1, vecs)]
    beside = [shifted(raw, "sub", b) for b in range(1, subs)]
    down_two, up_two, rim, back = call(
        rim_kernel,
        "rim",
        ((face, LOW), (face, LOW), ((6, width, 2 * PLANE), WIDE), ((2, 16, sites), WIDE)),
        (field, links),
        flops=1 << 24,
    )
    ahead_two, behind_two = shifted(down_two, "brick", -1), shifted(up_two, "brick", 1)
    place = (brick * layers).astype(jnp.int32).reshape((1,))
    part, table = call(
        functools.partial(local_kernel, total_x),
        "local",
        ((full, WIDE), ((2, count, sites), WIDE)),
        (place, field, links, back, rim, momenta, *beside),
        away=subs - 1,
        flops=1 << 25,
        scratch=(pltpu.VMEM(full, WIDE),),
        smem=True,
    )
    most, token = call(
        close_kernel,
        "close",
        ((full, WIDE), ((8, LANES), WIDE)),
        (part, ahead, behind, links, back),
        flops=1 << 24,
        scratch=(pltpu.VMEM((6, width, 2 * PLANE), WIDE),),
    )
    *across, ahead_two, behind_two, token = lax.optimization_barrier((*across, ahead_two, behind_two, token))
    raws = [raw, *across, *beside] + [shifted(array, "sub", b) for b in range(1, subs) for array in across]
    offsets = [(a, 0) for a in range(vecs)] + [(0, b) for b in range(1, subs)]
    offsets += [(a, b) for b in range(1, subs) for a in range(1, vecs)]
    (faces,) = call(
        face_kernel,
        "face",
        (((6, width, 2 * PLANE), WIDE),),
        (most, ahead_two, behind_two, links, token),
        flops=1 << 22,
    )
    brick_vec, brick_sub = brick // subs, brick % subs
    slots = jnp.stack([(sub - b - brick_sub) % subs for a, b in offsets]).astype(jnp.int32)
    scale = (3.0 * total_x * PLANE) ** (-0.5)
    depth = STEP * 6 * LANES
    columns = count * width
    blocks = call(
        functools.partial(product_kernel, [-a % vecs for a, b in offsets], count, scale),
        "product",
        (((subs, 2 * width, columns), LOW),) * vecs,
        (slots, most, faces, table, *raws),
        away=groups,
        flops=1 << 32,
        scratch=(
            pltpu.VMEM((groups * 2 * width, columns), WIDE),
            pltpu.VMEM((groups * 2 * width, depth), LOW),
            pltpu.VMEM((columns, depth), LOW),
            pltpu.VMEM((groups, *full), LOW),
            pltpu.SemaphoreType.DMA((groups, layers)),
        ),
        smem=True,
    )
    held = [shifted(block, "vec", a) if a else block for a, block in enumerate(blocks)]
    shares = []
    for q in range(vecs):
        place = (vec - brick_vec - q) % vecs
        block = held[0]
        for a in range(1, vecs):
            block = jnp.where(place == a, held[a], block)
        for r in range(subs):
            pairs = [
                (b * subs + s, ((b // subs + q) % vecs * subs + s) * subs + (b % subs + r) % subs)
                for b in range(bricks)
                for s in range(subs)
            ]
            shares.append(lax.ppermute(block[r], ("brick", "sub"), pairs))
    total = functools.reduce(jnp.add, [share.astype(WIDE) for share in shares])
    return jnp.transpose(total.reshape((2, width, count, width)), (1, 2, 0, 3))


def solution(mesh):
    in_specs = (
        P(("vec", "sub"), None, None, ("grp", "brick")),
        P(None, None, None, None, ("grp", "brick")),
        P(),
    )
    out_specs = P(("vec", "sub"), "grp", None, "brick")
    return jax.shard_map(shards, mesh=mesh, in_specs=in_specs, out_specs=out_specs, check_vma=False)
```

```python
import functools
import math

import jax
import jax.numpy as jnp
from jax import lax
from jax.experimental import pallas as pl
from jax.experimental.pallas import tpu as pltpu
from jax.sharding import PartitionSpec as P

LY = 64
LZ = 8
ITERS = 2
KAPPA = 0.125
LANES = 128
PLANE = LY * LZ
TILES = PLANE // LANES
ROWS = 16
BYTES = 1 << 20
LOW = jnp.bfloat16
WIDE = jnp.float32
STEP = 2
VMEM_LIMIT = 40 * 1024 * 1024
VMEM = pl.BlockSpec(memory_space=pltpu.VMEM)
AWAY = pl.BlockSpec(memory_space=pl.ANY)
SMEM = pl.BlockSpec(memory_space=pltpu.SMEM)


def shifted(array, axis, by):
    peers = lax.axis_size(axis)
    return lax.ppermute(array, axis, [(i, (i + by) % peers) for i in range(peers)])


def add_hop(total, link, field, adjoint):
    for row in range(3):
        for column in range(3):
            if adjoint:
                real, imag = link(column, row, 0), link(column, row, 1)
            else:
                real, imag = link(row, column, 0), link(row, column, 1)
            source_real, source_imag = field[2 * column], field[2 * column + 1]
            if adjoint:
                add_real = real * source_real + imag * source_imag
                add_imag = real * source_imag - imag * source_real
            else:
                add_real = real * source_real - imag * source_imag
                add_imag = real * source_imag + imag * source_real
            for part, add in ((0, add_real), (1, add_imag)):
                old = total[2 * row + part]
                total[2 * row + part] = add if old is None else old + add


def lane_roll(value, by):
    return pltpu.roll(value, by % LANES, 1)


def lanes_at(layer, tile):
    return pl.ds(pl.multiple_of(layer * PLANE + tile * LANES, LANES), LANES)


def row_groups(ref):
    size = min(ROWS, ref.shape[1])
    return [pl.ds(start, size) for start in range(0, ref.shape[1], size)]


def load(ref, rows, lanes):
    return [ref[k, rows, lanes].astype(WIDE) for k in range(6)]


def store(ref, rows, lanes, values):
    for k in range(6):
        ref[k, rows, lanes] = values[k].astype(ref.dtype)


def link_at(link_ref, direction, layer, tile):
    tiles = link_ref.shape[0] // 54

    def get(row, column, part):
        matrix = (direction * 3 + row) * 3 + column
        return link_ref[pl.ds((matrix * tiles + layer * TILES + tile) * 2 + part, 1), :]

    return get


def plane_hops(total, link_ref, back_ref, layer, tile, rows, fetch):
    here = fetch(tile)
    after, before = fetch((tile + 1) % TILES), fetch((tile + TILES - 1) % TILES)
    lane = lax.broadcasted_iota(jnp.int32, (rows.size, LANES), 1)
    ahead = [jnp.where(lane >= LANES - LZ, lane_roll(b, -LZ), lane_roll(a, -LZ)) for a, b in zip(here, after)]
    add_hop(total, link_at(link_ref, 1, layer, tile), ahead, False)
    behind = [jnp.where(lane < LZ, lane_roll(b, LZ), lane_roll(a, LZ)) for a, b in zip(here, before)]
    lanes = lanes_at(layer, tile)
    add_hop(total, lambda r, c, part: back_ref[part, pl.ds(3 * r + c, 1), lanes], behind, True)
    depth = lane % LZ
    ahead = [jnp.where(depth == LZ - 1, lane_roll(a, LZ - 1), lane_roll(a, -1)) for a in here]
    add_hop(total, link_at(link_ref, 2, layer, tile), ahead, False)
    turned = [None] * 6
    add_hop(turned, link_at(link_ref, 2, layer, tile), here, True)
    for k in range(6):
        total[k] += jnp.where(depth == 0, lane_roll(turned[k], 1 - LZ), lane_roll(turned[k], 1))
    return here


def combined(here, total):
    return [(1.0 - 6.0 * KAPPA) * a + KAPPA * b for a, b in zip(here, total)]


def first_step(layer, tile, rows, field_ref, link_ref, back_ref):
    layers = field_ref.shape[2] // PLANE
    total = [None] * 6
    if layer < layers - 1:
        source = load(field_ref, rows, lanes_at(layer + 1, tile))
        add_hop(total, link_at(link_ref, 0, layer, tile), source, False)
    if layer > 0:
        source = load(field_ref, rows, lanes_at(layer - 1, tile))
        add_hop(total, link_at(link_ref, 0, layer - 1, tile), source, True)
    fetch = lambda t: load(field_ref, rows, lanes_at(layer, t))
    return combined(plane_hops(total, link_ref, back_ref, layer, tile, rows, fetch), total)


def open_kernel(vector_ref, edge_ref, field_ref, raw_ref, down_ref, up_ref):
    vectors, sites = field_ref.shape[1:]
    tiles, layers = sites // LANES, sites // PLANE
    stride = 6 * tiles
    for k in range(6):
        for tile in range(tiles):
            row = ((k // 2) * tiles + tile) * 2 + k % 2
            value = vector_ref[pl.ds(row, vectors, stride=stride), :]
            field_ref[k, :, pl.ds(tile * LANES, LANES)] = value
            low = value.astype(LOW)
            raw_ref[k, :, pl.ds(tile * LANES, LANES)] = low
            if tile < TILES:
                down_ref[k, :, pl.ds(tile * LANES, LANES)] = low

    @pl.loop(0, TILES)
    def _(tile):
        for rows in row_groups(field_ref):
            turned = [None] * 6
            source = load(field_ref, rows, lanes_at(layers - 1, tile))
            link = lambda row, column, part: edge_ref[pl.ds(((3 * row + column) * TILES + tile) * 2 + part, 1), :]
            add_hop(turned, link, source, True)
            store(up_ref, rows, lanes_at(0, tile), turned)


def rim_kernel(field_ref, link_ref, down_ref, up_ref, rim_ref, back_ref):
    sites = field_ref.shape[2]
    tiles, layers = sites // LANES, sites // PLANE
    lane = lax.broadcasted_iota(jnp.int32, (9, LANES), 1)
    for layer in range(layers):
        for part in range(2):
            row = lambda tile: (9 * tiles + layer * TILES + tile) * 2 + part
            value = [link_ref[pl.ds(row(tile), 9, stride=2 * tiles), :] for tile in range(TILES)]
            value = [lane_roll(v, LZ) for v in value]
            for tile in range(TILES):
                back_ref[part, pl.ds(0, 9), lanes_at(layer, tile)] = jnp.where(lane < LZ, value[tile - 1], value[tile])

    for place, layer in enumerate((0, layers - 1)):

        @pl.loop(0, TILES)
        def _(tile):
            lanes = lanes_at(0, tile)
            for rows in row_groups(field_ref):
                new = first_step(layer, tile, rows, field_ref, link_ref, back_ref)
                store(rim_ref, rows, lanes_at(place, tile), new)
                if place == 0:
                    store(down_ref, rows, lanes, new)
                else:
                    turned = [None] * 6
                    add_hop(turned, link_at(link_ref, 0, layer, tile), new, True)
                    store(up_ref, rows, lanes, turned)


def unit_phase(turns):
    half = math.pi * (turns - jnp.round(turns))
    square = half * half
    cosine, sine = 1.0, 1.0
    for order in range(12, 0, -2):
        sine = 1.0 - square * sine * (1.0 / (order * (order + 1)))
        cosine = 1.0 - square * cosine * (1.0 / (order * (order - 1)))
    sine = half * sine
    return 1.0 - 2.0 * sine * sine, 2.0 * sine * cosine


def local_kernel(
    total_x, place_ref, field_ref, link_ref, back_ref, rim_ref, momenta_ref, *refs
):
    out_ref, table_ref, one_ref = refs[-3:]
    layers = field_ref.shape[2] // PLANE
    count = momenta_ref.shape[0]
    momenta = momenta_ref[...].astype(WIDE)
    lane = lax.broadcasted_iota(jnp.int32, (count, LANES), 1)

    @pl.loop(0, TILES)
    def _(tile):
        column = (tile * (LANES // LZ) + lane // LZ).astype(WIDE)
        depth = (lane % LZ).astype(WIDE)
        turns = [momenta[:, 1:2] * column / LY, momenta[:, 2:3] * depth / LZ]
        part = sum(t - jnp.round(t) for t in turns)
        for layer in range(layers):
            along = momenta[:, 0:1] * (place_ref[0] + layer).astype(WIDE) / total_x
            cosine, sine = unit_phase(along - jnp.round(along) + part)
            table_ref[0, :, lanes_at(layer, tile)] = cosine
            table_ref[1, :, lanes_at(layer, tile)] = sine


    one_ref[:, :, pl.ds(0, PLANE)] = rim_ref[:, :, pl.ds(0, PLANE)]
    one_ref[:, :, pl.ds((layers - 1) * PLANE, PLANE)] = rim_ref[:, :, pl.ds(PLANE, PLANE)]
    for layer in range(1, layers - 1):

        @pl.loop(0, TILES)
        def _(tile):
            for rows in row_groups(field_ref):
                new = first_step(layer, tile, rows, field_ref, link_ref, back_ref)
                store(one_ref, rows, lanes_at(layer, tile), new)

    for layer in range(layers):

        @pl.loop(0, TILES)
        def _(tile):
            for rows in row_groups(field_ref):
                new = first_step(layer, tile, rows, one_ref, link_ref, back_ref)
                if layer in (0, layers - 1):
                    own = load(field_ref, rows, lanes_at(layer, tile))
                    new = [a + KAPPA * KAPPA * b for a, b in zip(new, own)]
                store(out_ref, rows, lanes_at(layer, tile), new)


def close_kernel(part_ref, ahead_ref, behind_ref, link_ref, back_ref, out_ref, token_ref, change_ref):
    layers = part_ref.shape[2] // PLANE
    token_ref[...] = jnp.zeros_like(token_ref)

    @pl.loop(0, TILES)
    def _(tile):
        lanes = lanes_at(0, tile)
        for rows in row_groups(part_ref):
            store(change_ref, rows, lanes, [KAPPA * a for a in load(behind_ref, rows, lanes)])
            high = [None] * 6
            add_hop(high, link_at(link_ref, 0, layers - 1, tile), load(ahead_ref, rows, lanes), False)
            store(change_ref, rows, lanes_at(1, tile), [KAPPA * a for a in high])

    for layer in range(layers):

        @pl.loop(0, TILES)
        def _(tile):
            for rows in row_groups(part_ref):
                new = load(part_ref, rows, lanes_at(layer, tile))
                change = lambda place, t: load(change_ref, rows, lanes_at(place, t))
                hops = [None] * 6
                if layer == 1:
                    add_hop(hops, link_at(link_ref, 0, 0, tile), change(0, tile), True)
                if layer == layers - 2:
                    add_hop(hops, link_at(link_ref, 0, layer, tile), change(1, tile), False)
                for place, edge in ((0, 0), (1, layers - 1)):
                    if layer == edge:
                        if hops[0] is None:
                            hops = [jnp.zeros_like(a) for a in new]
                        here = plane_hops(hops, link_ref, back_ref, layer, tile, rows, lambda t: change(place, t))
                        new = [a + (1.0 - 6.0 * KAPPA) * b for a, b in zip(new, here)]
                if hops[0] is not None:
                    new = [a + KAPPA * b for a, b in zip(new, hops)]
                store(out_ref, rows, lanes_at(layer, tile), new)


def face_kernel(most_ref, ahead_ref, behind_ref, link_ref, token_ref, out_ref):
    layers = most_ref.shape[2] // PLANE

    @pl.loop(0, TILES)
    def _(tile):
        lanes, high = lanes_at(0, tile), lanes_at(1, tile)
        for rows in row_groups(most_ref):
            new = zip(load(most_ref, rows, lanes), load(behind_ref, rows, lanes))
            store(out_ref, rows, lanes, [a + KAPPA * b for a, b in new])
            hop = [None] * 6
            add_hop(hop, link_at(link_ref, 0, layers - 1, tile), load(ahead_ref, rows, lanes), False)
            new = zip(load(most_ref, rows, lanes_at(layers - 1, tile)), hop)
            store(out_ref, rows, high, [a + KAPPA * b for a, b in new])


def product_kernel(columns, begin, count, scale, slot_ref, most_ref, face_ref, table_ref, *refs):
    groups = len(columns)
    away_refs, out_refs, (total_ref, left_ref, right_ref, held_ref, copied) = refs[:groups], refs[groups:-5], refs[-5:]
    raw_refs = [held_ref.at[g] for g in range(groups)]
    vectors = most_ref.shape[1]
    layers = most_ref.shape[2] // PLANE
    depth = 6 * LANES
    step = left_ref.shape[1] // depth

    def copies(layer):
        here = pl.ds(pl.multiple_of(layer * PLANE, PLANE), PLANE)
        return [
            pltpu.make_async_copy(away_refs[g].at[:, :, here], held_ref.at[g, :, :, here], copied.at[g, layer])
            for g in range(groups)
        ]

    for layer in (*range(1, layers - 1), 0, layers - 1):
        for copy in copies(layer):
            copy.start()
    total_ref[...] = jnp.zeros_like(total_ref)

    def ready(layer, block):
        @pl.when(block % blocks == 0)
        def _():
            for copy in copies(layer):
                copy.wait()

    def add(field_ref, place):
        for part in range(step):
            own, lanes = place(part)
            field = [field_ref[k, :, own] for k in range(6)]
            one = [pl.ds(part * depth + 2 * color * LANES, LANES) for color in range(3)]
            two = [pl.ds(part * depth + (2 * color + 1) * LANES, LANES) for color in range(3)]
            for p in range(count):
                cosine = table_ref[0, pl.ds(begin + p, 1), lanes]
                sine = table_ref[1, pl.ds(begin + p, 1), lanes]
                rows = pl.ds(p * vectors, vectors)
                for color in range(3):
                    real, imag = field[2 * color], field[2 * color + 1]
                    right_ref[rows, one[color]] = (cosine * real + sine * imag).astype(LOW)
                    right_ref[rows, two[color]] = (cosine * imag - sine * real).astype(LOW)
            for g, raw_ref in enumerate(raw_refs):
                width = raw_ref.shape[1]
                first = pl.ds(2 * g * width, width)
                second = pl.ds((2 * g + 1) * width, width)
                for color in range(3):
                    real, imag = raw_ref[2 * color, :, lanes], raw_ref[2 * color + 1, :, lanes]
                    left_ref[first, one[color]] = real
                    left_ref[first, two[color]] = imag
                    left_ref[second, one[color]] = -imag
                    left_ref[second, two[color]] = real
        total_ref[...] += lax.dot_general(
            left_ref[...], right_ref[...], (((1,), (1,)), ((), ())), preferred_element_type=WIDE
        )

    blocks = TILES // step

    @pl.loop(0, (layers - 2) * blocks)
    def _(block):
        ready(1 + block // blocks, block)
        add(most_ref, lambda part: (lanes_at(1, block * step + part),) * 2)

    @pl.loop(0, 2 * blocks)
    def _(block):
        layer = block // blocks * (layers - 1)
        tile = block % blocks * step
        ready(layer, block)
        add(face_ref, lambda part: (lanes_at(0, block * step + part), lanes_at(layer, tile + part)))

    width = total_ref.shape[0] // groups
    for g in range(groups):
        block = total_ref[pl.ds(g * width, width), :] * scale
        out_refs[columns[g]][slot_ref[g]] = block.astype(LOW)


def call(kernel, name, shapes, operands, flops=0, scratch=(), smem=False, away=0):
    return pl.pallas_call(
        kernel,
        out_shape=tuple(jax.ShapeDtypeStruct(shape, dtype) for shape, dtype in shapes),
        in_specs=([SMEM] if smem else []) + [VMEM] * (len(operands) - smem - away) + [AWAY] * away,
        out_specs=(VMEM,) * len(shapes),
        scratch_shapes=list(scratch),
        compiler_params=pltpu.CompilerParams(vmem_limit_bytes=VMEM_LIMIT),
        cost_estimate=pl.CostEstimate(flops=flops, bytes_accessed=BYTES, transcendentals=0),
        name=name,
    )(*operands)


def shards(vectors, gauge_links, momenta):
    bricks, vecs, subs = (lax.axis_size(axis) for axis in ("brick", "vec", "sub"))
    groups = vecs * subs
    width, sites = vectors.shape[0], vectors.shape[3]
    layers, tiles = sites // PLANE, sites // LANES
    assert groups == bricks and layers > 1 and ITERS == 2
    total_x = bricks * layers
    count = momenta.shape[0]
    brick, vec, sub = (lax.axis_index(axis) for axis in ("brick", "vec", "sub"))
    tiled_vectors = jnp.swapaxes(vectors.reshape((width, 3, 2, tiles, LANES)), 2, 3).reshape((-1, LANES))
    links = jnp.swapaxes(gauge_links.reshape((27, 2, tiles, LANES)), 1, 2)
    edge = links[:9, tiles - TILES :].reshape((-1, LANES))
    links = links.reshape((-1, LANES))
    full, face = (6, width, sites), (6, width, PLANE)
    field, raw, down, up = call(
        open_kernel,
        "open",
        ((full, WIDE), (full, LOW), (face, LOW), (face, LOW)),
        (tiled_vectors, edge),
        flops=1 << 22,
    )
    ahead, behind = shifted(down, "brick", -1), shifted(up, "brick", 1)
    across = [shifted(raw, "vec", a) for a in range(1, vecs)]
    down_two, up_two, rim, back = call(
        rim_kernel,
        "rim",
        ((face, LOW), (face, LOW), ((6, width, 2 * PLANE), WIDE), ((2, 16, sites), WIDE)),
        (field, links),
        flops=1 << 24,
    )
    ahead_two, behind_two = shifted(down_two, "brick", -1), shifted(up_two, "brick", 1)
    place = (brick * layers).astype(jnp.int32).reshape((1,))
    part, table = call(
        functools.partial(local_kernel, total_x),
        "local",
        ((full, WIDE), ((2, count, sites), WIDE)),
        (place, field, links, back, rim, momenta),
        flops=1 << 25,
        scratch=(pltpu.VMEM(full, WIDE),),
        smem=True,
    )
    most, token = call(
        close_kernel,
        "close",
        ((full, WIDE), ((8, LANES), WIDE)),
        (part, ahead, behind, links, back),
        flops=1 << 24,
        scratch=(pltpu.VMEM((6, width, 2 * PLANE), WIDE),),
    )
    late, token = lax.optimization_barrier((raw, token))
    *across, ahead_two, behind_two, token = lax.optimization_barrier((*across, ahead_two, behind_two, token))
    raws = [raw, *across] + [shifted(array, "sub", b) for b in range(1, subs) for array in (late, *across)]
    offsets = [(a, b) for b in range(subs) for a in range(vecs)]
    (faces,) = call(
        face_kernel,
        "face",
        (((6, width, 2 * PLANE), WIDE),),
        (most, ahead_two, behind_two, links, token),
        flops=1 << 22,
    )
    brick_vec, brick_sub = brick // subs, brick % subs
    slots = jnp.stack([(sub - b - brick_sub) % subs for a, b in offsets]).astype(jnp.int32)
    scale = (3.0 * total_x * PLANE) ** (-0.5)
    depth = STEP * 6 * LANES
    unit = max(1, 2 * LANES // width)
    middle = unit * round(0.6 * count / unit) if unit < count else count // 2
    chunks = []
    for begin, end in ((0, middle), (middle, count)):
        columns = (end - begin) * width
        blocks = call(
            functools.partial(product_kernel, [-a % vecs for a, b in offsets], begin, end - begin, scale),
            "product",
            (((subs, 2 * width, columns), LOW),) * vecs,
            (slots, most, faces, table, *raws),
            away=groups,
            flops=1 << 31,
            scratch=(
                pltpu.VMEM((groups * 2 * width, columns), WIDE),
                pltpu.VMEM((groups * 2 * width, depth), LOW),
                pltpu.VMEM((columns, depth), LOW),
                pltpu.VMEM((groups, *full), LOW),
                pltpu.SemaphoreType.DMA((groups, layers)),
            ),
            smem=True,
        )
        chunks.append([blocks[0], *(shifted(block, "vec", a) for a, block in enumerate(blocks) if a)])
    (*held, chunks[1][0]) = lax.optimization_barrier((*chunks[0], chunks[1][0]))
    chunks[0] = held
    totals = []
    for held, size in zip(chunks, (middle, count - middle)):
        shares = []
        for q in range(vecs):
            place = (vec - brick_vec - q) % vecs
            block = held[0]
            for a in range(1, vecs):
                block = jnp.where(place == a, held[a], block)
            for r in range(subs):
                pairs = [
                    (b * subs + s, ((b // subs + q) % vecs * subs + s) * subs + (b % subs + r) % subs)
                    for b in range(bricks)
                    for s in range(subs)
                ]
                shares.append(lax.ppermute(block[r], ("brick", "sub"), pairs))
        if held is chunks[0]:
            *shares, chunks[1][0] = lax.optimization_barrier((*shares, chunks[1][0]))
        total = functools.reduce(jnp.add, [share.astype(WIDE) for share in shares])
        totals.append(total.reshape((2, width, size, width)))
    return jnp.transpose(jnp.concatenate(totals, axis=2), (1, 2, 0, 3))


def solution(mesh):
    in_specs = (
        P(("vec", "sub"), None, None, ("grp", "brick")),
        P(None, None, None, None, ("grp", "brick")),
        P(),
    )
    out_specs = P(("vec", "sub"), "grp", None, "brick")
    return jax.shard_map(shards, mesh=mesh, in_specs=in_specs, out_specs=out_specs, check_vma=False)
```

```python
import functools
import math

import jax
import jax.numpy as jnp
from jax import lax
from jax.experimental import pallas as pl
from jax.experimental.pallas import tpu as pltpu
from jax.sharding import PartitionSpec as P

LY = 64
LZ = 8
ITERS = 2
KAPPA = 0.125
LANES = 128
PLANE = LY * LZ
TILES = PLANE // LANES
ROWS = 16
BYTES = 1 << 20
LOW = jnp.bfloat16
WIDE = jnp.float32
STEP = 2
VMEM_LIMIT = 56 * 1024 * 1024
VMEM = pl.BlockSpec(memory_space=pltpu.VMEM)
SMEM = pl.BlockSpec(memory_space=pltpu.SMEM)


def shifted(array, axis, by):
    peers = lax.axis_size(axis)
    return lax.ppermute(array, axis, [(i, (i + by) % peers) for i in range(peers)])


def add_hop(total, link, field, adjoint):
    for row in range(3):
        for column in range(3):
            if adjoint:
                real, imag = link(column, row, 0), link(column, row, 1)
            else:
                real, imag = link(row, column, 0), link(row, column, 1)
            source_real, source_imag = field[2 * column], field[2 * column + 1]
            if adjoint:
                add_real = real * source_real + imag * source_imag
                add_imag = real * source_imag - imag * source_real
            else:
                add_real = real * source_real - imag * source_imag
                add_imag = real * source_imag + imag * source_real
            for part, add in ((0, add_real), (1, add_imag)):
                old = total[2 * row + part]
                total[2 * row + part] = add if old is None else old + add


def lane_roll(value, by):
    return pltpu.roll(value, by % LANES, 1)


def lanes_at(layer, tile):
    return pl.ds(pl.multiple_of(layer * PLANE + tile * LANES, LANES), LANES)


def row_groups(ref):
    size = min(ROWS, ref.shape[1])
    return [pl.ds(start, size) for start in range(0, ref.shape[1], size)]


def load(ref, rows, lanes):
    return [ref[k, rows, lanes].astype(WIDE) for k in range(6)]


def store(ref, rows, lanes, values):
    for k in range(6):
        ref[k, rows, lanes] = values[k].astype(ref.dtype)


def link_at(link_ref, direction, layer, tile):
    tiles = link_ref.shape[0] // 54

    def get(row, column, part):
        matrix = (direction * 3 + row) * 3 + column
        return link_ref[pl.ds((matrix * tiles + layer * TILES + tile) * 2 + part, 1), :]

    return get


def plane_hops(total, link_ref, back_ref, layer, tile, rows, fetch):
    here = fetch(tile)
    after, before = fetch((tile + 1) % TILES), fetch((tile + TILES - 1) % TILES)
    lane = lax.broadcasted_iota(jnp.int32, (rows.size, LANES), 1)
    ahead = [jnp.where(lane >= LANES - LZ, lane_roll(b, -LZ), lane_roll(a, -LZ)) for a, b in zip(here, after)]
    add_hop(total, link_at(link_ref, 1, layer, tile), ahead, False)
    behind = [jnp.where(lane < LZ, lane_roll(b, LZ), lane_roll(a, LZ)) for a, b in zip(here, before)]
    lanes = lanes_at(layer, tile)
    add_hop(total, lambda r, c, part: back_ref[part, pl.ds(3 * r + c, 1), lanes], behind, True)
    depth = lane % LZ
    ahead = [jnp.where(depth == LZ - 1, lane_roll(a, LZ - 1), lane_roll(a, -1)) for a in here]
    add_hop(total, link_at(link_ref, 2, layer, tile), ahead, False)
    turned = [None] * 6
    add_hop(turned, link_at(link_ref, 2, layer, tile), here, True)
    for k in range(6):
        total[k] += jnp.where(depth == 0, lane_roll(turned[k], 1 - LZ), lane_roll(turned[k], 1))
    return here


def combined(here, total):
    return [(1.0 - 6.0 * KAPPA) * a + KAPPA * b for a, b in zip(here, total)]


def one_step(layer, layers, tile, rows, fetch, link_ref, back_ref, extra=None):
    total = [None] * 6
    if layer < layers - 1:
        add_hop(total, link_at(link_ref, 0, layer, tile), fetch(layer + 1, tile), False)
    if layer > 0:
        add_hop(total, link_at(link_ref, 0, layer - 1, tile), fetch(layer - 1, tile), True)
    here = plane_hops(total, link_ref, back_ref, layer, tile, rows, lambda t: fetch(layer, t))
    if extra is not None:
        total = [a + b for a, b in zip(total, extra)]
    return combined(here, total)


def open_kernel(vector_ref, link_ref, field_ref, raw_ref, down_ref, up_ref):
    vectors, sites = field_ref.shape[1:]
    tiles, layers = sites // LANES, sites // PLANE
    stride = 6 * tiles
    for k in range(6):
        for tile in range(tiles):
            row = ((k // 2) * tiles + tile) * 2 + k % 2
            value = vector_ref[pl.ds(row, vectors, stride=stride), :]
            field_ref[k, :, pl.ds(tile * LANES, LANES)] = value
            low = value.astype(LOW)
            raw_ref[k, :, pl.ds(tile * LANES, LANES)] = low
            if tile < TILES:
                down_ref[k, :, pl.ds(tile * LANES, LANES)] = low

    @pl.loop(0, TILES)
    def _(tile):
        for rows in row_groups(field_ref):
            turned = [None] * 6
            source = load(field_ref, rows, lanes_at(layers - 1, tile))
            add_hop(turned, link_at(link_ref, 0, layers - 1, tile), source, True)
            store(up_ref, rows, lanes_at(0, tile), turned)


def rim_kernel(field_ref, link_ref, down_ref, up_ref, rim_ref, back_ref):
    sites = field_ref.shape[2]
    tiles, layers = sites // LANES, sites // PLANE
    lane = lax.broadcasted_iota(jnp.int32, (9, LANES), 1)
    for layer in range(layers):
        for part in range(2):
            row = lambda tile: (9 * tiles + layer * TILES + tile) * 2 + part
            value = [link_ref[pl.ds(row(tile), 9, stride=2 * tiles), :] for tile in range(TILES)]
            value = [lane_roll(v, LZ) for v in value]
            for tile in range(TILES):
                back_ref[part, pl.ds(0, 9), lanes_at(layer, tile)] = jnp.where(lane < LZ, value[tile - 1], value[tile])

    for place, layer in enumerate((0, layers - 1)):

        @pl.loop(0, TILES)
        def _(tile):
            lanes = lanes_at(0, tile)
            for rows in row_groups(field_ref):
                fetch = lambda at, t: load(field_ref, rows, lanes_at(at, t))
                new = one_step(layer, layers, tile, rows, fetch, link_ref, back_ref)
                store(rim_ref, rows, lanes_at(place, tile), new)
                if place == 0:
                    store(down_ref, rows, lanes, new)
                else:
                    turned = [None] * 6
                    add_hop(turned, link_at(link_ref, 0, layer, tile), new, True)
                    store(up_ref, rows, lanes, turned)


def unit_phase(turns):
    half = math.pi * (turns - jnp.round(turns))
    square = half * half
    cosine, sine = 1.0, 1.0
    for order in range(12, 0, -2):
        sine = 1.0 - square * sine * (1.0 / (order * (order + 1)))
        cosine = 1.0 - square * cosine * (1.0 / (order * (order - 1)))
    sine = half * sine
    return 1.0 - 2.0 * sine * sine, 2.0 * sine * cosine


def inner_kernel(total_x, place_ref, field_ref, link_ref, back_ref, momenta_ref, out_ref, table_ref):
    layers = field_ref.shape[2] // PLANE
    count = momenta_ref.shape[0]
    momenta = momenta_ref[...].astype(WIDE)
    lane = lax.broadcasted_iota(jnp.int32, (count, LANES), 1)

    @pl.loop(0, TILES)
    def _(tile):
        column = (tile * (LANES // LZ) + lane // LZ).astype(WIDE)
        depth = (lane % LZ).astype(WIDE)
        turns = [momenta[:, 1:2] * column / LY, momenta[:, 2:3] * depth / LZ]
        part = sum(t - jnp.round(t) for t in turns)
        for layer in range(layers):
            along = momenta[:, 0:1] * (place_ref[0] + layer).astype(WIDE) / total_x
            cosine, sine = unit_phase(along - jnp.round(along) + part)
            table_ref[0, :, lanes_at(layer, tile)] = cosine
            table_ref[1, :, lanes_at(layer, tile)] = sine


    for layer in range(1, layers - 1):

        @pl.loop(0, TILES)
        def _(tile):
            for rows in row_groups(field_ref):
                fetch = lambda at, t: load(field_ref, rows, lanes_at(at, t))
                new = one_step(layer, layers, tile, rows, fetch, link_ref, back_ref)
                store(out_ref, rows, lanes_at(layer - 1, tile), new)


def second_kernel(
    field_ref, inner_ref, rim_ref, ahead_ref, behind_ref, link_ref, back_ref, out_ref, most_ref, token_ref, edge_ref
):
    layers = field_ref.shape[2] // PLANE
    token_ref[...] = jnp.zeros_like(token_ref)

    @pl.loop(0, TILES)
    def _(tile):
        lanes, high = lanes_at(0, tile), lanes_at(1, tile)
        for rows in row_groups(field_ref):
            new = zip(load(rim_ref, rows, lanes), load(behind_ref, rows, lanes))
            store(edge_ref, rows, lanes, [a + KAPPA * b for a, b in new])
            hop = [None] * 6
            add_hop(hop, link_at(link_ref, 0, layers - 1, tile), load(ahead_ref, rows, lanes), False)
            store(edge_ref, rows, high, [a + KAPPA * b for a, b in zip(load(rim_ref, rows, high), hop)])

    for layer in range(layers):

        @pl.loop(0, TILES)
        def _(tile):
            for rows in row_groups(field_ref):

                def fetch(at, t):
                    if at in (0, layers - 1):
                        return load(edge_ref, rows, lanes_at(min(at, 1), t))
                    return load(inner_ref, rows, lanes_at(at - 1, t))

                extra = None
                if layer in (0, layers - 1):
                    extra = [KAPPA * a for a in load(field_ref, rows, lanes_at(layer, tile))]
                new = one_step(layer, layers, tile, rows, fetch, link_ref, back_ref, extra)
                if layer in (0, layers - 1):
                    store(most_ref, rows, lanes_at(min(layer, 1), tile), new)
                else:
                    store(out_ref, rows, lanes_at(layer - 1, tile), new)


def face_kernel(most_ref, ahead_ref, behind_ref, link_ref, token_ref, out_ref):
    layers = link_ref.shape[0] // 54 // TILES

    @pl.loop(0, TILES)
    def _(tile):
        lanes, high = lanes_at(0, tile), lanes_at(1, tile)
        for rows in row_groups(most_ref):
            new = zip(load(most_ref, rows, lanes), load(behind_ref, rows, lanes))
            store(out_ref, rows, lanes, [a + KAPPA * b for a, b in new])
            hop = [None] * 6
            add_hop(hop, link_at(link_ref, 0, layers - 1, tile), load(ahead_ref, rows, lanes), False)
            new = zip(load(most_ref, rows, high), hop)
            store(out_ref, rows, high, [a + KAPPA * b for a, b in new])


def product_kernel(columns, count, scale, slot_ref, inner_ref, face_ref, table_ref, *refs):
    groups = len(columns)
    raw_refs, out_refs, (total_ref, left_ref, right_ref) = refs[:groups], refs[groups:-3], refs[-3:]
    vectors = inner_ref.shape[1]
    layers = table_ref.shape[2] // PLANE
    depth = 6 * LANES
    step = left_ref.shape[1] // depth
    total_ref[...] = jnp.zeros_like(total_ref)

    def add(field_ref, place):
        for part in range(step):
            own, lanes = place(part)
            field = [field_ref[k, :, own] for k in range(6)]
            one = [pl.ds(part * depth + 2 * color * LANES, LANES) for color in range(3)]
            two = [pl.ds(part * depth + (2 * color + 1) * LANES, LANES) for color in range(3)]
            for p in range(count):
                cosine = table_ref[0, pl.ds(p, 1), lanes]
                sine = table_ref[1, pl.ds(p, 1), lanes]
                rows = pl.ds(p * vectors, vectors)
                for color in range(3):
                    real, imag = field[2 * color], field[2 * color + 1]
                    right_ref[rows, one[color]] = (cosine * real + sine * imag).astype(LOW)
                    right_ref[rows, two[color]] = (cosine * imag - sine * real).astype(LOW)
            for g, raw_ref in enumerate(raw_refs):
                width = raw_ref.shape[1]
                first = pl.ds(2 * g * width, width)
                second = pl.ds((2 * g + 1) * width, width)
                for color in range(3):
                    real, imag = raw_ref[2 * color, :, lanes], raw_ref[2 * color + 1, :, lanes]
                    left_ref[first, one[color]] = real
                    left_ref[first, two[color]] = imag
                    left_ref[second, one[color]] = -imag
                    left_ref[second, two[color]] = real
        total_ref[...] += lax.dot_general(
            left_ref[...], right_ref[...], (((1,), (1,)), ((), ())), preferred_element_type=WIDE
        )

    blocks = TILES // step

    @pl.loop(0, (layers - 2) * blocks)
    def _(block):
        add(inner_ref, lambda part: (lanes_at(0, block * step + part), lanes_at(1, block * step + part)))

    @pl.loop(0, 2 * blocks)
    def _(block):
        layer = block // blocks * (layers - 1)
        tile = block % blocks * step
        add(face_ref, lambda part: (lanes_at(0, block * step + part), lanes_at(layer, tile + part)))

    width = total_ref.shape[0] // groups
    for g in range(groups):
        block = total_ref[pl.ds(g * width, width), :] * scale
        out_refs[columns[g]][slot_ref[g]] = block.astype(LOW)


def sum_kernel(*refs):
    *share_refs, out_ref = refs
    width = out_ref.shape[1]
    count = out_ref.shape[0] // (2 * width)
    total = sum(ref[...].astype(WIDE) for ref in share_refs)
    for p in range(count):
        block = total[:, p * width : (p + 1) * width]
        for part in range(2):
            rows = pl.ds(2 * p + part, width, stride=2 * count)
            out_ref[rows, :] = block[part * width : (part + 1) * width]


def call(kernel, name, shapes, operands, flops=0, scratch=(), smem=False):
    return pl.pallas_call(
        kernel,
        out_shape=tuple(jax.ShapeDtypeStruct(shape, dtype) for shape, dtype in shapes),
        in_specs=[SMEM if smem and i == 0 else VMEM for i in range(len(operands))],
        out_specs=(VMEM,) * len(shapes),
        scratch_shapes=list(scratch),
        compiler_params=pltpu.CompilerParams(vmem_limit_bytes=VMEM_LIMIT),
        cost_estimate=pl.CostEstimate(flops=flops, bytes_accessed=BYTES, transcendentals=0),
        name=name,
    )(*operands)


def shards(vectors, gauge_links, momenta):
    bricks, vecs, subs = (lax.axis_size(axis) for axis in ("brick", "vec", "sub"))
    groups = vecs * subs
    width, sites = vectors.shape[0], vectors.shape[3]
    layers, tiles = sites // PLANE, sites // LANES
    assert groups == bricks and layers > 2 and ITERS == 2
    total_x = bricks * layers
    count = momenta.shape[0]
    brick, vec, sub = (lax.axis_index(axis) for axis in ("brick", "vec", "sub"))
    tiled_vectors = jnp.swapaxes(vectors.reshape((width, 3, 2, tiles, LANES)), 2, 3).reshape((-1, LANES))
    links = jnp.swapaxes(gauge_links.reshape((27, 2, tiles, LANES)), 1, 2).reshape((-1, LANES))
    full, face = (6, width, sites), (6, width, PLANE)
    field, raw, down, up = call(
        open_kernel,
        "open",
        ((full, WIDE), (full, LOW), (face, LOW), (face, LOW)),
        (tiled_vectors, links),
        flops=1 << 22,
    )
    ahead, behind = shifted(down, "brick", -1), shifted(up, "brick", 1)
    across = [shifted(raw, "vec", a) for a in range(1, vecs)]
    down_two, up_two, rim, back = call(
        rim_kernel,
        "rim",
        ((face, LOW), (face, LOW), ((6, width, 2 * PLANE), WIDE), ((2, 16, sites), WIDE)),
        (field, links),
        flops=1 << 24,
    )
    ahead_two, behind_two = shifted(down_two, "brick", -1), shifted(up_two, "brick", 1)
    place = (brick * layers).astype(jnp.int32).reshape((1,))
    inner, table = call(
        functools.partial(inner_kernel, total_x),
        "inner",
        (((6, width, sites - 2 * PLANE), WIDE), ((2, count, sites), WIDE)),
        (place, field, links, back, momenta),
        flops=1 << 24,
        smem=True,
    )
    smeared, most, token = call(
        second_kernel,
        "second",
        (((6, width, sites - 2 * PLANE), WIDE), ((6, width, 2 * PLANE), WIDE), ((8, LANES), WIDE)),
        (field, inner, rim, ahead, behind, links, back),
        flops=1 << 25,
        scratch=(pltpu.VMEM((6, width, 2 * PLANE), WIDE),),
    )
    late, token = lax.optimization_barrier((raw, token))
    *across, ahead_two, behind_two, token = lax.optimization_barrier((*across, ahead_two, behind_two, token))
    raws = [raw, *across] + [shifted(array, "sub", b) for b in range(1, subs) for array in (late, *across)]
    offsets = [(a, b) for b in range(subs) for a in range(vecs)]
    (faces,) = call(
        face_kernel,
        "face",
        (((6, width, 2 * PLANE), WIDE),),
        (most, ahead_two, behind_two, links, token),
        flops=1 << 22,
    )
    brick_vec, brick_sub = brick // subs, brick % subs
    slots = jnp.stack([(sub - b - brick_sub) % subs for a, b in offsets]).astype(jnp.int32)
    scale = (3.0 * total_x * PLANE) ** (-0.5)
    depth = STEP * 6 * LANES
    columns = count * width
    blocks = call(
        functools.partial(product_kernel, [-a % vecs for a, b in offsets], count, scale),
        "product",
        (((subs, 2 * width, columns), LOW),) * vecs,
        (slots, smeared, faces, table, *raws),
        flops=1 << 32,
        scratch=(
            pltpu.VMEM((groups * 2 * width, columns), WIDE),
            pltpu.VMEM((groups * 2 * width, depth), LOW),
            pltpu.VMEM((columns, depth), LOW),
        ),
        smem=True,
    )
    held = [shifted(block, "vec", a) if a else block for a, block in enumerate(blocks)]
    shares = []
    for q in range(vecs):
        place = (vec - brick_vec - q) % vecs
        block = held[0]
        for a in range(1, vecs):
            block = jnp.where(place == a, held[a], block)
        for r in range(subs):
            pairs = [
                (b * subs + s, ((b // subs + q) % vecs * subs + s) * subs + (b % subs + r) % subs)
                for b in range(bricks)
                for s in range(subs)
            ]
            shares.append(lax.ppermute(block[r], ("brick", "sub"), pairs))
    (total,) = call(sum_kernel, "sum", (((width * count * 2, width), WIDE),), shares, flops=1 << 20)
    return total.reshape((width, count, 2, width))


def solution(mesh):
    in_specs = (
        P(("vec", "sub"), None, None, ("grp", "brick")),
        P(None, None, None, None, ("grp", "brick")),
        P(),
    )
    out_specs = P(("vec", "sub"), "grp", None, "brick")
    return jax.shard_map(shards, mesh=mesh, in_specs=in_specs, out_specs=out_specs, check_vma=False)
```

```python
import functools
import math

import jax
import jax.numpy as jnp
from jax import lax
from jax.experimental import pallas as pl
from jax.experimental.pallas import tpu as pltpu
from jax.sharding import PartitionSpec as P

LY = 64
LZ = 8
ITERS = 2
KAPPA = 0.125
LANES = 128
PLANE = LY * LZ
TILES = PLANE // LANES
ROWS = 16
BYTES = 1 << 20
LOW = jnp.bfloat16
WIDE = jnp.float32
STEP = 2
VMEM_LIMIT = 40 * 1024 * 1024
VMEM = pl.BlockSpec(memory_space=pltpu.VMEM)
SMEM = pl.BlockSpec(memory_space=pltpu.SMEM)


def shifted(array, axis, by):
    peers = lax.axis_size(axis)
    return lax.ppermute(array, axis, [(i, (i + by) % peers) for i in range(peers)])


def add_hop(total, link, field, adjoint):
    for row in range(3):
        for column in range(3):
            if adjoint:
                real, imag = link(column, row, 0), link(column, row, 1)
            else:
                real, imag = link(row, column, 0), link(row, column, 1)
            source_real, source_imag = field[2 * column], field[2 * column + 1]
            if adjoint:
                add_real = real * source_real + imag * source_imag
                add_imag = real * source_imag - imag * source_real
            else:
                add_real = real * source_real - imag * source_imag
                add_imag = real * source_imag + imag * source_real
            for part, add in ((0, add_real), (1, add_imag)):
                old = total[2 * row + part]
                total[2 * row + part] = add if old is None else old + add


def lane_roll(value, by):
    return pltpu.roll(value, by % LANES, 1)


def lanes_at(layer, tile):
    return pl.ds(pl.multiple_of(layer * PLANE + tile * LANES, LANES), LANES)


def row_groups(ref):
    size = min(ROWS, ref.shape[1])
    return [pl.ds(start, size) for start in range(0, ref.shape[1], size)]


def load(ref, rows, lanes):
    return [ref[k, rows, lanes].astype(WIDE) for k in range(6)]


def store(ref, rows, lanes, values):
    for k in range(6):
        ref[k, rows, lanes] = values[k].astype(ref.dtype)


def link_at(link_ref, direction, layer, tile):
    tiles = link_ref.shape[0] // 54

    def get(row, column, part):
        matrix = (direction * 3 + row) * 3 + column
        return link_ref[pl.ds((matrix * tiles + layer * TILES + tile) * 2 + part, 1), :]

    return get


def plane_hops(total, link_ref, back_ref, layer, tile, rows, fetch):
    here = fetch(tile)
    after, before = fetch((tile + 1) % TILES), fetch((tile + TILES - 1) % TILES)
    lane = lax.broadcasted_iota(jnp.int32, (rows.size, LANES), 1)
    ahead = [jnp.where(lane >= LANES - LZ, lane_roll(b, -LZ), lane_roll(a, -LZ)) for a, b in zip(here, after)]
    add_hop(total, link_at(link_ref, 1, layer, tile), ahead, False)
    behind = [jnp.where(lane < LZ, lane_roll(b, LZ), lane_roll(a, LZ)) for a, b in zip(here, before)]
    lanes = lanes_at(layer, tile)
    add_hop(total, lambda r, c, part: back_ref[part, pl.ds(3 * r + c, 1), lanes], behind, True)
    depth = lane % LZ
    ahead = [jnp.where(depth == LZ - 1, lane_roll(a, LZ - 1), lane_roll(a, -1)) for a in here]
    add_hop(total, link_at(link_ref, 2, layer, tile), ahead, False)
    turned = [None] * 6
    add_hop(turned, link_at(link_ref, 2, layer, tile), here, True)
    for k in range(6):
        total[k] += jnp.where(depth == 0, lane_roll(turned[k], 1 - LZ), lane_roll(turned[k], 1))
    return here


def combined(here, total):
    return [(1.0 - 6.0 * KAPPA) * a + KAPPA * b for a, b in zip(here, total)]


def one_step(layer, layers, tile, rows, fetch, link_ref, back_ref, extra=None):
    total = [None] * 6
    if layer < layers - 1:
        add_hop(total, link_at(link_ref, 0, layer, tile), fetch(layer + 1, tile), False)
    if layer > 0:
        add_hop(total, link_at(link_ref, 0, layer - 1, tile), fetch(layer - 1, tile), True)
    here = plane_hops(total, link_ref, back_ref, layer, tile, rows, lambda t: fetch(layer, t))
    if extra is not None:
        total = [a + b for a, b in zip(total, extra)]
    return combined(here, total)


def open_kernel(vector_ref, link_ref, field_ref, raw_ref, down_ref, up_ref):
    vectors, sites = field_ref.shape[1:]
    tiles, layers = sites // LANES, sites // PLANE
    stride = 6 * tiles
    for k in range(6):
        for tile in range(tiles):
            row = ((k // 2) * tiles + tile) * 2 + k % 2
            value = vector_ref[pl.ds(row, vectors, stride=stride), :]
            field_ref[k, :, pl.ds(tile * LANES, LANES)] = value
            low = value.astype(LOW)
            raw_ref[k, :, pl.ds(tile * LANES, LANES)] = low
            if tile < TILES:
                down_ref[k, :, pl.ds(tile * LANES, LANES)] = low

    @pl.loop(0, TILES)
    def _(tile):
        for rows in row_groups(field_ref):
            turned = [None] * 6
            source = load(field_ref, rows, lanes_at(layers - 1, tile))
            add_hop(turned, link_at(link_ref, 0, layers - 1, tile), source, True)
            store(up_ref, rows, lanes_at(0, tile), turned)


def rim_kernel(field_ref, link_ref, down_ref, up_ref, rim_ref, back_ref):
    sites = field_ref.shape[2]
    tiles, layers = sites // LANES, sites // PLANE
    lane = lax.broadcasted_iota(jnp.int32, (9, LANES), 1)
    for layer in range(layers):
        for part in range(2):
            row = lambda tile: (9 * tiles + layer * TILES + tile) * 2 + part
            value = [link_ref[pl.ds(row(tile), 9, stride=2 * tiles), :] for tile in range(TILES)]
            value = [lane_roll(v, LZ) for v in value]
            for tile in range(TILES):
                back_ref[part, pl.ds(0, 9), lanes_at(layer, tile)] = jnp.where(lane < LZ, value[tile - 1], value[tile])

    for place, layer in enumerate((0, layers - 1)):

        @pl.loop(0, TILES)
        def _(tile):
            lanes = lanes_at(0, tile)
            for rows in row_groups(field_ref):
                fetch = lambda at, t: load(field_ref, rows, lanes_at(at, t))
                new = one_step(layer, layers, tile, rows, fetch, link_ref, back_ref)
                store(rim_ref, rows, lanes_at(place, tile), new)
                if place == 0:
                    store(down_ref, rows, lanes, new)
                else:
                    turned = [None] * 6
                    add_hop(turned, link_at(link_ref, 0, layer, tile), new, True)
                    store(up_ref, rows, lanes, turned)


def unit_phase(turns):
    half = math.pi * (turns - jnp.round(turns))
    square = half * half
    cosine, sine = 1.0, 1.0
    for order in range(12, 0, -2):
        sine = 1.0 - square * sine * (1.0 / (order * (order + 1)))
        cosine = 1.0 - square * cosine * (1.0 / (order * (order - 1)))
    sine = half * sine
    return 1.0 - 2.0 * sine * sine, 2.0 * sine * cosine


def inner_kernel(total_x, place_ref, field_ref, link_ref, back_ref, momenta_ref, out_ref, table_ref):
    layers = field_ref.shape[2] // PLANE
    count = momenta_ref.shape[0]
    momenta = momenta_ref[...].astype(WIDE)
    lane = lax.broadcasted_iota(jnp.int32, (count, LANES), 1)

    @pl.loop(0, TILES)
    def _(tile):
        column = (tile * (LANES // LZ) + lane // LZ).astype(WIDE)
        depth = (lane % LZ).astype(WIDE)
        turns = [momenta[:, 1:2] * column / LY, momenta[:, 2:3] * depth / LZ]
        part = sum(t - jnp.round(t) for t in turns)
        for layer in range(layers):
            along = momenta[:, 0:1] * (place_ref[0] + layer).astype(WIDE) / total_x
            cosine, sine = unit_phase(along - jnp.round(along) + part)
            table_ref[0, :, lanes_at(layer, tile)] = cosine
            table_ref[1, :, lanes_at(layer, tile)] = sine


    for layer in range(1, layers - 1):

        @pl.loop(0, TILES)
        def _(tile):
            for rows in row_groups(field_ref):
                fetch = lambda at, t: load(field_ref, rows, lanes_at(at, t))
                new = one_step(layer, layers, tile, rows, fetch, link_ref, back_ref)
                store(out_ref, rows, lanes_at(layer - 1, tile), new)


def second_kernel(
    field_ref, inner_ref, rim_ref, ahead_ref, behind_ref, link_ref, back_ref, out_ref, token_ref, edge_ref
):
    layers = field_ref.shape[2] // PLANE
    token_ref[...] = jnp.zeros_like(token_ref)

    @pl.loop(0, TILES)
    def _(tile):
        lanes, high = lanes_at(0, tile), lanes_at(1, tile)
        for rows in row_groups(field_ref):
            new = zip(load(rim_ref, rows, lanes), load(behind_ref, rows, lanes))
            store(edge_ref, rows, lanes, [a + KAPPA * b for a, b in new])
            hop = [None] * 6
            add_hop(hop, link_at(link_ref, 0, layers - 1, tile), load(ahead_ref, rows, lanes), False)
            store(edge_ref, rows, high, [a + KAPPA * b for a, b in zip(load(rim_ref, rows, high), hop)])

    for layer in range(layers):

        @pl.loop(0, TILES)
        def _(tile):
            for rows in row_groups(field_ref):

                def fetch(at, t):
                    if at in (0, layers - 1):
                        return load(edge_ref, rows, lanes_at(min(at, 1), t))
                    return load(inner_ref, rows, lanes_at(at - 1, t))

                extra = None
                if layer in (0, layers - 1):
                    extra = [KAPPA * a for a in load(field_ref, rows, lanes_at(layer, tile))]
                new = one_step(layer, layers, tile, rows, fetch, link_ref, back_ref, extra)
                store(out_ref, rows, lanes_at(layer, tile), new)


def face_kernel(most_ref, ahead_ref, behind_ref, link_ref, token_ref, out_ref):
    layers = link_ref.shape[0] // 54 // TILES

    @pl.loop(0, TILES)
    def _(tile):
        lanes, high = lanes_at(0, tile), lanes_at(1, tile)
        for rows in row_groups(most_ref):
            new = zip(load(most_ref, rows, lanes), load(behind_ref, rows, lanes))
            store(out_ref, rows, lanes, [a + KAPPA * b for a, b in new])
            hop = [None] * 6
            add_hop(hop, link_at(link_ref, 0, layers - 1, tile), load(ahead_ref, rows, lanes), False)
            new = zip(load(most_ref, rows, lanes_at(layers - 1, tile)), hop)
            store(out_ref, rows, high, [a + KAPPA * b for a, b in new])


def product_kernel(columns, count, scale, slot_ref, most_ref, face_ref, table_ref, *refs):
    groups = len(columns)
    raw_refs, out_refs, (total_ref, left_ref, right_ref) = refs[:groups], refs[groups:-3], refs[-3:]
    vectors = most_ref.shape[1]
    layers = table_ref.shape[2] // PLANE
    depth = 6 * LANES
    step = left_ref.shape[1] // depth
    total_ref[...] = jnp.zeros_like(total_ref)

    def add(field_ref, place):
        for part in range(step):
            own, lanes = place(part)
            field = [field_ref[k, :, own] for k in range(6)]
            one = [pl.ds(part * depth + 2 * color * LANES, LANES) for color in range(3)]
            two = [pl.ds(part * depth + (2 * color + 1) * LANES, LANES) for color in range(3)]
            for p in range(count):
                cosine = table_ref[0, pl.ds(p, 1), lanes]
                sine = table_ref[1, pl.ds(p, 1), lanes]
                rows = pl.ds(p * vectors, vectors)
                for color in range(3):
                    real, imag = field[2 * color], field[2 * color + 1]
                    right_ref[rows, one[color]] = (cosine * real + sine * imag).astype(LOW)
                    right_ref[rows, two[color]] = (cosine * imag - sine * real).astype(LOW)
            for g, raw_ref in enumerate(raw_refs):
                width = raw_ref.shape[1]
                first = pl.ds(2 * g * width, width)
                second = pl.ds((2 * g + 1) * width, width)
                for color in range(3):
                    real, imag = raw_ref[2 * color, :, lanes], raw_ref[2 * color + 1, :, lanes]
                    left_ref[first, one[color]] = real
                    left_ref[first, two[color]] = imag
                    left_ref[second, one[color]] = -imag
                    left_ref[second, two[color]] = real
        total_ref[...] += lax.dot_general(
            left_ref[...], right_ref[...], (((1,), (1,)), ((), ())), preferred_element_type=WIDE
        )

    blocks = TILES // step

    @pl.loop(0, (layers - 2) * blocks)
    def _(block):
        add(most_ref, lambda part: (lanes_at(1, block * step + part),) * 2)

    @pl.loop(0, 2 * blocks)
    def _(block):
        layer = block // blocks * (layers - 1)
        tile = block % blocks * step
        add(face_ref, lambda part: (lanes_at(0, block * step + part), lanes_at(layer, tile + part)))

    width = total_ref.shape[0] // groups
    for g in range(groups):
        block = total_ref[pl.ds(g * width, width), :] * scale
        out_refs[columns[g]][slot_ref[g]] = block.astype(LOW)


def sum_kernel(*refs):
    *share_refs, out_ref = refs
    width = out_ref.shape[1]
    count = out_ref.shape[0] // (2 * width)
    total = sum(ref[...].astype(WIDE) for ref in share_refs)
    for p in range(count):
        block = total[:, p * width : (p + 1) * width]
        for part in range(2):
            rows = pl.ds(2 * p + part, width, stride=2 * count)
            out_ref[rows, :] = block[part * width : (part + 1) * width]


def call(kernel, name, shapes, operands, flops=0, scratch=(), smem=False, alias=None):
    return pl.pallas_call(
        kernel,
        out_shape=tuple(jax.ShapeDtypeStruct(shape, dtype) for shape, dtype in shapes),
        in_specs=[SMEM if smem and i == 0 else VMEM for i in range(len(operands))],
        out_specs=(VMEM,) * len(shapes),
        scratch_shapes=list(scratch),
        input_output_aliases=alias or {},
        compiler_params=pltpu.CompilerParams(vmem_limit_bytes=VMEM_LIMIT),
        cost_estimate=pl.CostEstimate(flops=flops, bytes_accessed=BYTES, transcendentals=0),
        name=name,
    )(*operands)


def shards(vectors, gauge_links, momenta):
    bricks, vecs, subs = (lax.axis_size(axis) for axis in ("brick", "vec", "sub"))
    groups = vecs * subs
    width, sites = vectors.shape[0], vectors.shape[3]
    layers, tiles = sites // PLANE, sites // LANES
    assert groups == bricks and layers > 2 and ITERS == 2
    total_x = bricks * layers
    count = momenta.shape[0]
    brick, vec, sub = (lax.axis_index(axis) for axis in ("brick", "vec", "sub"))
    tiled_vectors = jnp.swapaxes(vectors.reshape((width, 3, 2, tiles, LANES)), 2, 3).reshape((-1, LANES))
    links = jnp.swapaxes(gauge_links.reshape((27, 2, tiles, LANES)), 1, 2).reshape((-1, LANES))
    full, face = (6, width, sites), (6, width, PLANE)
    field, raw, down, up = call(
        open_kernel,
        "open",
        ((full, WIDE), (full, LOW), (face, LOW), (face, LOW)),
        (tiled_vectors, links),
        flops=1 << 22,
    )
    ahead, behind = shifted(down, "brick", -1), shifted(up, "brick", 1)
    across = [shifted(raw, "vec", a) for a in range(1, vecs)]
    down_two, up_two, rim, back = call(
        rim_kernel,
        "rim",
        ((face, LOW), (face, LOW), ((6, width, 2 * PLANE), WIDE), ((2, 16, sites), WIDE)),
        (field, links),
        flops=1 << 24,
    )
    ahead_two, behind_two = shifted(down_two, "brick", -1), shifted(up_two, "brick", 1)
    place = (brick * layers).astype(jnp.int32).reshape((1,))
    inner, table = call(
        functools.partial(inner_kernel, total_x),
        "inner",
        (((6, width, sites - 2 * PLANE), WIDE), ((2, count, sites), WIDE)),
        (place, field, links, back, momenta),
        flops=1 << 24,
        smem=True,
    )
    most, token = call(
        second_kernel,
        "second",
        ((full, WIDE), ((8, LANES), WIDE)),
        (field, inner, rim, ahead, behind, links, back),
        alias={0: 0},
        flops=1 << 25,
        scratch=(pltpu.VMEM((6, width, 2 * PLANE), WIDE),),
    )
    late, token = lax.optimization_barrier((raw, token))
    *across, ahead_two, behind_two, token = lax.optimization_barrier((*across, ahead_two, behind_two, token))
    raws = [raw, *across] + [shifted(array, "sub", b) for b in range(1, subs) for array in (late, *across)]
    offsets = [(a, b) for b in range(subs) for a in range(vecs)]
    (faces,) = call(
        face_kernel,
        "face",
        (((6, width, 2 * PLANE), WIDE),),
        (most, ahead_two, behind_two, links, token),
        flops=1 << 22,
    )
    brick_vec, brick_sub = brick // subs, brick % subs
    slots = jnp.stack([(sub - b - brick_sub) % subs for a, b in offsets]).astype(jnp.int32)
    scale = (3.0 * total_x * PLANE) ** (-0.5)
    depth = STEP * 6 * LANES
    columns = count * width
    blocks = call(
        functools.partial(product_kernel, [-a % vecs for a, b in offsets], count, scale),
        "product",
        (((subs, 2 * width, columns), LOW),) * vecs,
        (slots, most, faces, table, *raws),
        flops=1 << 32,
        scratch=(
            pltpu.VMEM((groups * 2 * width, columns), WIDE),
            pltpu.VMEM((groups * 2 * width, depth), LOW),
            pltpu.VMEM((columns, depth), LOW),
        ),
        smem=True,
    )
    held = [shifted(block, "vec", a) if a else block for a, block in enumerate(blocks)]
    shares = []
    for q in range(vecs):
        place = (vec - brick_vec - q) % vecs
        block = held[0]
        for a in range(1, vecs):
            block = jnp.where(place == a, held[a], block)
        for r in range(subs):
            pairs = [
                (b * subs + s, ((b // subs + q) % vecs * subs + s) * subs + (b % subs + r) % subs)
                for b in range(bricks)
                for s in range(subs)
            ]
            shares.append(lax.ppermute(block[r], ("brick", "sub"), pairs))
    (total,) = call(sum_kernel, "sum", (((width * count * 2, width), WIDE),), shares, flops=1 << 20)
    return total.reshape((width, count, 2, width))


def solution(mesh):
    in_specs = (
        P(("vec", "sub"), None, None, ("grp", "brick")),
        P(None, None, None, None, ("grp", "brick")),
        P(),
    )
    out_specs = P(("vec", "sub"), "grp", None, "brick")
    return jax.shard_map(shards, mesh=mesh, in_specs=in_specs, out_specs=out_specs, check_vma=False)
```

```python
import functools
import math

import jax
import jax.numpy as jnp
from jax import lax
from jax.experimental import pallas as pl
from jax.experimental.pallas import tpu as pltpu
from jax.sharding import PartitionSpec as P

LY = 64
LZ = 8
ITERS = 2
KAPPA = 0.125
LANES = 128
PLANE = LY * LZ
TILES = PLANE // LANES
ROWS = 16
BYTES = 1 << 20
LOW = jnp.bfloat16
WIDE = jnp.float32
STEP = 2
VMEM_LIMIT = 40 * 1024 * 1024
VMEM = pl.BlockSpec(memory_space=pltpu.VMEM)
AWAY = pl.BlockSpec(memory_space=pltpu.HBM)
SMEM = pl.BlockSpec(memory_space=pltpu.SMEM)


def shifted(array, axis, by):
    peers = lax.axis_size(axis)
    return lax.ppermute(array, axis, [(i, (i + by) % peers) for i in range(peers)])


def add_hop(total, link, field, adjoint):
    for row in range(3):
        for column in range(3):
            if adjoint:
                real, imag = link(column, row, 0), link(column, row, 1)
            else:
                real, imag = link(row, column, 0), link(row, column, 1)
            source_real, source_imag = field[2 * column], field[2 * column + 1]
            if adjoint:
                add_real = real * source_real + imag * source_imag
                add_imag = real * source_imag - imag * source_real
            else:
                add_real = real * source_real - imag * source_imag
                add_imag = real * source_imag + imag * source_real
            for part, add in ((0, add_real), (1, add_imag)):
                old = total[2 * row + part]
                total[2 * row + part] = add if old is None else old + add


def lane_roll(value, by):
    return pltpu.roll(value, by % LANES, 1)


def lanes_at(layer, tile):
    return pl.ds(pl.multiple_of(layer * PLANE + tile * LANES, LANES), LANES)


def row_groups(ref):
    size = min(ROWS, ref.shape[1])
    return [pl.ds(start, size) for start in range(0, ref.shape[1], size)]


def load(ref, rows, lanes):
    return [ref[k, rows, lanes].astype(WIDE) for k in range(6)]


def store(ref, rows, lanes, values):
    for k in range(6):
        ref[k, rows, lanes] = values[k].astype(ref.dtype)


def link_at(link_ref, direction, layer, tile):
    tiles = link_ref.shape[0] // 54

    def get(row, column, part):
        matrix = (direction * 3 + row) * 3 + column
        return link_ref[pl.ds((matrix * tiles + layer * TILES + tile) * 2 + part, 1), :]

    return get


def plane_hops(total, link_ref, back_ref, layer, tile, rows, fetch):
    here = fetch(tile)
    after, before = fetch((tile + 1) % TILES), fetch((tile + TILES - 1) % TILES)
    lane = lax.broadcasted_iota(jnp.int32, (rows.size, LANES), 1)
    ahead = [jnp.where(lane >= LANES - LZ, lane_roll(b, -LZ), lane_roll(a, -LZ)) for a, b in zip(here, after)]
    add_hop(total, link_at(link_ref, 1, layer, tile), ahead, False)
    behind = [jnp.where(lane < LZ, lane_roll(b, LZ), lane_roll(a, LZ)) for a, b in zip(here, before)]
    lanes = lanes_at(layer, tile)
    add_hop(total, lambda r, c, part: back_ref[part, pl.ds(3 * r + c, 1), lanes], behind, True)
    depth = lane % LZ
    ahead = [jnp.where(depth == LZ - 1, lane_roll(a, LZ - 1), lane_roll(a, -1)) for a in here]
    add_hop(total, link_at(link_ref, 2, layer, tile), ahead, False)
    turned = [None] * 6
    add_hop(turned, link_at(link_ref, 2, layer, tile), here, True)
    for k in range(6):
        total[k] += jnp.where(depth == 0, lane_roll(turned[k], 1 - LZ), lane_roll(turned[k], 1))
    return here


def combined(here, total):
    return [(1.0 - 6.0 * KAPPA) * a + KAPPA * b for a, b in zip(here, total)]


def one_step(layer, layers, tile, rows, fetch, link_ref, back_ref, extra=None):
    total = [None] * 6
    if layer < layers - 1:
        add_hop(total, link_at(link_ref, 0, layer, tile), fetch(layer + 1, tile), False)
    if layer > 0:
        add_hop(total, link_at(link_ref, 0, layer - 1, tile), fetch(layer - 1, tile), True)
    here = plane_hops(total, link_ref, back_ref, layer, tile, rows, lambda t: fetch(layer, t))
    if extra is not None:
        total = [a + b for a, b in zip(total, extra)]
    return combined(here, total)


def open_kernel(vector_ref, link_ref, field_ref, raw_ref, down_ref, up_ref):
    vectors, sites = field_ref.shape[1:]
    tiles, layers = sites // LANES, sites // PLANE
    stride = 6 * tiles
    for k in range(6):
        for tile in range(tiles):
            row = ((k // 2) * tiles + tile) * 2 + k % 2
            value = vector_ref[pl.ds(row, vectors, stride=stride), :]
            field_ref[k, :, pl.ds(tile * LANES, LANES)] = value
            low = value.astype(LOW)
            raw_ref[k, :, pl.ds(tile * LANES, LANES)] = low
            if tile < TILES:
                down_ref[k, :, pl.ds(tile * LANES, LANES)] = low

    @pl.loop(0, TILES)
    def _(tile):
        for rows in row_groups(field_ref):
            turned = [None] * 6
            source = load(field_ref, rows, lanes_at(layers - 1, tile))
            add_hop(turned, link_at(link_ref, 0, layers - 1, tile), source, True)
            store(up_ref, rows, lanes_at(0, tile), turned)


def rim_kernel(field_ref, link_ref, down_ref, up_ref, rim_ref, back_ref):
    sites = field_ref.shape[2]
    tiles, layers = sites // LANES, sites // PLANE
    lane = lax.broadcasted_iota(jnp.int32, (9, LANES), 1)
    for layer in range(layers):
        for part in range(2):
            row = lambda tile: (9 * tiles + layer * TILES + tile) * 2 + part
            value = [link_ref[pl.ds(row(tile), 9, stride=2 * tiles), :] for tile in range(TILES)]
            value = [lane_roll(v, LZ) for v in value]
            for tile in range(TILES):
                back_ref[part, pl.ds(0, 9), lanes_at(layer, tile)] = jnp.where(lane < LZ, value[tile - 1], value[tile])

    for place, layer in enumerate((0, layers - 1)):

        @pl.loop(0, TILES)
        def _(tile):
            lanes = lanes_at(0, tile)
            for rows in row_groups(field_ref):
                fetch = lambda at, t: load(field_ref, rows, lanes_at(at, t))
                new = one_step(layer, layers, tile, rows, fetch, link_ref, back_ref)
                store(rim_ref, rows, lanes_at(place, tile), new)
                if place == 0:
                    store(down_ref, rows, lanes, new)
                else:
                    turned = [None] * 6
                    add_hop(turned, link_at(link_ref, 0, layer, tile), new, True)
                    store(up_ref, rows, lanes, turned)


def unit_phase(turns):
    half = math.pi * (turns - jnp.round(turns))
    square = half * half
    cosine, sine = 1.0, 1.0
    for order in range(12, 0, -2):
        sine = 1.0 - square * sine * (1.0 / (order * (order + 1)))
        cosine = 1.0 - square * cosine * (1.0 / (order * (order - 1)))
    sine = half * sine
    return 1.0 - 2.0 * sine * sine, 2.0 * sine * cosine


def inner_kernel(total_x, place_ref, field_ref, link_ref, back_ref, momenta_ref, *refs):
    out_ref, table_ref = refs[-2:]
    layers = field_ref.shape[2] // PLANE
    count = momenta_ref.shape[0]
    momenta = momenta_ref[...].astype(WIDE)
    lane = lax.broadcasted_iota(jnp.int32, (count, LANES), 1)

    @pl.loop(0, TILES)
    def _(tile):
        column = (tile * (LANES // LZ) + lane // LZ).astype(WIDE)
        depth = (lane % LZ).astype(WIDE)
        turns = [momenta[:, 1:2] * column / LY, momenta[:, 2:3] * depth / LZ]
        part = sum(t - jnp.round(t) for t in turns)
        for layer in range(layers):
            along = momenta[:, 0:1] * (place_ref[0] + layer).astype(WIDE) / total_x
            cosine, sine = unit_phase(along - jnp.round(along) + part)
            table_ref[0, :, lanes_at(layer, tile)] = cosine
            table_ref[1, :, lanes_at(layer, tile)] = sine


    for layer in range(1, layers - 1):

        @pl.loop(0, TILES)
        def _(tile):
            for rows in row_groups(field_ref):
                fetch = lambda at, t: load(field_ref, rows, lanes_at(at, t))
                new = one_step(layer, layers, tile, rows, fetch, link_ref, back_ref)
                store(out_ref, rows, lanes_at(layer - 1, tile), new)


def second_kernel(
    field_ref, inner_ref, rim_ref, ahead_ref, behind_ref, link_ref, back_ref, out_ref, token_ref, edge_ref
):
    layers = field_ref.shape[2] // PLANE
    token_ref[...] = jnp.zeros_like(token_ref)

    @pl.loop(0, TILES)
    def _(tile):
        lanes, high = lanes_at(0, tile), lanes_at(1, tile)
        for rows in row_groups(field_ref):
            new = zip(load(rim_ref, rows, lanes), load(behind_ref, rows, lanes))
            store(edge_ref, rows, lanes, [a + KAPPA * b for a, b in new])
            hop = [None] * 6
            add_hop(hop, link_at(link_ref, 0, layers - 1, tile), load(ahead_ref, rows, lanes), False)
            store(edge_ref, rows, high, [a + KAPPA * b for a, b in zip(load(rim_ref, rows, high), hop)])

    for layer in range(layers):

        @pl.loop(0, TILES)
        def _(tile):
            for rows in row_groups(field_ref):

                def fetch(at, t):
                    if at in (0, layers - 1):
                        return load(edge_ref, rows, lanes_at(min(at, 1), t))
                    return load(inner_ref, rows, lanes_at(at - 1, t))

                extra = None
                if layer in (0, layers - 1):
                    extra = [KAPPA * a for a in load(field_ref, rows, lanes_at(layer, tile))]
                new = one_step(layer, layers, tile, rows, fetch, link_ref, back_ref, extra)
                store(out_ref, rows, lanes_at(layer, tile), new)


def face_kernel(most_ref, ahead_ref, behind_ref, link_ref, token_ref, out_ref):
    layers = link_ref.shape[0] // 54 // TILES

    @pl.loop(0, TILES)
    def _(tile):
        lanes, high = lanes_at(0, tile), lanes_at(1, tile)
        for rows in row_groups(most_ref):
            new = zip(load(most_ref, rows, lanes), load(behind_ref, rows, lanes))
            store(out_ref, rows, lanes, [a + KAPPA * b for a, b in new])
            hop = [None] * 6
            add_hop(hop, link_at(link_ref, 0, layers - 1, tile), load(ahead_ref, rows, lanes), False)
            new = zip(load(most_ref, rows, lanes_at(layers - 1, tile)), hop)
            store(out_ref, rows, high, [a + KAPPA * b for a, b in new])


def product_kernel(columns, count, scale, slot_ref, most_ref, face_ref, table_ref, *refs):
    groups = len(columns)
    raw_refs, out_refs, (total_ref, left_ref, right_ref) = refs[:groups], refs[groups:-3], refs[-3:]
    vectors = most_ref.shape[1]
    layers = table_ref.shape[2] // PLANE
    depth = 6 * LANES
    step = left_ref.shape[1] // depth
    total_ref[...] = jnp.zeros_like(total_ref)

    def add(field_ref, place):
        for part in range(step):
            own, lanes = place(part)
            field = [field_ref[k, :, own] for k in range(6)]
            one = [pl.ds(part * depth + 2 * color * LANES, LANES) for color in range(3)]
            two = [pl.ds(part * depth + (2 * color + 1) * LANES, LANES) for color in range(3)]
            for p in range(count):
                cosine = table_ref[0, pl.ds(p, 1), lanes]
                sine = table_ref[1, pl.ds(p, 1), lanes]
                rows = pl.ds(p * vectors, vectors)
                for color in range(3):
                    real, imag = field[2 * color], field[2 * color + 1]
                    right_ref[rows, one[color]] = (cosine * real + sine * imag).astype(LOW)
                    right_ref[rows, two[color]] = (cosine * imag - sine * real).astype(LOW)
            for g, raw_ref in enumerate(raw_refs):
                width = raw_ref.shape[1]
                first = pl.ds(2 * g * width, width)
                second = pl.ds((2 * g + 1) * width, width)
                for color in range(3):
                    real, imag = raw_ref[2 * color, :, lanes], raw_ref[2 * color + 1, :, lanes]
                    left_ref[first, one[color]] = real
                    left_ref[first, two[color]] = imag
                    left_ref[second, one[color]] = -imag
                    left_ref[second, two[color]] = real
        total_ref[...] += lax.dot_general(
            left_ref[...], right_ref[...], (((1,), (1,)), ((), ())), preferred_element_type=WIDE
        )

    blocks = TILES // step

    @pl.loop(0, (layers - 2) * blocks)
    def _(block):
        add(most_ref, lambda part: (lanes_at(1, block * step + part),) * 2)

    @pl.loop(0, 2 * blocks)
    def _(block):
        layer = block // blocks * (layers - 1)
        tile = block % blocks * step
        add(face_ref, lambda part: (lanes_at(0, block * step + part), lanes_at(layer, tile + part)))

    width = total_ref.shape[0] // groups
    for g in range(groups):
        block = total_ref[pl.ds(g * width, width), :] * scale
        out_refs[columns[g]][slot_ref[g]] = block.astype(LOW)


def sum_kernel(*refs):
    *share_refs, out_ref = refs
    width = out_ref.shape[1]
    count = out_ref.shape[0] // (2 * width)
    total = sum(ref[...].astype(WIDE) for ref in share_refs)
    for p in range(count):
        block = total[:, p * width : (p + 1) * width]
        for part in range(2):
            rows = pl.ds(2 * p + part, width, stride=2 * count)
            out_ref[rows, :] = block[part * width : (part + 1) * width]


def call(kernel, name, shapes, operands, flops=0, scratch=(), smem=False, alias=None, away=0):
    return pl.pallas_call(
        kernel,
        out_shape=tuple(jax.ShapeDtypeStruct(shape, dtype) for shape, dtype in shapes),
        in_specs=([SMEM] if smem else []) + [VMEM] * (len(operands) - smem - away) + [AWAY] * away,
        out_specs=(VMEM,) * len(shapes),
        scratch_shapes=list(scratch),
        input_output_aliases=alias or {},
        compiler_params=pltpu.CompilerParams(vmem_limit_bytes=VMEM_LIMIT),
        cost_estimate=pl.CostEstimate(flops=flops, bytes_accessed=BYTES, transcendentals=0),
        name=name,
    )(*operands)


def shards(vectors, gauge_links, momenta):
    bricks, vecs, subs = (lax.axis_size(axis) for axis in ("brick", "vec", "sub"))
    groups = vecs * subs
    width, sites = vectors.shape[0], vectors.shape[3]
    layers, tiles = sites // PLANE, sites // LANES
    assert groups == bricks and layers > 2 and ITERS == 2
    total_x = bricks * layers
    count = momenta.shape[0]
    brick, vec, sub = (lax.axis_index(axis) for axis in ("brick", "vec", "sub"))
    tiled_vectors = jnp.swapaxes(vectors.reshape((width, 3, 2, tiles, LANES)), 2, 3).reshape((-1, LANES))
    links = jnp.swapaxes(gauge_links.reshape((27, 2, tiles, LANES)), 1, 2).reshape((-1, LANES))
    full, face = (6, width, sites), (6, width, PLANE)
    field, raw, down, up = call(
        open_kernel,
        "open",
        ((full, WIDE), (full, LOW), (face, LOW), (face, LOW)),
        (tiled_vectors, links),
        flops=1 << 22,
    )
    ahead, behind = shifted(down, "brick", -1), shifted(up, "brick", 1)
    across = [shifted(raw, "vec", a) for a in range(1, vecs)]
    beside = [shifted(raw, "sub", b) for b in range(1, subs)]
    down_two, up_two, rim, back = call(
        rim_kernel,
        "rim",
        ((face, LOW), (face, LOW), ((6, width, 2 * PLANE), WIDE), ((2, 16, sites), WIDE)),
        (field, links),
        flops=1 << 24,
    )
    ahead_two, behind_two = shifted(down_two, "brick", -1), shifted(up_two, "brick", 1)
    place = (brick * layers).astype(jnp.int32).reshape((1,))
    inner, table = call(
        functools.partial(inner_kernel, total_x),
        "inner",
        (((6, width, sites - 2 * PLANE), WIDE), ((2, count, sites), WIDE)),
        (place, field, links, back, momenta, *beside),
        away=subs - 1,
        flops=1 << 24,
        smem=True,
    )
    most, token = call(
        second_kernel,
        "second",
        ((full, WIDE), ((8, LANES), WIDE)),
        (field, inner, rim, ahead, behind, links, back),
        alias={0: 0},
        flops=1 << 25,
        scratch=(pltpu.VMEM((6, width, 2 * PLANE), WIDE),),
    )
    *across, ahead_two, behind_two, token = lax.optimization_barrier((*across, ahead_two, behind_two, token))
    raws = [raw, *across, *beside] + [shifted(array, "sub", b) for b in range(1, subs) for array in across]
    offsets = [(a, 0) for a in range(vecs)] + [(0, b) for b in range(1, subs)]
    offsets += [(a, b) for b in range(1, subs) for a in range(1, vecs)]
    (faces,) = call(
        face_kernel,
        "face",
        (((6, width, 2 * PLANE), WIDE),),
        (most, ahead_two, behind_two, links, token),
        flops=1 << 22,
    )
    brick_vec, brick_sub = brick // subs, brick % subs
    slots = jnp.stack([(sub - b - brick_sub) % subs for a, b in offsets]).astype(jnp.int32)
    scale = (3.0 * total_x * PLANE) ** (-0.5)
    depth = STEP * 6 * LANES
    columns = count * width
    blocks = call(
        functools.partial(product_kernel, [-a % vecs for a, b in offsets], count, scale),
        "product",
        (((subs, 2 * width, columns), LOW),) * vecs,
        (slots, most, faces, table, *raws),
        flops=1 << 32,
        scratch=(
            pltpu.VMEM((groups * 2 * width, columns), WIDE),
            pltpu.VMEM((groups * 2 * width, depth), LOW),
            pltpu.VMEM((columns, depth), LOW),
        ),
        smem=True,
    )
    held = [shifted(block, "vec", a) if a else block for a, block in enumerate(blocks)]
    shares = []
    for q in range(vecs):
        place = (vec - brick_vec - q) % vecs
        block = held[0]
        for a in range(1, vecs):
            block = jnp.where(place == a, held[a], block)
        for r in range(subs):
            pairs = [
                (b * subs + s, ((b // subs + q) % vecs * subs + s) * subs + (b % subs + r) % subs)
                for b in range(bricks)
                for s in range(subs)
            ]
            shares.append(lax.ppermute(block[r], ("brick", "sub"), pairs))
    (total,) = call(sum_kernel, "sum", (((width * count * 2, width), WIDE),), shares, flops=1 << 20)
    return total.reshape((width, count, 2, width))


def solution(mesh):
    in_specs = (
        P(("vec", "sub"), None, None, ("grp", "brick")),
        P(None, None, None, None, ("grp", "brick")),
        P(),
    )
    out_specs = P(("vec", "sub"), "grp", None, "brick")
    return jax.shard_map(shards, mesh=mesh, in_specs=in_specs, out_specs=out_specs, check_vma=False)
```

```python
import functools
import math

import jax
import jax.numpy as jnp
from jax import lax
from jax.experimental import pallas as pl
from jax.experimental.pallas import tpu as pltpu
from jax.sharding import PartitionSpec as P

LY = 64
LZ = 8
ITERS = 2
KAPPA = 0.125
LANES = 128
PLANE = LY * LZ
TILES = PLANE // LANES
ROWS = 16
BYTES = 1 << 20
LOW = jnp.bfloat16
WIDE = jnp.float32
STEP = 2
VMEM_LIMIT = 40 * 1024 * 1024
VMEM = pl.BlockSpec(memory_space=pltpu.VMEM)
SMEM = pl.BlockSpec(memory_space=pltpu.SMEM)


def shifted(array, axis, by):
    peers = lax.axis_size(axis)
    return lax.ppermute(array, axis, [(i, (i + by) % peers) for i in range(peers)])


def add_hop(total, link, field, adjoint):
    for row in range(3):
        for column in range(3):
            if adjoint:
                real, imag = link(column, row, 0), link(column, row, 1)
            else:
                real, imag = link(row, column, 0), link(row, column, 1)
            source_real, source_imag = field[2 * column], field[2 * column + 1]
            if adjoint:
                add_real = real * source_real + imag * source_imag
                add_imag = real * source_imag - imag * source_real
            else:
                add_real = real * source_real - imag * source_imag
                add_imag = real * source_imag + imag * source_real
            for part, add in ((0, add_real), (1, add_imag)):
                old = total[2 * row + part]
                total[2 * row + part] = add if old is None else old + add


def lane_roll(value, by):
    return pltpu.roll(value, by % LANES, 1)


def lanes_at(layer, tile):
    return pl.ds(pl.multiple_of(layer * PLANE + tile * LANES, LANES), LANES)


def row_groups(ref):
    size = min(ROWS, ref.shape[1])
    return [pl.ds(start, size) for start in range(0, ref.shape[1], size)]


def load(ref, rows, lanes):
    return [ref[k, rows, lanes].astype(WIDE) for k in range(6)]


def store(ref, rows, lanes, values):
    for k in range(6):
        ref[k, rows, lanes] = values[k].astype(ref.dtype)


def link_at(link_ref, direction, layer, tile):
    tiles = link_ref.shape[0] // 54

    def get(row, column, part):
        matrix = (direction * 3 + row) * 3 + column
        return link_ref[pl.ds((matrix * tiles + layer * TILES + tile) * 2 + part, 1), :]

    return get


def plane_hops(total, link_ref, back_ref, layer, tile, rows, fetch):
    here = fetch(tile)
    after, before = fetch((tile + 1) % TILES), fetch((tile + TILES - 1) % TILES)
    lane = lax.broadcasted_iota(jnp.int32, (rows.size, LANES), 1)
    ahead = [jnp.where(lane >= LANES - LZ, lane_roll(b, -LZ), lane_roll(a, -LZ)) for a, b in zip(here, after)]
    add_hop(total, link_at(link_ref, 1, layer, tile), ahead, False)
    behind = [jnp.where(lane < LZ, lane_roll(b, LZ), lane_roll(a, LZ)) for a, b in zip(here, before)]
    lanes = lanes_at(layer, tile)
    add_hop(total, lambda r, c, part: back_ref[part, pl.ds(3 * r + c, 1), lanes], behind, True)
    depth = lane % LZ
    ahead = [jnp.where(depth == LZ - 1, lane_roll(a, LZ - 1), lane_roll(a, -1)) for a in here]
    add_hop(total, link_at(link_ref, 2, layer, tile), ahead, False)
    turned = [None] * 6
    add_hop(turned, link_at(link_ref, 2, layer, tile), here, True)
    for k in range(6):
        total[k] += jnp.where(depth == 0, lane_roll(turned[k], 1 - LZ), lane_roll(turned[k], 1))
    return here


def combined(here, total):
    return [(1.0 - 6.0 * KAPPA) * a + KAPPA * b for a, b in zip(here, total)]


def one_step(layer, layers, tile, rows, fetch, link_ref, back_ref, extra=None):
    total = [None] * 6
    if layer < layers - 1:
        add_hop(total, link_at(link_ref, 0, layer, tile), fetch(layer + 1, tile), False)
    if layer > 0:
        add_hop(total, link_at(link_ref, 0, layer - 1, tile), fetch(layer - 1, tile), True)
    here = plane_hops(total, link_ref, back_ref, layer, tile, rows, lambda t: fetch(layer, t))
    if extra is not None:
        total = [a + b for a, b in zip(total, extra)]
    return combined(here, total)


def open_kernel(vector_ref, link_ref, field_ref, raw_ref, down_ref, up_ref):
    vectors, sites = field_ref.shape[1:]
    tiles, layers = sites // LANES, sites // PLANE
    stride = 6 * tiles
    for k in range(6):
        for tile in range(tiles):
            row = ((k // 2) * tiles + tile) * 2 + k % 2
            value = vector_ref[pl.ds(row, vectors, stride=stride), :]
            field_ref[k, :, pl.ds(tile * LANES, LANES)] = value
            low = value.astype(LOW)
            raw_ref[k, :, pl.ds(tile * LANES, LANES)] = low
            if tile < TILES:
                down_ref[k, :, pl.ds(tile * LANES, LANES)] = low

    @pl.loop(0, TILES)
    def _(tile):
        for rows in row_groups(field_ref):
            turned = [None] * 6
            source = load(field_ref, rows, lanes_at(layers - 1, tile))
            add_hop(turned, link_at(link_ref, 0, layers - 1, tile), source, True)
            store(up_ref, rows, lanes_at(0, tile), turned)


def rim_kernel(field_ref, link_ref, down_ref, up_ref, rim_ref, back_ref):
    sites = field_ref.shape[2]
    tiles, layers = sites // LANES, sites // PLANE
    lane = lax.broadcasted_iota(jnp.int32, (9, LANES), 1)
    for layer in range(layers):
        for part in range(2):
            row = lambda tile: (9 * tiles + layer * TILES + tile) * 2 + part
            value = [link_ref[pl.ds(row(tile), 9, stride=2 * tiles), :] for tile in range(TILES)]
            value = [lane_roll(v, LZ) for v in value]
            for tile in range(TILES):
                back_ref[part, pl.ds(0, 9), lanes_at(layer, tile)] = jnp.where(lane < LZ, value[tile - 1], value[tile])

    for place, layer in enumerate((0, layers - 1)):

        @pl.loop(0, TILES)
        def _(tile):
            lanes = lanes_at(0, tile)
            for rows in row_groups(field_ref):
                fetch = lambda at, t: load(field_ref, rows, lanes_at(at, t))
                new = one_step(layer, layers, tile, rows, fetch, link_ref, back_ref)
                store(rim_ref, rows, lanes_at(place, tile), new)
                if place == 0:
                    store(down_ref, rows, lanes, new)
                else:
                    turned = [None] * 6
                    add_hop(turned, link_at(link_ref, 0, layer, tile), new, True)
                    store(up_ref, rows, lanes, turned)


def unit_phase(turns):
    half = math.pi * (turns - jnp.round(turns))
    square = half * half
    cosine, sine = 1.0, 1.0
    for order in range(12, 0, -2):
        sine = 1.0 - square * sine * (1.0 / (order * (order + 1)))
        cosine = 1.0 - square * cosine * (1.0 / (order * (order - 1)))
    sine = half * sine
    return 1.0 - 2.0 * sine * sine, 2.0 * sine * cosine


def inner_kernel(total_x, place_ref, field_ref, link_ref, back_ref, momenta_ref, *refs):
    out_ref, table_ref = refs[-2:]
    layers = field_ref.shape[2] // PLANE
    count = momenta_ref.shape[0]
    momenta = momenta_ref[...].astype(WIDE)
    lane = lax.broadcasted_iota(jnp.int32, (count, LANES), 1)

    @pl.loop(0, TILES)
    def _(tile):
        column = (tile * (LANES // LZ) + lane // LZ).astype(WIDE)
        depth = (lane % LZ).astype(WIDE)
        turns = [momenta[:, 1:2] * column / LY, momenta[:, 2:3] * depth / LZ]
        part = sum(t - jnp.round(t) for t in turns)
        for layer in range(layers):
            along = momenta[:, 0:1] * (place_ref[0] + layer).astype(WIDE) / total_x
            cosine, sine = unit_phase(along - jnp.round(along) + part)
            table_ref[0, :, lanes_at(layer, tile)] = cosine
            table_ref[1, :, lanes_at(layer, tile)] = sine


    for layer in range(1, layers - 1):

        @pl.loop(0, TILES)
        def _(tile):
            for rows in row_groups(field_ref):
                fetch = lambda at, t: load(field_ref, rows, lanes_at(at, t))
                new = one_step(layer, layers, tile, rows, fetch, link_ref, back_ref)
                store(out_ref, rows, lanes_at(layer - 1, tile), new)


def second_kernel(
    field_ref, inner_ref, rim_ref, ahead_ref, behind_ref, link_ref, back_ref, out_ref, token_ref, edge_ref
):
    layers = field_ref.shape[2] // PLANE
    token_ref[...] = jnp.zeros_like(token_ref)

    @pl.loop(0, TILES)
    def _(tile):
        lanes, high = lanes_at(0, tile), lanes_at(1, tile)
        for rows in row_groups(field_ref):
            new = zip(load(rim_ref, rows, lanes), load(behind_ref, rows, lanes))
            store(edge_ref, rows, lanes, [a + KAPPA * b for a, b in new])
            hop = [None] * 6
            add_hop(hop, link_at(link_ref, 0, layers - 1, tile), load(ahead_ref, rows, lanes), False)
            store(edge_ref, rows, high, [a + KAPPA * b for a, b in zip(load(rim_ref, rows, high), hop)])

    for layer in range(layers):

        @pl.loop(0, TILES)
        def _(tile):
            for rows in row_groups(field_ref):

                def fetch(at, t):
                    if at in (0, layers - 1):
                        return load(edge_ref, rows, lanes_at(min(at, 1), t))
                    return load(inner_ref, rows, lanes_at(at - 1, t))

                extra = None
                if layer in (0, layers - 1):
                    extra = [KAPPA * a for a in load(field_ref, rows, lanes_at(layer, tile))]
                new = one_step(layer, layers, tile, rows, fetch, link_ref, back_ref, extra)
                store(out_ref, rows, lanes_at(layer, tile), new)


def face_kernel(most_ref, ahead_ref, behind_ref, link_ref, token_ref, out_ref):
    layers = link_ref.shape[0] // 54 // TILES

    @pl.loop(0, TILES)
    def _(tile):
        lanes, high = lanes_at(0, tile), lanes_at(1, tile)
        for rows in row_groups(most_ref):
            new = zip(load(most_ref, rows, lanes), load(behind_ref, rows, lanes))
            store(out_ref, rows, lanes, [a + KAPPA * b for a, b in new])
            hop = [None] * 6
            add_hop(hop, link_at(link_ref, 0, layers - 1, tile), load(ahead_ref, rows, lanes), False)
            new = zip(load(most_ref, rows, lanes_at(layers - 1, tile)), hop)
            store(out_ref, rows, high, [a + KAPPA * b for a, b in new])


def product_kernel(columns, count, scale, slot_ref, most_ref, face_ref, table_ref, *refs):
    groups = len(columns)
    raw_refs, out_refs, (total_ref, left_ref, right_ref) = refs[:groups], refs[groups:-3], refs[-3:]
    vectors = most_ref.shape[1]
    layers = table_ref.shape[2] // PLANE
    depth = 6 * LANES
    step = left_ref.shape[1] // depth
    total_ref[...] = jnp.zeros_like(total_ref)

    def add(field_ref, place):
        for part in range(step):
            own, lanes = place(part)
            field = [field_ref[k, :, own] for k in range(6)]
            one = [pl.ds(part * depth + 2 * color * LANES, LANES) for color in range(3)]
            two = [pl.ds(part * depth + (2 * color + 1) * LANES, LANES) for color in range(3)]
            for p in range(count):
                cosine = table_ref[0, pl.ds(p, 1), lanes]
                sine = table_ref[1, pl.ds(p, 1), lanes]
                rows = pl.ds(p * vectors, vectors)
                for color in range(3):
                    real, imag = field[2 * color], field[2 * color + 1]
                    right_ref[rows, one[color]] = (cosine * real + sine * imag).astype(LOW)
                    right_ref[rows, two[color]] = (cosine * imag - sine * real).astype(LOW)
            for g, raw_ref in enumerate(raw_refs):
                width = raw_ref.shape[1]
                first = pl.ds(2 * g * width, width)
                second = pl.ds((2 * g + 1) * width, width)
                for color in range(3):
                    real, imag = raw_ref[2 * color, :, lanes], raw_ref[2 * color + 1, :, lanes]
                    left_ref[first, one[color]] = real
                    left_ref[first, two[color]] = imag
                    left_ref[second, one[color]] = -imag
                    left_ref[second, two[color]] = real
        total_ref[...] += lax.dot_general(
            left_ref[...], right_ref[...], (((1,), (1,)), ((), ())), preferred_element_type=WIDE
        )

    blocks = TILES // step

    @pl.loop(0, (layers - 2) * blocks)
    def _(block):
        add(most_ref, lambda part: (lanes_at(1, block * step + part),) * 2)

    @pl.loop(0, 2 * blocks)
    def _(block):
        layer = block // blocks * (layers - 1)
        tile = block % blocks * step
        add(face_ref, lambda part: (lanes_at(0, block * step + part), lanes_at(layer, tile + part)))

    width = total_ref.shape[0] // groups
    for g in range(groups):
        block = total_ref[pl.ds(g * width, width), :] * scale
        out_refs[columns[g]][slot_ref[g]] = block.astype(LOW)


def sum_kernel(*refs):
    *share_refs, out_ref = refs
    width = out_ref.shape[1]
    count = out_ref.shape[0] // (2 * width)
    total = sum(ref[...].astype(WIDE) for ref in share_refs)
    for p in range(count):
        block = total[:, p * width : (p + 1) * width]
        for part in range(2):
            rows = pl.ds(2 * p + part, width, stride=2 * count)
            out_ref[rows, :] = block[part * width : (part + 1) * width]


def call(kernel, name, shapes, operands, flops=0, scratch=(), smem=False, alias=None):
    return pl.pallas_call(
        kernel,
        out_shape=tuple(jax.ShapeDtypeStruct(shape, dtype) for shape, dtype in shapes),
        in_specs=([SMEM] if smem else []) + [VMEM] * (len(operands) - smem),
        out_specs=(VMEM,) * len(shapes),
        scratch_shapes=list(scratch),
        input_output_aliases=alias or {},
        compiler_params=pltpu.CompilerParams(vmem_limit_bytes=VMEM_LIMIT),
        cost_estimate=pl.CostEstimate(flops=flops, bytes_accessed=BYTES, transcendentals=0),
        name=name,
    )(*operands)


def shards(vectors, gauge_links, momenta):
    bricks, vecs, subs = (lax.axis_size(axis) for axis in ("brick", "vec", "sub"))
    groups = vecs * subs
    width, sites = vectors.shape[0], vectors.shape[3]
    layers, tiles = sites // PLANE, sites // LANES
    assert groups == bricks and layers > 2 and ITERS == 2
    total_x = bricks * layers
    count = momenta.shape[0]
    brick, vec, sub = (lax.axis_index(axis) for axis in ("brick", "vec", "sub"))
    tiled_vectors = jnp.swapaxes(vectors.reshape((width, 3, 2, tiles, LANES)), 2, 3).reshape((-1, LANES))
    links = jnp.swapaxes(gauge_links.reshape((27, 2, tiles, LANES)), 1, 2).reshape((-1, LANES))
    full, face = (6, width, sites), (6, width, PLANE)
    field, raw, down, up = call(
        open_kernel,
        "open",
        ((full, WIDE), (full, LOW), (face, LOW), (face, LOW)),
        (tiled_vectors, links),
        flops=1 << 22,
    )
    ahead, behind = shifted(down, "brick", -1), shifted(up, "brick", 1)
    across = [shifted(raw, "vec", a) for a in range(1, vecs)]
    beside = [shifted(raw, "sub", b) for b in range(1, subs)]
    down_two, up_two, rim, back = call(
        rim_kernel,
        "rim",
        ((face, LOW), (face, LOW), ((6, width, 2 * PLANE), WIDE), ((2, 16, sites), WIDE)),
        (field, links),
        flops=1 << 24,
    )
    ahead_two, behind_two = shifted(down_two, "brick", -1), shifted(up_two, "brick", 1)
    place = (brick * layers).astype(jnp.int32).reshape((1,))
    inner, table = call(
        functools.partial(inner_kernel, total_x),
        "inner",
        (((6, width, sites - 2 * PLANE), WIDE), ((2, count, sites), WIDE)),
        (place, field, links, back, momenta, *(array[0, :ROWS, :LANES] for array in beside)),
        flops=1 << 24,
        smem=True,
    )
    most, token = call(
        second_kernel,
        "second",
        ((full, WIDE), ((8, LANES), WIDE)),
        (field, inner, rim, ahead, behind, links, back),
        alias={0: 0},
        flops=1 << 25,
        scratch=(pltpu.VMEM((6, width, 2 * PLANE), WIDE),),
    )
    *across, ahead_two, behind_two, token = lax.optimization_barrier((*across, ahead_two, behind_two, token))
    raws = [raw, *across, *beside] + [shifted(array, "sub", b) for b in range(1, subs) for array in across]
    offsets = [(a, 0) for a in range(vecs)] + [(0, b) for b in range(1, subs)]
    offsets += [(a, b) for b in range(1, subs) for a in range(1, vecs)]
    (faces,) = call(
        face_kernel,
        "face",
        (((6, width, 2 * PLANE), WIDE),),
        (most, ahead_two, behind_two, links, token),
        flops=1 << 22,
    )
    brick_vec, brick_sub = brick // subs, brick % subs
    slots = jnp.stack([(sub - b - brick_sub) % subs for a, b in offsets]).astype(jnp.int32)
    scale = (3.0 * total_x * PLANE) ** (-0.5)
    depth = STEP * 6 * LANES
    columns = count * width
    blocks = call(
        functools.partial(product_kernel, [-a % vecs for a, b in offsets], count, scale),
        "product",
        (((subs, 2 * width, columns), LOW),) * vecs,
        (slots, most, faces, table, *raws),
        flops=1 << 32,
        scratch=(
            pltpu.VMEM((groups * 2 * width, columns), WIDE),
            pltpu.VMEM((groups * 2 * width, depth), LOW),
            pltpu.VMEM((columns, depth), LOW),
        ),
        smem=True,
    )
    held = [shifted(block, "vec", a) if a else block for a, block in enumerate(blocks)]
    shares = []
    for q in range(vecs):
        place = (vec - brick_vec - q) % vecs
        block = held[0]
        for a in range(1, vecs):
            block = jnp.where(place == a, held[a], block)
        for r in range(subs):
            pairs = [
                (b * subs + s, ((b // subs + q) % vecs * subs + s) * subs + (b % subs + r) % subs)
                for b in range(bricks)
                for s in range(subs)
            ]
            shares.append(lax.ppermute(block[r], ("brick", "sub"), pairs))
    (total,) = call(sum_kernel, "sum", (((width * count * 2, width), WIDE),), shares, flops=1 << 20)
    return total.reshape((width, count, 2, width))


def solution(mesh):
    in_specs = (
        P(("vec", "sub"), None, None, ("grp", "brick")),
        P(None, None, None, None, ("grp", "brick")),
        P(),
    )
    out_specs = P(("vec", "sub"), "grp", None, "brick")
    return jax.shard_map(shards, mesh=mesh, in_specs=in_specs, out_specs=out_specs, check_vma=False)
```

```python
import functools
import math

import jax
import jax.numpy as jnp
from jax import lax
from jax.experimental import pallas as pl
from jax.experimental.pallas import tpu as pltpu
from jax.sharding import PartitionSpec as P

LY = 64
LZ = 8
ITERS = 2
KAPPA = 0.125
LANES = 128
PLANE = LY * LZ
TILES = PLANE // LANES
ROWS = 16
BYTES = 1 << 20
LOW = jnp.bfloat16
WIDE = jnp.float32
STEP = 2
VMEM_LIMIT = 40 * 1024 * 1024
VMEM = pl.BlockSpec(memory_space=pltpu.VMEM)
SMEM = pl.BlockSpec(memory_space=pltpu.SMEM)


def shifted(array, axis, by):
    peers = lax.axis_size(axis)
    return lax.ppermute(array, axis, [(i, (i + by) % peers) for i in range(peers)])


def add_hop(total, link, field, adjoint):
    for row in range(3):
        for column in range(3):
            if adjoint:
                real, imag = link(column, row, 0), link(column, row, 1)
            else:
                real, imag = link(row, column, 0), link(row, column, 1)
            source_real, source_imag = field[2 * column], field[2 * column + 1]
            if adjoint:
                add_real = real * source_real + imag * source_imag
                add_imag = real * source_imag - imag * source_real
            else:
                add_real = real * source_real - imag * source_imag
                add_imag = real * source_imag + imag * source_real
            for part, add in ((0, add_real), (1, add_imag)):
                old = total[2 * row + part]
                total[2 * row + part] = add if old is None else old + add


def lane_roll(value, by):
    return pltpu.roll(value, by % LANES, 1)


def lanes_at(layer, tile):
    return pl.ds(pl.multiple_of(layer * PLANE + tile * LANES, LANES), LANES)


def row_groups(ref):
    size = min(ROWS, ref.shape[1])
    return [pl.ds(start, size) for start in range(0, ref.shape[1], size)]


def load(ref, rows, lanes):
    return [ref[k, rows, lanes].astype(WIDE) for k in range(6)]


def store(ref, rows, lanes, values):
    for k in range(6):
        ref[k, rows, lanes] = values[k].astype(ref.dtype)


def link_at(link_ref, direction, layer, tile):
    tiles = link_ref.shape[0] // 54

    def get(row, column, part):
        matrix = (direction * 3 + row) * 3 + column
        return link_ref[pl.ds((matrix * tiles + layer * TILES + tile) * 2 + part, 1), :]

    return get


def plane_hops(total, link_ref, back_ref, layer, tile, rows, fetch):
    here = fetch(tile)
    after, before = fetch((tile + 1) % TILES), fetch((tile + TILES - 1) % TILES)
    lane = lax.broadcasted_iota(jnp.int32, (rows.size, LANES), 1)
    ahead = [jnp.where(lane >= LANES - LZ, lane_roll(b, -LZ), lane_roll(a, -LZ)) for a, b in zip(here, after)]
    add_hop(total, link_at(link_ref, 1, layer, tile), ahead, False)
    behind = [jnp.where(lane < LZ, lane_roll(b, LZ), lane_roll(a, LZ)) for a, b in zip(here, before)]
    lanes = lanes_at(layer, tile)
    add_hop(total, lambda r, c, part: back_ref[part, pl.ds(3 * r + c, 1), lanes], behind, True)
    depth = lane % LZ
    ahead = [jnp.where(depth == LZ - 1, lane_roll(a, LZ - 1), lane_roll(a, -1)) for a in here]
    add_hop(total, link_at(link_ref, 2, layer, tile), ahead, False)
    turned = [None] * 6
    add_hop(turned, link_at(link_ref, 2, layer, tile), here, True)
    for k in range(6):
        total[k] += jnp.where(depth == 0, lane_roll(turned[k], 1 - LZ), lane_roll(turned[k], 1))
    return here


def combined(here, total):
    return [(1.0 - 6.0 * KAPPA) * a + KAPPA * b for a, b in zip(here, total)]


def one_step(layer, layers, tile, rows, fetch, link_ref, back_ref, extra=None):
    total = [None] * 6
    if layer < layers - 1:
        add_hop(total, link_at(link_ref, 0, layer, tile), fetch(layer + 1, tile), False)
    if layer > 0:
        add_hop(total, link_at(link_ref, 0, layer - 1, tile), fetch(layer - 1, tile), True)
    here = plane_hops(total, link_ref, back_ref, layer, tile, rows, lambda t: fetch(layer, t))
    if extra is not None:
        total = [a + b for a, b in zip(total, extra)]
    return combined(here, total)


def open_kernel(vector_ref, link_ref, field_ref, raw_ref, down_ref, up_ref):
    vectors, sites = field_ref.shape[1:]
    tiles, layers = sites // LANES, sites // PLANE
    stride = 6 * tiles
    for k in range(6):
        for tile in range(tiles):
            row = ((k // 2) * tiles + tile) * 2 + k % 2
            value = vector_ref[pl.ds(row, vectors, stride=stride), :]
            field_ref[k, :, pl.ds(tile * LANES, LANES)] = value
            low = value.astype(LOW)
            raw_ref[k, :, pl.ds(tile * LANES, LANES)] = low
            if tile < TILES:
                down_ref[k, :, pl.ds(tile * LANES, LANES)] = low

    @pl.loop(0, TILES, unroll=True)
    def _(tile):
        for rows in row_groups(field_ref):
            turned = [None] * 6
            source = load(field_ref, rows, lanes_at(layers - 1, tile))
            add_hop(turned, link_at(link_ref, 0, layers - 1, tile), source, True)
            store(up_ref, rows, lanes_at(0, tile), turned)


def rim_kernel(field_ref, link_ref, down_ref, up_ref, rim_ref, back_ref):
    sites = field_ref.shape[2]
    tiles, layers = sites // LANES, sites // PLANE
    lane = lax.broadcasted_iota(jnp.int32, (9, LANES), 1)
    for layer in range(layers):
        for part in range(2):
            row = lambda tile: (9 * tiles + layer * TILES + tile) * 2 + part
            value = [link_ref[pl.ds(row(tile), 9, stride=2 * tiles), :] for tile in range(TILES)]
            value = [lane_roll(v, LZ) for v in value]
            for tile in range(TILES):
                back_ref[part, pl.ds(0, 9), lanes_at(layer, tile)] = jnp.where(lane < LZ, value[tile - 1], value[tile])

    for place, layer in enumerate((0, layers - 1)):

        @pl.loop(0, TILES, unroll=True)
        def _(tile):
            lanes = lanes_at(0, tile)
            for rows in row_groups(field_ref):
                fetch = lambda at, t: load(field_ref, rows, lanes_at(at, t))
                new = one_step(layer, layers, tile, rows, fetch, link_ref, back_ref)
                store(rim_ref, rows, lanes_at(place, tile), new)
                if place == 0:
                    store(down_ref, rows, lanes, new)
                else:
                    turned = [None] * 6
                    add_hop(turned, link_at(link_ref, 0, layer, tile), new, True)
                    store(up_ref, rows, lanes, turned)


def unit_phase(turns):
    half = math.pi * (turns - jnp.round(turns))
    square = half * half
    cosine, sine = 1.0, 1.0
    for order in range(12, 0, -2):
        sine = 1.0 - square * sine * (1.0 / (order * (order + 1)))
        cosine = 1.0 - square * cosine * (1.0 / (order * (order - 1)))
    sine = half * sine
    return 1.0 - 2.0 * sine * sine, 2.0 * sine * cosine


def inner_kernel(total_x, place_ref, field_ref, link_ref, back_ref, momenta_ref, out_ref, table_ref):
    layers = field_ref.shape[2] // PLANE
    count = momenta_ref.shape[0]
    momenta = momenta_ref[...].astype(WIDE)
    lane = lax.broadcasted_iota(jnp.int32, (count, LANES), 1)

    @pl.loop(0, TILES, unroll=True)
    def _(tile):
        column = (tile * (LANES // LZ) + lane // LZ).astype(WIDE)
        depth = (lane % LZ).astype(WIDE)
        turns = [momenta[:, 1:2] * column / LY, momenta[:, 2:3] * depth / LZ]
        part = sum(t - jnp.round(t) for t in turns)
        for layer in range(layers):
            along = momenta[:, 0:1] * (place_ref[0] + layer).astype(WIDE) / total_x
            cosine, sine = unit_phase(along - jnp.round(along) + part)
            table_ref[0, :, lanes_at(layer, tile)] = cosine
            table_ref[1, :, lanes_at(layer, tile)] = sine


    for layer in range(1, layers - 1):

        @pl.loop(0, TILES, unroll=True)
        def _(tile):
            for rows in row_groups(field_ref):
                fetch = lambda at, t: load(field_ref, rows, lanes_at(at, t))
                new = one_step(layer, layers, tile, rows, fetch, link_ref, back_ref)
                store(out_ref, rows, lanes_at(layer - 1, tile), new)


def second_kernel(
    field_ref, inner_ref, rim_ref, ahead_ref, behind_ref, link_ref, back_ref, out_ref, token_ref, edge_ref
):
    layers = field_ref.shape[2] // PLANE
    token_ref[...] = jnp.zeros_like(token_ref)

    @pl.loop(0, TILES, unroll=True)
    def _(tile):
        lanes, high = lanes_at(0, tile), lanes_at(1, tile)
        for rows in row_groups(field_ref):
            new = zip(load(rim_ref, rows, lanes), load(behind_ref, rows, lanes))
            store(edge_ref, rows, lanes, [a + KAPPA * b for a, b in new])
            hop = [None] * 6
            add_hop(hop, link_at(link_ref, 0, layers - 1, tile), load(ahead_ref, rows, lanes), False)
            store(edge_ref, rows, high, [a + KAPPA * b for a, b in zip(load(rim_ref, rows, high), hop)])

    for layer in range(layers):

        @pl.loop(0, TILES, unroll=True)
        def _(tile):
            for rows in row_groups(field_ref):

                def fetch(at, t):
                    if at in (0, layers - 1):
                        return load(edge_ref, rows, lanes_at(min(at, 1), t))
                    return load(inner_ref, rows, lanes_at(at - 1, t))

                extra = None
                if layer in (0, layers - 1):
                    extra = [KAPPA * a for a in load(field_ref, rows, lanes_at(layer, tile))]
                new = one_step(layer, layers, tile, rows, fetch, link_ref, back_ref, extra)
                store(out_ref, rows, lanes_at(layer, tile), new)


def face_kernel(most_ref, ahead_ref, behind_ref, link_ref, token_ref, out_ref):
    layers = link_ref.shape[0] // 54 // TILES

    @pl.loop(0, TILES, unroll=True)
    def _(tile):
        lanes, high = lanes_at(0, tile), lanes_at(1, tile)
        for rows in row_groups(most_ref):
            new = zip(load(most_ref, rows, lanes), load(behind_ref, rows, lanes))
            store(out_ref, rows, lanes, [a + KAPPA * b for a, b in new])
            hop = [None] * 6
            add_hop(hop, link_at(link_ref, 0, layers - 1, tile), load(ahead_ref, rows, lanes), False)
            new = zip(load(most_ref, rows, lanes_at(layers - 1, tile)), hop)
            store(out_ref, rows, high, [a + KAPPA * b for a, b in new])


def product_kernel(columns, count, scale, slot_ref, most_ref, face_ref, table_ref, *refs):
    groups = len(columns)
    raw_refs, out_refs, (total_ref, left_ref, right_ref) = refs[:groups], refs[groups:-3], refs[-3:]
    vectors = most_ref.shape[1]
    layers = table_ref.shape[2] // PLANE
    depth = 6 * LANES
    step = left_ref.shape[1] // depth
    total_ref[...] = jnp.zeros_like(total_ref)

    def add(field_ref, place):
        for part in range(step):
            own, lanes = place(part)
            field = [field_ref[k, :, own] for k in range(6)]
            one = [pl.ds(part * depth + 2 * color * LANES, LANES) for color in range(3)]
            two = [pl.ds(part * depth + (2 * color + 1) * LANES, LANES) for color in range(3)]
            for p in range(count):
                cosine = table_ref[0, pl.ds(p, 1), lanes]
                sine = table_ref[1, pl.ds(p, 1), lanes]
                rows = pl.ds(p * vectors, vectors)
                for color in range(3):
                    real, imag = field[2 * color], field[2 * color + 1]
                    right_ref[rows, one[color]] = (cosine * real + sine * imag).astype(LOW)
                    right_ref[rows, two[color]] = (cosine * imag - sine * real).astype(LOW)
            for g, raw_ref in enumerate(raw_refs):
                width = raw_ref.shape[1]
                first = pl.ds(2 * g * width, width)
                second = pl.ds((2 * g + 1) * width, width)
                for color in range(3):
                    real, imag = raw_ref[2 * color, :, lanes], raw_ref[2 * color + 1, :, lanes]
                    left_ref[first, one[color]] = real
                    left_ref[first, two[color]] = imag
                    left_ref[second, one[color]] = -imag
                    left_ref[second, two[color]] = real
        total_ref[...] += lax.dot_general(
            left_ref[...], right_ref[...], (((1,), (1,)), ((), ())), preferred_element_type=WIDE
        )

    blocks = TILES // step

    @pl.loop(0, (layers - 2) * blocks)
    def _(block):
        add(most_ref, lambda part: (lanes_at(1, block * step + part),) * 2)

    @pl.loop(0, 2 * blocks)
    def _(block):
        layer = block // blocks * (layers - 1)
        tile = block % blocks * step
        add(face_ref, lambda part: (lanes_at(0, block * step + part), lanes_at(layer, tile + part)))

    width = total_ref.shape[0] // groups
    for g in range(groups):
        block = total_ref[pl.ds(g * width, width), :] * scale
        out_refs[columns[g]][slot_ref[g]] = block.astype(LOW)


def sum_kernel(*refs):
    *share_refs, out_ref = refs
    width = out_ref.shape[1]
    count = out_ref.shape[0] // (2 * width)
    total = sum(ref[...].astype(WIDE) for ref in share_refs)
    for p in range(count):
        block = total[:, p * width : (p + 1) * width]
        for part in range(2):
            rows = pl.ds(2 * p + part, width, stride=2 * count)
            out_ref[rows, :] = block[part * width : (part + 1) * width]


def call(kernel, name, shapes, operands, flops=0, scratch=(), smem=False, alias=None):
    return pl.pallas_call(
        kernel,
        out_shape=tuple(jax.ShapeDtypeStruct(shape, dtype) for shape, dtype in shapes),
        in_specs=[SMEM if smem and i == 0 else VMEM for i in range(len(operands))],
        out_specs=(VMEM,) * len(shapes),
        scratch_shapes=list(scratch),
        input_output_aliases=alias or {},
        compiler_params=pltpu.CompilerParams(vmem_limit_bytes=VMEM_LIMIT),
        cost_estimate=pl.CostEstimate(flops=flops, bytes_accessed=BYTES, transcendentals=0),
        name=name,
    )(*operands)


def shards(vectors, gauge_links, momenta):
    bricks, vecs, subs = (lax.axis_size(axis) for axis in ("brick", "vec", "sub"))
    groups = vecs * subs
    width, sites = vectors.shape[0], vectors.shape[3]
    layers, tiles = sites // PLANE, sites // LANES
    assert groups == bricks and layers > 2 and ITERS == 2
    total_x = bricks * layers
    count = momenta.shape[0]
    brick, vec, sub = (lax.axis_index(axis) for axis in ("brick", "vec", "sub"))
    tiled_vectors = jnp.swapaxes(vectors.reshape((width, 3, 2, tiles, LANES)), 2, 3).reshape((-1, LANES))
    links = jnp.swapaxes(gauge_links.reshape((27, 2, tiles, LANES)), 1, 2).reshape((-1, LANES))
    full, face = (6, width, sites), (6, width, PLANE)
    field, raw, down, up = call(
        open_kernel,
        "open",
        ((full, WIDE), (full, LOW), (face, LOW), (face, LOW)),
        (tiled_vectors, links),
        flops=1 << 22,
    )
    ahead, behind = shifted(down, "brick", -1), shifted(up, "brick", 1)
    across = [shifted(raw, "vec", a) for a in range(1, vecs)]
    down_two, up_two, rim, back = call(
        rim_kernel,
        "rim",
        ((face, LOW), (face, LOW), ((6, width, 2 * PLANE), WIDE), ((2, 16, sites), WIDE)),
        (field, links),
        flops=1 << 24,
    )
    ahead_two, behind_two = shifted(down_two, "brick", -1), shifted(up_two, "brick", 1)
    place = (brick * layers).astype(jnp.int32).reshape((1,))
    inner, table = call(
        functools.partial(inner_kernel, total_x),
        "inner",
        (((6, width, sites - 2 * PLANE), WIDE), ((2, count, sites), WIDE)),
        (place, field, links, back, momenta),
        flops=1 << 24,
        smem=True,
    )
    most, token = call(
        second_kernel,
        "second",
        ((full, WIDE), ((8, LANES), WIDE)),
        (field, inner, rim, ahead, behind, links, back),
        alias={0: 0},
        flops=1 << 25,
        scratch=(pltpu.VMEM((6, width, 2 * PLANE), WIDE),),
    )
    late, token = lax.optimization_barrier((raw, token))
    *across, ahead_two, behind_two, token = lax.optimization_barrier((*across, ahead_two, behind_two, token))
    raws = [raw, *across] + [shifted(array, "sub", b) for b in range(1, subs) for array in (late, *across)]
    offsets = [(a, b) for b in range(subs) for a in range(vecs)]
    (faces,) = call(
        face_kernel,
        "face",
        (((6, width, 2 * PLANE), WIDE),),
        (most, ahead_two, behind_two, links, token),
        flops=1 << 22,
    )
    brick_vec, brick_sub = brick // subs, brick % subs
    slots = jnp.stack([(sub - b - brick_sub) % subs for a, b in offsets]).astype(jnp.int32)
    scale = (3.0 * total_x * PLANE) ** (-0.5)
    depth = STEP * 6 * LANES
    columns = count * width
    blocks = call(
        functools.partial(product_kernel, [-a % vecs for a, b in offsets], count, scale),
        "product",
        (((subs, 2 * width, columns), LOW),) * vecs,
        (slots, most, faces, table, *raws),
        flops=1 << 32,
        scratch=(
            pltpu.VMEM((groups * 2 * width, columns), WIDE),
            pltpu.VMEM((groups * 2 * width, depth), LOW),
            pltpu.VMEM((columns, depth), LOW),
        ),
        smem=True,
    )
    held = [shifted(block, "vec", a) if a else block for a, block in enumerate(blocks)]
    shares = []
    for q in range(vecs):
        place = (vec - brick_vec - q) % vecs
        block = held[0]
        for a in range(1, vecs):
            block = jnp.where(place == a, held[a], block)
        for r in range(subs):
            pairs = [
                (b * subs + s, ((b // subs + q) % vecs * subs + s) * subs + (b % subs + r) % subs)
                for b in range(bricks)
                for s in range(subs)
            ]
            shares.append(lax.ppermute(block[r], ("brick", "sub"), pairs))
    (total,) = call(sum_kernel, "sum", (((width * count * 2, width), WIDE),), shares, flops=1 << 20)
    return total.reshape((width, count, 2, width))


def solution(mesh):
    in_specs = (
        P(("vec", "sub"), None, None, ("grp", "brick")),
        P(None, None, None, None, ("grp", "brick")),
        P(),
    )
    out_specs = P(("vec", "sub"), "grp", None, "brick")
    return jax.shard_map(shards, mesh=mesh, in_specs=in_specs, out_specs=out_specs, check_vma=False)
```
